32 devices in a mesh: rep: 2 (over x), grp: 2 (over core), ep: 8 (over z, y).
Axes of the slice: x: 2, y: 2, z: 4, core: 2. Of those that a mesh axis runs over, the one named last changes fastest.
Arguments:
- tokens: bfloat16 [4096, 4096], P(('rep', 'grp', 'ep')), parts along dimension 0, may hold values from -6 to 6
- expert_ids: int32 [4096, 8], P(('rep', 'grp', 'ep')), parts along dimension 0, may hold values from 0 to 15, all different within a row; in each aligned block of 128 rows (0 to 127, 128 to 255, ...) at most 128 rows name the same one
- route_scores: float32 [4096, 8], P(('rep', 'grp', 'ep')), parts along dimension 0, may hold values from -8 to 8
- down_latent: bfloat16 [4096, 1024], P('ep'), may hold values from -0.09375 to 0.09375
- gate_weight: bfloat16 [16, 1024, 2048], P(('grp', 'ep')), may hold values from -0.1875 to 0.1875
- up_weight: bfloat16 [16, 1024, 2048], P(('grp', 'ep')), may hold values from -0.1875 to 0.1875
- out_weight: bfloat16 [16, 2048, 1024], P(('grp', 'ep')), may hold values from -0.125 to 0.125
- up_latent: bfloat16 [1024, 4096], P(None, 'ep'), may hold values from -0.1875 to 0.1875
Outputs:
- layer_out: bfloat16 [4096, 4096], P(('rep', 'grp', 'ep')), parts along dimension 0
The draws below stay inside these ranges and needn't reach their ends.
There are 2 independent parts, one for each index of `rep`. The reference program is written for one: setup_inputs(seed, part) draws one part's arguments, and reference() takes and returns one part's arrays. A program takes and returns all parts, laid end to end along the dimension named above; an argument that names none is the same for every part. Nothing has to cross between parts.
Inputs may be any that keep to these rules, and one draw needn't show every extreme that they name: `expert_ids`: each token names 8 different experts. Among the 128 tokens of one device no expert is named more than 128 times, and in every draw some expert is named exactly 128 times there.
All inputs are finite; a program needn't handle non-finite values.
Results may differ from the reference program's by a relative error of at most 0.014.
Values may be sent and summed in bfloat16 or wider, within the bound.
No kernel may reach another device: no remote copies, remote signals or barrier semaphores. Data moves between devices by JAX's collectives and lax.ppermute only.
A program may use at most 128 MiB of HBM per device.

```python
import math
import jax
import jax.numpy as jnp
import numpy as np
from jax import lax

D = 4096
L = 1024
H = 2048
TOP = 8
TOK_DEV = 128
TOKENS = 2048
EXPERTS = 16
GROUP_EXPERTS = 8
GROUPS = 2
CAP = 128
N_GRP = 2
N_EP = 8


def steps_of(rng, extent, shards, smallest, high):
    factor_of, own = 1.0, jax.random.fold_in(rng, 6)
    for dim, parts in shards:
        steps = jnp.exp(jax.random.uniform(jax.random.fold_in(own, dim), (parts,), jnp.float32, smallest / len(shards), high / len(shards)))
        factor_of = factor_of * jnp.repeat(steps, extent[dim] // parts).reshape([-1 if axis == dim else 1 for axis in range(len(extent))])
    return factor_of


def routed_block(stream_key, own, number, rows, amount, top, most, lean):
    sequence = jax.random.permutation(stream_key, amount)
    packed, usual = shares(amount, rows * top, most, lean, True), shares(amount, rows * top, most, lean, False)
    places = jnp.arange(amount)

    def named(sizes, offset_by):
        used = int((sizes > 0).sum())
        fixed = max(1, used // 4)
        shifted = fixed + (places - fixed + offset_by * (used - fixed)) % max(1, amount - fixed)
        return jnp.zeros((amount,), jnp.int32).at[sequence[jnp.where(places < fixed, places, shifted)]].set(jnp.asarray(sizes, jnp.int32))

    sizes = jnp.where(number % 4 == 0, named(packed, number // 4), named(usual, number - number // 4 - 1))
    mixed = jax.random.permutation(jax.random.fold_in(own, 3), amount)
    donor, sink = mixed[0:amount // 2 * 2:2], mixed[1:amount // 2 * 2:2]
    slack = jnp.minimum(sizes[donor] - 1, most - sizes[sink]) // 2
    slack = jnp.where((donor == sequence[0]) | (sink == sequence[0]) | (sizes[sink] == 0), 0, jnp.maximum(slack, 0))
    shifted = jax.random.randint(jax.random.fold_in(own, 4), (amount // 2,), 0, 1 << 20) % (slack + 1)
    sizes = sizes.at[donor].add(-shifted).at[sink].add(shifted)
    labels = jnp.searchsorted(jnp.cumsum(sizes), jnp.arange(rows * top), side="right").astype(jnp.int32)
    table = labels.reshape(top, rows).T
    table = table[jax.random.permutation(jax.random.fold_in(own, 1), rows)]
    offset_by = jax.random.randint(jax.random.fold_in(own, 2), (rows, 1), 0, top)
    return jnp.take_along_axis(table, (jnp.arange(top)[None, :] + offset_by) % top, axis=1)


def shares(number_of, total, limit, skew, full):
    weights = [(1 << 20) // math.isqrt(standing ** skew) + 1 for standing in range(1, number_of + 1)]
    largest = limit if full else min(limit, max(-(-total // number_of), total * weights[0] // sum(weights)))
    least = 1 if total - largest >= number_of - 1 else 0
    holding, surplus = [largest] + [least] * (number_of - 1), total - largest - least * (number_of - 1)
    while surplus > 0:
        free = [i for i in range(1, number_of) if holding[i] < largest] or [i for i in range(1, number_of) if holding[i] < limit]
        pool, budget = sum([weights[i] for i in free]), surplus
        for i in free:
            addition = min(limit - holding[i], max(1, budget * weights[i] // pool), surplus)
            holding[i] = holding[i] + addition
            surplus = surplus - addition
    return np.array(holding)


def scatter_about(own_key, shape, spread, limit, cuts=(), kind=jnp.bfloat16):
    array = jax.random.normal(own_key, shape, jnp.float32) * spread
    if len(cuts) > 0:
        array = steps_of(own_key, shape, cuts, -0.22, 0.18) * array
    return jnp.clip(array, min=-limit, max=limit).astype(kind)


def setup_inputs(seed: int = 0, part: int = 0) -> dict:
    streams_of = jax.random.split(jax.random.key(seed), 9)
    part_keys = jax.random.split(jax.random.fold_in(streams_of[8], part), 9)
    tokens = scatter_about(part_keys[0], (TOKENS, D), 1.0, 6.0, ((0, 16),))
    expert_ids_keys = jax.random.split(jax.random.fold_in(part_keys[1], 1), TOKENS // TOK_DEV)
    expert_ids_turns = jax.random.permutation(jax.random.fold_in(part_keys[1], 3), TOKENS // TOK_DEV)
    expert_ids = jax.vmap(lambda own, number: routed_block(jax.random.fold_in(part_keys[1], 2), own, number, TOK_DEV, EXPERTS, TOP, CAP, 2))(expert_ids_keys, expert_ids_turns).reshape((TOKENS, TOP))
    route_scores = scatter_about(part_keys[2], (TOKENS, TOP), 2.0, 8.0, ((0, 16),), jnp.float32)
    down_latent = scatter_about(streams_of[3], (D, L), D ** -0.5, 0.09375, ((0, 8),))
    gate_weight = scatter_about(streams_of[4], (EXPERTS, L, H), L ** -0.5, 0.1875, ((0, 16),))
    up_weight = scatter_about(streams_of[5], (EXPERTS, L, H), L ** -0.5, 0.1875, ((0, 16),))
    out_weight = scatter_about(streams_of[6], (EXPERTS, H, L), H ** -0.5, 0.125, ((0, 16),))
    up_latent = scatter_about(streams_of[7], (L, D), L ** -0.5, 0.1875, ((1, 8),))
    return {"tokens": tokens, "expert_ids": expert_ids, "route_scores": route_scores, "down_latent": down_latent, "gate_weight": gate_weight, "up_weight": up_weight, "out_weight": out_weight, "up_latent": up_latent}


route_scale = 2.5
row_block = 128


def reference(tokens, expert_ids, route_scores, down_latent, gate_weight, up_weight, out_weight, up_latent):
    latent = jnp.dot(tokens, down_latent, preferred_element_type=jnp.float32).astype(jnp.bfloat16)
    sigmoids = jax.nn.sigmoid(route_scores.astype(jnp.float32))
    weights = (route_scale * sigmoids / jnp.sum(sigmoids, axis=1, keepdims=True)).astype(jnp.bfloat16)
    flat_ids = expert_ids.reshape(-1).astype(jnp.int32)
    n_assign = flat_ids.shape[0]
    onehot = (flat_ids[:, None] == jnp.arange(EXPERTS, dtype=jnp.int32)[None, :]).astype(jnp.int32)
    slot_ranks = jnp.sum((jnp.cumsum(onehot, axis=0) - onehot) * onehot, axis=1).astype(jnp.int32)
    counts = jnp.sum(onehot, axis=0).astype(jnp.int32)
    max_rows = N_GRP * N_EP * CAP
    row_table = jnp.full((EXPERTS, max_rows), n_assign, jnp.int32)
    row_table = row_table.at[flat_ids, slot_ranks].set(jnp.arange(n_assign, dtype=jnp.int32))
    replies = jnp.zeros((n_assign + 1, L), jnp.bfloat16)

    def expert_step(expert, replies):
        expert = jnp.asarray(expert).astype(jnp.int32)
        w_gate = lax.dynamic_index_in_dim(gate_weight, expert, 0, keepdims=False)
        w_up = lax.dynamic_index_in_dim(up_weight, expert, 0, keepdims=False)
        w_out = lax.dynamic_index_in_dim(out_weight, expert, 0, keepdims=False)
        listing = lax.dynamic_index_in_dim(row_table, expert, 0, keepdims=False)
        n_blocks = (counts[expert] + row_block - 1) // row_block

        def block_step(block_number, replies):
            block_start = (jnp.asarray(block_number).astype(jnp.int32) * row_block).astype(jnp.int32)
            picked = lax.dynamic_slice_in_dim(listing, block_start, row_block)
            block_rows = latent[jnp.minimum(picked, n_assign - 1) // TOP]
            gate_value = jnp.dot(block_rows, w_gate, preferred_element_type=jnp.float32)
            up_value = jnp.dot(block_rows, w_up, preferred_element_type=jnp.float32)
            hidden = (jax.nn.silu(gate_value) * up_value).astype(jnp.bfloat16)
            outputs = jnp.dot(hidden, w_out, preferred_element_type=jnp.float32).astype(jnp.bfloat16)
            return replies.at[picked].set(outputs)

        return lax.fori_loop(0, n_blocks, block_step, replies)

    replies = lax.fori_loop(0, EXPERTS, expert_step, replies)
    answers = replies[:n_assign].reshape(TOKENS, TOP, L).astype(jnp.float32)
    route_owner = expert_ids // GROUP_EXPERTS
    group_terms = []
    for group_index in range(GROUPS):
        scaled = jnp.where(route_owner == group_index, weights.astype(jnp.float32), 0.0)
        group_terms.append(jnp.sum(scaled[:, :, None] * answers, axis=1))
    group_parts = lax.optimization_barrier(jnp.stack(group_terms, axis=1).astype(jnp.bfloat16))
    combined = jnp.sum(group_parts.astype(jnp.float32), axis=1).astype(jnp.bfloat16)
    return jnp.dot(combined, up_latent, preferred_element_type=jnp.float32).astype(jnp.bfloat16)
```

```python
import jax
import jax.numpy as jnp
from jax import lax
from jax.sharding import PartitionSpec as P

route_scale = 2.5


def swap_cores(array):
    return lax.ppermute(array, "grp", [(0, 1), (1, 0)])


def dense_weights(expert_ids, route_scores, expert_count):
    sigmoids = jax.nn.sigmoid(route_scores)
    weights = (route_scale * sigmoids / jnp.sum(sigmoids, axis=1, keepdims=True)).astype(
        jnp.bfloat16
    )
    named = expert_ids[:, :, None] == jnp.arange(expert_count, dtype=jnp.int32)[None, None, :]
    return jnp.sum(jnp.where(named, weights.astype(jnp.float32)[:, :, None], 0.0), axis=1)


def expert_apply(rows, scale, gate_weight, up_weight, out_weight):
    gate_value = jnp.dot(rows, gate_weight, preferred_element_type=jnp.float32)
    up_value = jnp.dot(rows, up_weight, preferred_element_type=jnp.float32)
    hidden = (jax.nn.silu(gate_value) * up_value).astype(jnp.bfloat16)
    out = jnp.dot(hidden, out_weight, preferred_element_type=jnp.float32)
    return (out * scale).astype(jnp.bfloat16)


def body(
    tokens, expert_ids, route_scores, down_latent, gate_weight, up_weight, out_weight, up_latent
):
    group_count = lax.axis_size("grp")
    ep_count = lax.axis_size("ep")
    expert_count = group_count * ep_count * gate_weight.shape[0]
    group = lax.axis_index("grp")
    token_count = tokens.shape[0]
    latent_width = down_latent.shape[1]

    half = down_latent.shape[0] // 2
    own_down = lax.all_gather(
        lax.dynamic_slice_in_dim(down_latent, group * half, half, 0), "ep", axis=0, tiled=True
    )
    other_down = swap_cores(own_down)

    weights = dense_weights(expert_ids, route_scores, expert_count)
    weights = lax.all_gather(weights, ("grp", "ep"), axis=0, tiled=True)
    expert = group * ep_count + lax.axis_index("ep")
    scale = lax.dynamic_slice_in_dim(weights, expert, 1, 1)
    scale = scale.reshape(group_count, ep_count * token_count, 1)
    own_scale = lax.dynamic_index_in_dim(scale, group, 0, keepdims=False)
    other_scale = lax.dynamic_index_in_dim(scale, 1 - group, 0, keepdims=False)

    halves = tokens.reshape(token_count, ep_count, 2, half)
    own_tokens = lax.dynamic_index_in_dim(halves, group, 2, keepdims=False)
    other_tokens = lax.dynamic_index_in_dim(halves, 1 - group, 2, keepdims=False)
    latent = jnp.dot(
        own_tokens.reshape(token_count, -1), own_down, preferred_element_type=jnp.float32
    ) + jnp.dot(
        other_tokens.reshape(token_count, -1), other_down, preferred_element_type=jnp.float32
    )
    own_rows = lax.all_gather(latent.astype(jnp.bfloat16), "ep", axis=0, tiled=True)
    other_rows = swap_cores(own_rows)

    own_part = expert_apply(own_rows, own_scale, gate_weight[0], up_weight[0], out_weight[0])
    other_part = expert_apply(other_rows, other_scale, gate_weight[0], up_weight[0], out_weight[0])
    both = (own_part.astype(jnp.float32) + swap_cores(other_part).astype(jnp.float32)).astype(
        jnp.bfloat16
    )
    combined = lax.psum_scatter(both, "ep", scatter_dimension=0, tiled=True)

    width = up_latent.shape[1] // 2
    own_up = lax.all_gather(
        lax.dynamic_slice_in_dim(up_latent, group * width, width, 1), "ep", axis=0
    )
    other_up = swap_cores(own_up)
    own_out = jnp.einsum(
        "tl,elw->tew", combined, own_up, preferred_element_type=jnp.float32
    ).astype(jnp.bfloat16)
    other_out = jnp.einsum(
        "tl,elw->tew", combined, other_up, preferred_element_type=jnp.float32
    ).astype(jnp.bfloat16)
    first = jnp.where(group == 0, own_out, other_out)
    second = jnp.where(group == 0, other_out, own_out)
    return jnp.stack([first, second], axis=2).reshape(token_count, -1)


def solution(mesh):
    in_specs = (
        P(("rep", "grp", "ep"), None),
        P(("rep", "grp", "ep"), None),
        P(("rep", "grp", "ep"), None),
        P("ep", None),
        P(("grp", "ep"), None, None),
        P(("grp", "ep"), None, None),
        P(("grp", "ep"), None, None),
        P(None, "ep"),
    )
    out_specs = P(("rep", "grp", "ep"), None)
    return jax.shard_map(body, mesh=mesh, in_specs=in_specs, out_specs=out_specs, check_vma=False)
```

```python
import functools

import jax
import jax.numpy as jnp
from jax import lax
from jax.experimental import pallas as pl
from jax.experimental.pallas import tpu as pltpu
from jax.sharding import PartitionSpec as P

route_scale = 2.5


def swap_cores(array):
    return lax.ppermute(array, "grp", [(0, 1), (1, 0)])


def swap_reps(array):
    return lax.ppermute(array, "rep", [(i, i ^ 1) for i in range(lax.axis_size("rep"))])


def swap_ep(array, mask):
    return lax.ppermute(array, "ep", [(i, i ^ mask) for i in range(lax.axis_size("ep"))])


def gather_ep(piece):
    along = [piece] + [swap_ep(piece, 2 * k) for k in range(1, lax.axis_size("ep") // 2)]
    return [(near, swap_ep(near, 1)) for near in along]


def dense_weights(expert_ids, route_scores, expert_count):
    sigmoids = jax.nn.sigmoid(route_scores)
    weights = (route_scale * sigmoids / jnp.sum(sigmoids, axis=1, keepdims=True)).astype(
        jnp.bfloat16
    )
    named = expert_ids[None, :, :] == jnp.arange(expert_count, dtype=jnp.int32)[:, None, None]
    return jnp.sum(jnp.where(named, weights.astype(jnp.float32)[None, :, :], 0.0), axis=2)


def expert_kernel(
    steps, near, far, other, scale, gate, up, out, own_sum, other_sum, rows, total
):
    step = pl.program_id(0)
    count = near.shape[0]

    @pl.when(step == 0)
    def _():
        rows[:count] = near[...]
        rows[count : 2 * count] = far[...]
        rows[2 * count :] = other[...]
        total[...] = jnp.zeros_like(total)

    width = 256
    for start in range(0, gate.shape[2], width):
        columns = slice(start, start + width)
        gate_value = jnp.dot(rows[...], gate[0, :, columns], preferred_element_type=jnp.float32)
        up_value = jnp.dot(rows[...], up[0, :, columns], preferred_element_type=jnp.float32)
        hidden = gate_value / (1.0 + jnp.exp(-gate_value)) * up_value
        total[...] += jnp.dot(
            hidden.astype(jnp.bfloat16), out[0, columns, :], preferred_element_type=jnp.float32
        )

    @pl.when(step == steps - 1)
    def _():
        factor = scale[:, :1]
        own_sum[...] = (total[: 2 * count] * factor[: 2 * count]).astype(jnp.bfloat16)
        other_sum[...] = (total[2 * count :] * factor[2 * count :]).astype(jnp.bfloat16)


def expert_apply(near, far, other, scale, gate_weight, up_weight, out_weight):
    count, latent_width = near.shape
    hidden_width = gate_weight.shape[2]
    block = 512
    steps = hidden_width // block
    whole = lambda array: pl.BlockSpec(array.shape, lambda i: (0,) * array.ndim)
    sums = jax.ShapeDtypeStruct((2 * count, latent_width), jnp.bfloat16)
    return pl.pallas_call(
        functools.partial(expert_kernel, steps),
        grid=(steps,),
        out_shape=(sums, sums),
        in_specs=[
            whole(near),
            whole(far),
            whole(other),
            whole(scale),
            pl.BlockSpec((1, latent_width, block), lambda i: (0, 0, i)),
            pl.BlockSpec((1, latent_width, block), lambda i: (0, 0, i)),
            pl.BlockSpec((1, block, latent_width), lambda i: (0, i, 0)),
        ],
        out_specs=(whole(sums), whole(sums)),
        scratch_shapes=[
            pltpu.VMEM((4 * count, latent_width), jnp.bfloat16),
            pltpu.VMEM((4 * count, latent_width), jnp.float32),
        ],
        compiler_params=pltpu.CompilerParams(vmem_limit_bytes=40 * 1024 * 1024),
        cost_estimate=pl.CostEstimate(
            flops=24 * count * latent_width * hidden_width,
            bytes_accessed=6 * latent_width * hidden_width,
            transcendentals=4 * count * hidden_width,
        ),
        name="expert",
    )(near, far, other, scale, gate_weight, up_weight, out_weight)


def body(
    tokens, expert_ids, route_scores, down_latent, gate_weight, up_weight, out_weight, up_latent
):
    group_count = lax.axis_size("grp")
    ep_count = lax.axis_size("ep")
    expert_count = group_count * ep_count * gate_weight.shape[0]
    group = lax.axis_index("grp")
    place = lax.axis_index("ep")
    side = lax.axis_index("rep") % 2
    token_count = tokens.shape[0]
    latent_width = down_latent.shape[1]
    pieces = ep_count // 2

    quarter = down_latent.shape[0] // 4
    down_piece = lax.dynamic_slice_in_dim(down_latent, (2 * side + group) * quarter, quarter, 0)
    down_pieces = gather_ep(down_piece)
    cut = tokens.reshape(token_count, ep_count, 2, 2 * quarter)
    kept = lax.dynamic_index_in_dim(cut, side, 2, keepdims=False)
    given = lax.dynamic_index_in_dim(cut, 1 - side, 2, keepdims=False)
    inner = jnp.concatenate([kept, swap_reps(given)], axis=0)
    inner = inner.reshape(2 * token_count, ep_count, 2, quarter).transpose(1, 2, 0, 3)

    def columns(core, k):
        parts = [
            lax.dynamic_slice(
                inner, (place ^ (2 * k + y), core, 0, 0), (1, 1, 2 * token_count, quarter)
            )[0, 0]
            for y in range(2)
        ]
        return jnp.concatenate(parts, axis=1)

    partial = jnp.zeros((2 * token_count, latent_width), jnp.float32)
    for k, (near, far) in enumerate(down_pieces):
        both = jnp.concatenate([near, far], axis=0)
        swapped = swap_cores(both)
        partial += jnp.dot(columns(group, k), both, preferred_element_type=jnp.float32)
        partial += jnp.dot(columns(1 - group, k), swapped, preferred_element_type=jnp.float32)
    arrived = swap_reps(partial[token_count:].astype(jnp.bfloat16))
    latent = (partial[:token_count] + arrived.astype(jnp.float32)).astype(jnp.bfloat16)

    weights = dense_weights(expert_ids, route_scores, expert_count)
    scale = lax.all_to_all(weights, ("grp", "ep"), split_axis=0, concat_axis=0, tiled=True)
    scale = scale.reshape(group_count, ep_count, token_count)

    def scale_of(k):
        rows = [
            lax.dynamic_slice(scale, (core, place ^ (2 * k + y), 0), (1, 1, token_count))
            for core in (group, 1 - group)
            for y in range(2)
        ]
        rows = jnp.concatenate(rows, axis=0).reshape(4 * token_count, 1)
        return jnp.broadcast_to(rows, (4 * token_count, 128))

    latent_pieces = gather_ep(latent)
    combined = jnp.zeros((token_count, latent_width), jnp.float32)
    for k, (near, far) in enumerate(latent_pieces):
        other = swap_cores(jnp.concatenate([near, far], axis=0))
        own_sum, other_sum = expert_apply(
            near, far, other, scale_of(k), gate_weight, up_weight, out_weight
        )
        chip = own_sum.astype(jnp.float32) + swap_cores(other_sum).astype(jnp.float32)
        away = swap_ep(chip[token_count:].astype(jnp.bfloat16), 1)
        pair = chip[:token_count] + away.astype(jnp.float32)
        if k == 0:
            combined += pair
        else:
            combined += swap_ep(pair.astype(jnp.bfloat16), 2 * k).astype(jnp.float32)
    combined = combined.astype(jnp.bfloat16)

    inner_quarter = latent_width // 4
    up_piece = lax.dynamic_slice_in_dim(
        up_latent, (2 * side + group) * inner_quarter, inner_quarter, 0
    )
    mine = lax.all_gather(up_piece, "ep", axis=0)
    across = swap_reps(mine)
    layer_out = 0.0
    for array, side_of, core_of in (
        (mine, side, group),
        (across, 1 - side, group),
        (swap_cores(mine), side, 1 - group),
        (swap_cores(across), 1 - side, 1 - group),
    ):
        part = lax.dynamic_slice_in_dim(
            combined, (2 * side_of + core_of) * inner_quarter, inner_quarter, 1
        )
        layer_out += jnp.einsum("tl,elw->tew", part, array, preferred_element_type=jnp.float32)
    return layer_out.astype(jnp.bfloat16).reshape(token_count, -1)


def solution(mesh):
    in_specs = (
        P(("rep", "grp", "ep"), None),
        P(("rep", "grp", "ep"), None),
        P(("rep", "grp", "ep"), None),
        P("ep", None),
        P(("grp", "ep"), None, None),
        P(("grp", "ep"), None, None),
        P(("grp", "ep"), None, None),
        P(None, "ep"),
    )
    out_specs = P(("rep", "grp", "ep"), None)
    return jax.shard_map(body, mesh=mesh, in_specs=in_specs, out_specs=out_specs, check_vma=False)
```

```python
import jax
import jax.numpy as jnp
from jax import lax
from jax.experimental import pallas as pl
from jax.experimental.pallas import tpu as pltpu
from jax.sharding import PartitionSpec as P

route_scale = 2.5
mebi = 1024 * 1024
in_vmem = pl.BlockSpec(memory_space=pltpu.VMEM)
anywhere = pl.BlockSpec(memory_space=pl.ANY)
after = lax.optimization_barrier


def swap_cores(array):
    return lax.ppermute(array, "grp", [(0, 1), (1, 0)])


def swap_reps(array):
    return lax.ppermute(array, "rep", [(i, i ^ 1) for i in range(lax.axis_size("rep"))])


def swap_ep(array, mask):
    return lax.ppermute(array, "ep", [(i, i ^ mask) for i in range(lax.axis_size("ep"))])


def gather_line(piece):
    line = [piece]
    for k in range(1, lax.axis_size("ep") // 2):
        low = k & -k
        line.append(swap_ep(line[k ^ low], 2 * low))
    return line


def dense_weights(expert_ids, route_scores, expert_count):
    sigmoids = jax.nn.sigmoid(route_scores)
    weights = (route_scale * sigmoids / jnp.sum(sigmoids, axis=1, keepdims=True)).astype(
        jnp.bfloat16
    )
    named = expert_ids[None, :, :] == jnp.arange(expert_count, dtype=jnp.int32)[:, None, None]
    return jnp.sum(jnp.where(named, weights.astype(jnp.float32)[None, :, :], 0.0), axis=2)


def expert_kernel(own, other, scale, gate, up, out, own_sum, other_sum, rows, hidden, held):
    count = own.shape[0]
    width = 256
    rows[:count] = own[...]
    rows[count:] = other[...]

    def products(start):
        columns = pl.ds(pl.multiple_of(start, width), width)
        return (
            jnp.dot(rows[...], gate[0, :, columns], preferred_element_type=jnp.float32),
            jnp.dot(rows[...], up[0, :, columns], preferred_element_type=jnp.float32),
        )

    def activate(gate_value, up_value, start):
        value = gate_value / (1.0 + jnp.exp(-gate_value)) * up_value
        hidden[:, pl.ds(pl.multiple_of(start, width), width)] = value.astype(jnp.bfloat16)

    hidden_width = gate.shape[2]
    held[0], held[1] = products(0)

    def step(i, carry):
        start = i * 2 * width
        first = products(start + width)
        activate(held[0], held[1], start)
        second = products(start + 2 * width)
        activate(*first, start + width)
        held[0], held[1] = second
        return carry

    steps = hidden_width // (2 * width)
    lax.fori_loop(0, steps - 1, step, 0)
    last = products(hidden_width - width)
    activate(held[0], held[1], hidden_width - 2 * width)
    activate(*last, hidden_width - width)

    def finish(i, carry):
        columns = pl.ds(pl.multiple_of(i * width, width), width)
        value = jnp.dot(hidden[...], out[0, :, columns], preferred_element_type=jnp.float32)
        value = (value * scale[:, :1]).astype(jnp.bfloat16)
        own_sum[:, columns] = value[:count]
        other_sum[:, columns] = value[count:]
        return carry

    lax.fori_loop(0, out.shape[2] // width, finish, 0)


def expert_apply(own, other, scale, gate_weight, up_weight, out_weight):
    count, latent_width = own.shape
    hidden_width = gate_weight.shape[2]
    sums = jax.ShapeDtypeStruct((count, latent_width), jnp.bfloat16)
    return pl.pallas_call(
        expert_kernel,
        out_shape=(sums, sums),
        in_specs=[in_vmem] * 6,
        out_specs=(in_vmem,) * 2,
        scratch_shapes=[
            pltpu.VMEM((2 * count, latent_width), jnp.bfloat16),
            pltpu.VMEM((2 * count, hidden_width), jnp.bfloat16),
            pltpu.VMEM((2, 2 * count, 256), jnp.float32),
        ],
        compiler_params=pltpu.CompilerParams(vmem_limit_bytes=16 * mebi),
        cost_estimate=pl.CostEstimate(
            flops=12 * count * latent_width * hidden_width,
            bytes_accessed=8 * count * latent_width,
            transcendentals=2 * count * hidden_width,
        ),
        name="expert",
    )(own, other, scale, gate_weight, up_weight, out_weight)


def project_kernel(order, *refs):
    terms, stacks, (layer_out, combined) = refs[:-10], refs[-10:-2], refs[-2:]
    quarter, block = stacks[0].shape[1:]

    @pl.when(pl.program_id(0) == 0)
    def _():
        total = terms[0][...].astype(jnp.float32)
        for term in terms[1:]:
            total += term[...].astype(jnp.float32)
        combined[...] = total.astype(jnp.bfloat16)

    for y in range(2):
        value = 0.0
        for source in range(4):
            columns = pl.ds(pl.multiple_of(order[1 + source] * quarter, quarter), quarter)
            value += jnp.dot(
                combined[:, columns], stacks[4 * y + source][0], preferred_element_type=jnp.float32
            )
        start = pl.multiple_of((order[5] ^ y) * block, block)
        layer_out[:, pl.ds(start, block)] = value.astype(jnp.bfloat16)


def project(order, terms, stacks):
    count, latent_width = terms[0].shape
    pieces, quarter, block = stacks[0].shape
    whole = pl.BlockSpec((count, latent_width), lambda i, order: (0, 0))
    return pl.pallas_call(
        project_kernel,
        grid_spec=pltpu.PrefetchScalarGridSpec(
            num_scalar_prefetch=1,
            grid=(pieces,),
            in_specs=[whole] * len(terms)
            + [pl.BlockSpec((1, quarter, block), lambda i, order: (i, 0, 0))] * len(stacks),
            out_specs=pl.BlockSpec((count, 2 * block), lambda i, order: (0, order[0] ^ i)),
            scratch_shapes=[pltpu.VMEM((count, latent_width), jnp.bfloat16)],
        ),
        out_shape=jax.ShapeDtypeStruct((count, 2 * pieces * block), jnp.bfloat16),
        compiler_params=pltpu.CompilerParams(vmem_limit_bytes=28 * mebi),
        cost_estimate=pl.CostEstimate(
            flops=4 * count * latent_width * pieces * block,
            bytes_accessed=8 * latent_width * pieces * block,
            transcendentals=0,
        ),
        name="project",
    )(order, *terms, *stacks)


def body(
    tokens, expert_ids, route_scores, down_latent, gate_weight, up_weight, out_weight, up_latent
):
    group_count = lax.axis_size("grp")
    ep_count = lax.axis_size("ep")
    expert_count = group_count * ep_count * gate_weight.shape[0]
    group = lax.axis_index("grp")
    place = lax.axis_index("ep")
    side = lax.axis_index("rep") % 2
    own_quarter = 2 * side + group
    token_count = tokens.shape[0]
    latent_width = down_latent.shape[1]
    pieces = ep_count // 2

    quarter = down_latent.shape[0] // 4
    line = gather_line(lax.dynamic_slice_in_dim(down_latent, own_quarter * quarter, quarter, 0))
    cut = tokens.reshape(token_count, ep_count, 2, 2 * quarter)
    kept = lax.dynamic_index_in_dim(cut, side, 2, keepdims=False)
    given = lax.dynamic_index_in_dim(cut, 1 - side, 2, keepdims=False)
    inner = jnp.concatenate([kept, swap_reps(given)], axis=0)
    inner = inner.reshape(2 * token_count, ep_count, 2, quarter).transpose(1, 2, 0, 3)

    weights = dense_weights(expert_ids, route_scores, expert_count)
    scale = lax.all_to_all(weights, ("grp", "ep"), split_axis=0, concat_axis=0, tiled=True)
    scale = scale.reshape(group_count, ep_count, token_count)

    def scale_of(offset):
        rows = [
            lax.dynamic_slice(scale, (core, place ^ offset, 0), (1, 1, token_count))
            for core in (group, 1 - group)
        ]
        rows = jnp.concatenate(rows, axis=0).reshape(2 * token_count, 1)
        return jnp.broadcast_to(rows, (2 * token_count, 128))

    def columns_of(core, k):
        parts = [
            lax.dynamic_slice(
                inner, (place ^ (2 * k + y), core, 0, 0), (1, 1, 2 * token_count, quarter)
            )[0, 0]
            for y in range(2)
        ]
        return jnp.concatenate(parts, axis=1)

    scales = [scale_of(offset) for offset in range(ep_count)]
    columns = [(columns_of(group, k), columns_of(1 - group, k)) for k in range(pieces)]
    line[-1], scales, columns = after((line[-1], scales, columns))

    inner_quarter = latent_width // 4
    up_piece = lax.dynamic_slice_in_dim(up_latent, own_quarter * inner_quarter, inner_quarter, 0)
    line[-1], up_piece = after((line[-1], up_piece))
    up_line = gather_line(up_piece)

    partial = jnp.zeros((2 * token_count, latent_width), jnp.float32)
    for k, near in enumerate(line):
        if k == pieces - 1:
            near, partial = after((near, partial))
        both = jnp.concatenate([near, swap_ep(near, 1)], axis=0)
        swapped = swap_cores(both)
        if k == pieces - 2:
            waiting = both, swapped
            continue
        if k == pieces - 1:
            for given, block in zip(columns[k - 1], waiting):
                partial += jnp.dot(given, block, preferred_element_type=jnp.float32)
        for given, block in zip(columns[k], (both, swapped)):
            partial += jnp.dot(given, block, preferred_element_type=jnp.float32)
    arrived = swap_reps(partial[token_count:].astype(jnp.bfloat16))
    latent = (partial[:token_count] + arrived.astype(jnp.float32)).astype(jnp.bfloat16)

    state = {("near", 0): latent}
    swaps = {}

    def fetch(k):
        low = k & -k
        state["near", k] = swap_ep(state["near", k ^ low], 2 * low)

    def fetch_far(k):
        state["far", k] = swap_ep(state["near", k], 1)

    def work(kind, k, previous):
        own = state[kind, k]
        operands = (own, swap_cores(own))
        if previous is not None:
            operands, previous = after((operands, previous))
        own_sum, other_sum = expert_apply(
            *operands, scales[2 * k + (kind == "far")], gate_weight, up_weight, out_weight
        )
        swaps[kind, k] = own_sum, swap_cores(other_sum)
        return own_sum

    def chip_sum(kind, k):
        own_sum, swapped = swaps[kind, k]
        return own_sum.astype(jnp.float32) + swapped.astype(jnp.float32)

    order_of_work = [("near", 0), ("far", 0)]
    for k in range(1, pieces):
        order_of_work += [("near", k), ("far", k)]
    order_of_work[-2:] = order_of_work[:-3:-1]
    for k in range(1, pieces):
        fetch(k)
    for k in range(pieces):
        fetch_far(k)
    sent, pairs, previous = {}, {}, None
    for number, (kind, k) in enumerate(order_of_work):
        token = work(kind, k, previous)
        previous = [token]
        done = order_of_work[number - 1] if number >= 1 else None
        if done is not None and done[0] == "far":
            sent[done[1]] = chip_sum(*done).astype(jnp.bfloat16)
            sent[done[1]], token = after((sent[done[1]], token))
            previous = [token, sent[done[1]]]
        if number >= 3:
            kind, k = order_of_work[number - 3]
            if kind == "far" and k < pieces - 1:
                away = swap_ep(sent[k], 1).astype(jnp.float32)
                pairs[k] = (chip_sum("near", k) + away).astype(jnp.bfloat16)
                pairs[k], token = after((pairs[k], token))
                previous = [token, pairs[k]]
    k = pieces - 1
    away = swap_ep(sent[k], 1).astype(jnp.float32)
    pairs[k] = (chip_sum("near", k) + away).astype(jnp.bfloat16)
    if k - 1 not in pairs:
        away = swap_ep(sent[k - 1], 1).astype(jnp.float32)
        pairs[k - 1] = (chip_sum("near", k - 1) + away).astype(jnp.bfloat16)
    terms = [pairs[0]] + [swap_ep(pairs[k], 2 * k) for k in range(1, pieces)]

    up_near = jnp.stack(up_line)
    up_far = swap_ep(up_near, 1)
    across_near, across_far = swap_reps(up_near), swap_reps(up_far)
    stacks = [
        up_near,
        across_near,
        swap_cores(up_near),
        swap_cores(across_near),
        up_far,
        across_far,
        swap_cores(up_far),
        swap_cores(across_far),
    ]

    order = jnp.stack(
        [
            place // 2,
            own_quarter,
            own_quarter ^ 2,
            own_quarter ^ 1,
            own_quarter ^ 3,
            place % 2,
        ]
    ).astype(jnp.int32)
    return project(order, terms, stacks)


def solution(mesh):
    in_specs = (
        P(("rep", "grp", "ep"), None),
        P(("rep", "grp", "ep"), None),
        P(("rep", "grp", "ep"), None),
        P("ep", None),
        P(("grp", "ep"), None, None),
        P(("grp", "ep"), None, None),
        P(("grp", "ep"), None, None),
        P(None, "ep"),
    )
    out_specs = P(("rep", "grp", "ep"), None)
    return jax.shard_map(body, mesh=mesh, in_specs=in_specs, out_specs=out_specs, check_vma=False)
```

```python
import functools

import jax
import jax.numpy as jnp
from jax import lax
from jax.experimental import pallas as pl
from jax.experimental.pallas import tpu as pltpu
from jax.sharding import PartitionSpec as P

route_scale = 2.5
mebi = 1024 * 1024
in_vmem = pl.BlockSpec(memory_space=pltpu.VMEM)
in_smem = pl.BlockSpec(memory_space=pltpu.SMEM)
anywhere = pl.BlockSpec(memory_space=pl.ANY)


def after(value, *others):
    return lax.optimization_barrier((value, *others))[0]


def join(*values):
    return lax.optimization_barrier(values)


def swap_cores(array):
    return lax.ppermute(array, "grp", [(0, 1), (1, 0)])


def swap_reps(array):
    return lax.ppermute(array, "rep", [(i, i ^ 1) for i in range(lax.axis_size("rep"))])


def swap_ep(array, mask):
    return lax.ppermute(array, "ep", [(i, i ^ mask) for i in range(lax.axis_size("ep"))])


def first_steps(piece, steps):
    return {0: piece} | {k: swap_ep(piece, 2 * k) for k in range(1, steps) if k & (k - 1) == 0}


def dense_weights(expert_ids, route_scores, expert_count):
    sigmoids = jax.nn.sigmoid(route_scores)
    weights = (route_scale * sigmoids / jnp.sum(sigmoids, axis=1, keepdims=True)).astype(
        jnp.bfloat16
    )
    named = expert_ids[None, :, :] == jnp.arange(expert_count, dtype=jnp.int32)[:, None, None]
    return jnp.sum(jnp.where(named, weights.astype(jnp.float32)[None, :, :], 0.0), axis=2)


def columns_kernel(ep_count, quarter, where, tokens, kept, given):
    place, side, group = where[0], where[1], where[2]
    for offset in range(ep_count):
        for core in range(2):
            to = pl.ds(((offset // 2 * 2 + core) * 2 + offset % 2) * quarter, quarter)
            shard = (place ^ offset) * 4 + (group ^ core)
            for half, part in ((side, kept), (1 - side, given)):
                start = pl.multiple_of((shard + 2 * half) * quarter, quarter)
                part[:, to] = tokens[:, pl.ds(start, quarter)]


def split_columns(tokens, ep_count, quarter, place, side, group):
    count = tokens.shape[0]
    if quarter % 128 == 0:
        half = jax.ShapeDtypeStruct((count, 2 * ep_count * quarter), tokens.dtype)
        return pl.pallas_call(
            functools.partial(columns_kernel, ep_count, quarter),
            out_shape=(half, half),
            in_specs=[in_smem, in_vmem],
            out_specs=(in_vmem, in_vmem),
            compiler_params=pltpu.CompilerParams(vmem_limit_bytes=8 * mebi),
            name="split_columns",
        )(jnp.stack([place, side, group]).astype(jnp.int32), tokens)
    cut = tokens.reshape(count, ep_count, 2, 2, quarter)
    parts = [], []
    for step in range(ep_count // 2):
        for core in (group, 1 - group):
            for offset in (2 * step, 2 * step + 1):
                for half, part in zip((side, 1 - side), parts):
                    start = (0, place ^ offset, half, core, 0)
                    part.append(lax.dynamic_slice(cut, start, (count, 1, 1, 1, quarter)))
    kept, given = [jnp.stack(part, axis=1).reshape(count, -1) for part in parts]
    return kept, given


def down_kernel(steps, last, *refs):
    (kept, given), blocks = refs[:2], refs[2 : 2 + 4 * len(steps)]
    so_far, results = (refs[-3], refs[-2:]) if last else (None, refs[-1:])
    depth = 2 * blocks[0].shape[0]
    width = 256
    for start in range(0, blocks[0].shape[1], width):
        columns = slice(start, start + width)
        total = 0.0 if so_far is None else so_far[:, columns]
        for i, step in enumerate(steps):
            for core in range(2):
                inner = pl.ds((2 * step + core) * depth, depth)
                rows = jnp.concatenate([kept[:, inner], given[:, inner]], axis=0)
                near, far = blocks[4 * i + 2 * core], blocks[4 * i + 2 * core + 1]
                block = jnp.concatenate([near[:, columns], far[:, columns]], axis=0)
                total += jnp.dot(rows, block, preferred_element_type=jnp.float32)
        if last:
            count = kept.shape[0]
            results[0][:, columns] = total[:count]
            results[1][:, columns] = total[count:].astype(jnp.bfloat16)
        else:
            results[0][:, columns] = total


def down_project(steps, kept, given, blocks, so_far=None):
    count, inner = kept.shape
    latent_width = blocks[0].shape[1]
    operands = (kept, given, *blocks) + (() if so_far is None else (so_far,))
    if so_far is None:
        shapes = (jax.ShapeDtypeStruct((2 * count, latent_width), jnp.float32),)
    else:
        shapes = (
            jax.ShapeDtypeStruct((count, latent_width), jnp.float32),
            jax.ShapeDtypeStruct((count, latent_width), jnp.bfloat16),
        )
    return pl.pallas_call(
        functools.partial(down_kernel, steps, so_far is not None),
        out_shape=shapes,
        in_specs=[in_vmem] * len(operands),
        out_specs=(in_vmem,) * len(shapes),
        compiler_params=pltpu.CompilerParams(vmem_limit_bytes=16 * mebi),
        cost_estimate=pl.CostEstimate(
            flops=16 * len(steps) * count * blocks[0].shape[0] * latent_width,
            bytes_accessed=2 * len(blocks) * blocks[0].shape[0] * latent_width,
            transcendentals=0,
        ),
        name="down_project",
    )(*operands)


def expert_kernel(positions, *refs):
    owns, others, scales = [refs[i * positions : (i + 1) * positions] for i in range(3)]
    gate, up, out = refs[3 * positions : 3 * positions + 3]
    sums = refs[3 * positions + 3 : 5 * positions + 3]
    rows, hidden, held = refs[-3:]
    count = owns[0].shape[0]
    width = 256
    for i in range(positions):
        rows[2 * i * count : (2 * i + 1) * count] = owns[i][...]
        rows[(2 * i + 1) * count : (2 * i + 2) * count] = others[i][...]

    def products(start):
        columns = pl.ds(pl.multiple_of(start, width), width)
        return (
            jnp.dot(rows[...], gate[0, :, columns], preferred_element_type=jnp.float32),
            jnp.dot(rows[...], up[0, :, columns], preferred_element_type=jnp.float32),
        )

    def activate(gate_value, up_value, start):
        value = gate_value / (1.0 + jnp.exp(-gate_value)) * up_value
        hidden[:, pl.ds(pl.multiple_of(start, width), width)] = value.astype(jnp.bfloat16)

    hidden_width = gate.shape[2]
    held[0], held[1] = products(0)

    def step(i, carry):
        start = i * 2 * width
        first = products(start + width)
        activate(held[0], held[1], start)
        second = products(start + 2 * width)
        activate(*first, start + width)
        held[0], held[1] = second
        return carry

    steps = hidden_width // (2 * width)
    lax.fori_loop(0, steps - 1, step, 0)
    last = products(hidden_width - width)
    activate(held[0], held[1], hidden_width - 2 * width)
    activate(*last, hidden_width - width)

    def finish(i, carry):
        columns = pl.ds(pl.multiple_of(i * width, width), width)
        value = jnp.dot(hidden[...], out[0, :, columns], preferred_element_type=jnp.float32)
        for j in range(positions):
            scaled = value[2 * j * count : 2 * (j + 1) * count] * scales[j][:, :1]
            sums[2 * j][:, columns] = scaled[:count].astype(jnp.bfloat16)
            sums[2 * j + 1][:, columns] = scaled[count:].astype(jnp.bfloat16)
        return carry

    lax.fori_loop(0, out.shape[2] // width, finish, 0)


def expert_apply(owns, others, scales, gate_weight, up_weight, out_weight):
    positions = len(owns)
    count, latent_width = owns[0].shape
    hidden_width = gate_weight.shape[2]
    rows = 2 * positions * count
    sums = jax.ShapeDtypeStruct((count, latent_width), jnp.bfloat16)
    return pl.pallas_call(
        functools.partial(expert_kernel, positions),
        out_shape=(sums,) * (2 * positions),
        in_specs=[in_vmem] * (3 * positions + 3),
        out_specs=(in_vmem,) * (2 * positions),
        scratch_shapes=[
            pltpu.VMEM((rows, latent_width), jnp.bfloat16),
            pltpu.VMEM((rows, hidden_width), jnp.bfloat16),
            pltpu.VMEM((2, rows, 256), jnp.float32),
        ],
        compiler_params=pltpu.CompilerParams(vmem_limit_bytes=16 * mebi),
        cost_estimate=pl.CostEstimate(
            flops=6 * rows * latent_width * hidden_width,
            bytes_accessed=4 * rows * latent_width,
            transcendentals=rows * hidden_width,
        ),
        name="expert",
    )(*owns, *others, *scales, gate_weight, up_weight, out_weight)


def project_kernel(rep_count, where, *refs):
    terms, refs = refs[:-8], refs[-8:]
    mine, swapped, layer_out, combined, held, blocks, read_sems, sems = refs
    inner, width = mine.shape[1:]
    ep_count = mine.shape[0] // rep_count
    group = where[0]

    def read(e, rep):
        shard = rep * ep_count + e
        return pltpu.make_async_copy(mine.at[shard], held.at[shard], read_sems.at[shard])

    for e in range(ep_count):
        for rep in range(rep_count):
            read(e, rep).start()
    total = terms[0][...].astype(jnp.float32)
    for term in terms[1:]:
        total += term[...].astype(jnp.float32)
    combined[...] = total.astype(jnp.bfloat16)

    def sent(e):
        columns = pl.ds(e * width, width)
        return pltpu.make_async_copy(blocks.at[:, columns], layer_out.at[:, columns], sems.at[e])

    for e in range(ep_count):
        value = 0.0
        for rep in range(rep_count):
            read(e, rep).wait()
            for core, array in ((1 - group, swapped), (group, held)):
                columns = pl.ds(pl.multiple_of((2 * rep + core) * inner, inner), inner)
                value += jnp.dot(
                    combined[:, columns],
                    array[rep * ep_count + e],
                    preferred_element_type=jnp.float32,
                )
        blocks[:, e * width : (e + 1) * width] = value.astype(jnp.bfloat16)
        sent(e).start()
    for e in range(ep_count):
        sent(e).wait()


def project(terms, mine, swapped, rep_count, group):
    count, latent_width = terms[0].shape
    shards, inner, width = mine.shape
    ep_count = shards // rep_count
    return pl.pallas_call(
        functools.partial(project_kernel, rep_count),
        in_specs=[in_smem] + [in_vmem] * len(terms) + [anywhere, in_vmem],
        out_specs=anywhere,
        out_shape=jax.ShapeDtypeStruct((count, ep_count * width), jnp.bfloat16),
        scratch_shapes=[
            pltpu.VMEM((count, latent_width), jnp.bfloat16),
            pltpu.VMEM(mine.shape, mine.dtype),
            pltpu.VMEM((count, ep_count * width), jnp.bfloat16),
            pltpu.SemaphoreType.DMA((shards,)),
            pltpu.SemaphoreType.DMA((ep_count,)),
        ],
        compiler_params=pltpu.CompilerParams(vmem_limit_bytes=16 * mebi),
        cost_estimate=pl.CostEstimate(
            flops=2 * count * latent_width * ep_count * width,
            bytes_accessed=2 * latent_width * ep_count * width,
            transcendentals=0,
        ),
        name="project",
    )(group.reshape(1).astype(jnp.int32), *terms, mine, swapped)


def body(
    tokens, expert_ids, route_scores, down_latent, gate_weight, up_weight, out_weight, up_latent
):
    rep_count = lax.axis_size("rep")
    group_count = lax.axis_size("grp")
    ep_count = lax.axis_size("ep")
    expert_count = group_count * ep_count * gate_weight.shape[0]
    rep, group, place = lax.axis_index("rep"), lax.axis_index("grp"), lax.axis_index("ep")
    side = rep % 2
    token_count = tokens.shape[0]
    latent_width = down_latent.shape[1]
    steps = ep_count // 2

    quarter = down_latent.shape[0] // 4
    kept, given = split_columns(tokens, ep_count, quarter, place, side, group)
    shard = after(down_latent, kept)

    def own_piece(core):
        start = (2 * side + core) * quarter
        return lax.dynamic_slice_in_dim(shard, start, quarter, 0)

    taken = swap_reps(given)
    near = first_steps(own_piece(group), steps)
    far = {0: swap_ep(near[0], 1)}
    weights = dense_weights(after(expert_ids, kept), route_scores, expert_count)
    near[1], far[0], weights = join(near[1], far[0], weights)
    far[1] = swap_ep(near[1], 1)
    others = {k: near[k] for k in near if k > 1}
    near[1], taken, *arrived = join(near[1], taken, *others.values())
    near.update(zip(others, arrived))

    scale = lax.all_to_all(weights, ("grp", "ep"), split_axis=0, concat_axis=0, tiled=True)
    scale = scale.reshape(group_count, ep_count, token_count)

    def scale_of(offset):
        rows = [
            lax.dynamic_slice(scale, (core, place ^ offset, 0), (1, 1, token_count))
            for core in (group, 1 - group)
        ]
        rows = jnp.concatenate(rows, axis=0).reshape(2 * token_count, 1)
        return jnp.broadcast_to(rows, (2 * token_count, 128))

    last = steps - 1
    for k in range(2, steps):
        if k & (k - 1):
            low = k & -k
            near[k] = swap_ep(near[k ^ low], 2 * low)
        if k == last:
            near[k], scale, far[1] = join(near[k], scale, far[1])
        far[k] = swap_ep(near[k], 1)
    scales = [scale_of(offset) for offset in range(ep_count)]
    blocks = []
    for k in range(steps):
        other = own_piece(1 - group) if k == 0 else swap_cores(near[k])
        blocks.append((near[k], far[k], other, swap_cores(far[k])))
    early = list(range(last))
    (partial,) = down_project(early, kept, taken, [b for k in early for b in blocks[k]])
    late = [after(blocks[-1][0], partial, *scales), *blocks[-1][1:]]
    own_part, sent_part = down_project([last], kept, taken, late, partial)
    latent = (own_part + swap_reps(sent_part).astype(jnp.float32)).astype(jnp.bfloat16)

    inner = latent_width // (2 * rep_count)
    up_piece = lax.dynamic_slice_in_dim(up_latent, (2 * rep + group) * inner, inner, 0)
    mine = lax.all_gather(after(up_piece, sent_part), ("rep", "ep"), axis=0)

    near = first_steps(latent, steps)
    far = {0: swap_ep(latent, 1)}
    away, sent, pairs, back = {}, {}, {}, {}

    def run(which, coming):
        owns = [(near, far)[y][k] for k, y in which]
        operands = owns + [swap_cores(own) for own in owns]
        if back:
            operands = join(*operands, *sent.values(), *pairs.values(), *[b[1] for b in back.values()])
        count = len(which)
        sums = expert_apply(
            operands[:count],
            operands[count : 2 * count],
            [scales[2 * k + y] for k, y in which],
            gate_weight,
            up_weight,
            out_weight,
        )
        names = [(table, key) for table, keys in coming for key in keys]
        sums = join(*sums, *[table[key] for table, key in names])
        for (table, key), value in zip(names, sums[2 * count :]):
            table[key] = value
        for i, (k, y) in enumerate(which):
            back[k, y] = sums[2 * i], swap_cores(sums[2 * i + 1])
            if y == 1:
                sent[k] = chip_sum(k, 1).astype(jnp.bfloat16)
        for k in list(sent):
            if k not in away:
                away[k] = swap_ep(sent[k], 1)

    def chip_sum(k, y):
        own, swapped = back[k, y]
        return own.astype(jnp.float32) + swapped.astype(jnp.float32)

    def pair_sum(k):
        return (chip_sum(k, 0) + away[k].astype(jnp.float32)).astype(jnp.bfloat16)

    calls = [[(0, 0)]] + [[(k - 1, 1), (k, 0)] for k in range(1, last)]
    calls += [[(last - 1, 1), (last, 1)], [(last, 0)]]
    coming = [(near, [k for k in near if k]), (far, [0])]
    for which in calls:
        returning = [k for k in away if k not in pairs]
        run(which, coming + [(away, returning)])
        for k in returning:
            if (k, 0) in back:
                pairs[k] = pair_sum(k)
        new_far = [k for k in near if k not in far]
        new_near = [
            k for k in range(1, steps) if k not in near and k ^ (k & -k) in near
        ]
        for k in new_far:
            far[k] = swap_ep(near[k], 1)
        for k in new_near:
            near[k] = swap_ep(near[k ^ (k & -k)], 2 * (k & -k))
        coming = [(near, new_near), (far, new_far)]
    mine = after(mine, back[last, 0][0])
    swapped = swap_cores(mine)
    for k in range(steps):
        if k not in pairs:
            pairs[k] = pair_sum(k)
    terms = [pairs[0]] + [swap_ep(pairs[k], 2 * k) for k in range(1, steps)]
    return project(terms, mine, swapped, rep_count, group)


def solution(mesh):
    in_specs = (
        P(("rep", "grp", "ep"), None),
        P(("rep", "grp", "ep"), None),
        P(("rep", "grp", "ep"), None),
        P("ep", None),
        P(("grp", "ep"), None, None),
        P(("grp", "ep"), None, None),
        P(("grp", "ep"), None, None),
        P(None, "ep"),
    )
    out_specs = P(("rep", "grp", "ep"), None)
    return jax.shard_map(body, mesh=mesh, in_specs=in_specs, out_specs=out_specs, check_vma=False)
```

```python
import functools

import jax
import jax.numpy as jnp
from jax import lax
from jax.experimental import pallas as pl
from jax.experimental.pallas import tpu as pltpu
from jax.sharding import PartitionSpec as P

route_scale = 2.5
mebi = 1024 * 1024
in_vmem = pl.BlockSpec(memory_space=pltpu.VMEM)
in_smem = pl.BlockSpec(memory_space=pltpu.SMEM)
in_hbm = pl.BlockSpec(memory_space=pltpu.HBM)
anywhere = pl.BlockSpec(memory_space=pl.ANY)


def after(value, *others):
    return lax.optimization_barrier((value, *others))[0]


def join(*values):
    return lax.optimization_barrier(values)


def swap_cores(array):
    return lax.ppermute(array, "grp", [(0, 1), (1, 0)])


def swap_reps(array):
    return lax.ppermute(array, "rep", [(i, i ^ 1) for i in range(lax.axis_size("rep"))])


def swap_ep(array, mask):
    return lax.ppermute(array, "ep", [(i, i ^ mask) for i in range(lax.axis_size("ep"))])


def first_steps(piece, steps):
    return {0: piece} | {k: swap_ep(piece, 2 * k) for k in range(1, steps) if k & (k - 1) == 0}


def dense_weights(expert_ids, route_scores, expert_count):
    sigmoids = jax.nn.sigmoid(route_scores)
    weights = (route_scale * sigmoids / jnp.sum(sigmoids, axis=1, keepdims=True)).astype(
        jnp.bfloat16
    )
    named = expert_ids[None, :, :] == jnp.arange(expert_count, dtype=jnp.int32)[:, None, None]
    return jnp.sum(jnp.where(named, weights.astype(jnp.float32)[None, :, :], 0.0), axis=2)


def columns_kernel(ep_count, quarter, where, tokens, kept, given):
    place, side, group = where[0], where[1], where[2]
    for offset in range(ep_count):
        for core in range(2):
            to = pl.ds(((offset // 2 * 2 + core) * 2 + offset % 2) * quarter, quarter)
            shard = (place ^ offset) * 4 + (group ^ core)
            for half, part in ((side, kept), (1 - side, given)):
                start = pl.multiple_of((shard + 2 * half) * quarter, quarter)
                part[:, to] = tokens[:, pl.ds(start, quarter)]


def split_columns(tokens, ep_count, quarter, place, side, group):
    count = tokens.shape[0]
    if quarter % 128 == 0:
        half = jax.ShapeDtypeStruct((count, 2 * ep_count * quarter), tokens.dtype)
        return pl.pallas_call(
            functools.partial(columns_kernel, ep_count, quarter),
            out_shape=(half, half),
            in_specs=[in_smem, in_vmem],
            out_specs=(in_vmem, in_vmem),
            compiler_params=pltpu.CompilerParams(vmem_limit_bytes=8 * mebi),
            name="split_columns",
        )(jnp.stack([place, side, group]).astype(jnp.int32), tokens)
    cut = tokens.reshape(count, ep_count, 2, 2, quarter)
    parts = [], []
    for step in range(ep_count // 2):
        for core in (group, 1 - group):
            for offset in (2 * step, 2 * step + 1):
                for half, part in zip((side, 1 - side), parts):
                    start = (0, place ^ offset, half, core, 0)
                    part.append(lax.dynamic_slice(cut, start, (count, 1, 1, 1, quarter)))
    kept, given = [jnp.stack(part, axis=1).reshape(count, -1) for part in parts]
    return kept, given


def down_kernel(steps, last, *refs):
    (kept, given), blocks = refs[:2], refs[2 : 2 + 4 * len(steps)]
    so_far, results = (refs[-3], refs[-2:]) if last else (None, refs[-1:])
    depth = 2 * blocks[0].shape[0]
    width = 256
    for start in range(0, blocks[0].shape[1], width):
        columns = slice(start, start + width)
        total = 0.0 if so_far is None else so_far[:, columns]
        for i, step in enumerate(steps):
            for core in range(2):
                inner = pl.ds((2 * step + core) * depth, depth)
                rows = jnp.concatenate([kept[:, inner], given[:, inner]], axis=0)
                near, far = blocks[4 * i + 2 * core], blocks[4 * i + 2 * core + 1]
                block = jnp.concatenate([near[:, columns], far[:, columns]], axis=0)
                total += jnp.dot(rows, block, preferred_element_type=jnp.float32)
        if last:
            count = kept.shape[0]
            results[0][:, columns] = total[:count]
            results[1][:, columns] = total[count:].astype(jnp.bfloat16)
        else:
            results[0][:, columns] = total


def down_project(steps, kept, given, blocks, so_far=None):
    count, inner = kept.shape
    latent_width = blocks[0].shape[1]
    operands = (kept, given, *blocks) + (() if so_far is None else (so_far,))
    if so_far is None:
        shapes = (jax.ShapeDtypeStruct((2 * count, latent_width), jnp.float32),)
    else:
        shapes = (
            jax.ShapeDtypeStruct((count, latent_width), jnp.float32),
            jax.ShapeDtypeStruct((count, latent_width), jnp.bfloat16),
        )
    return pl.pallas_call(
        functools.partial(down_kernel, steps, so_far is not None),
        out_shape=shapes,
        in_specs=[in_vmem] * len(operands),
        out_specs=(in_vmem,) * len(shapes),
        compiler_params=pltpu.CompilerParams(vmem_limit_bytes=16 * mebi),
        cost_estimate=pl.CostEstimate(
            flops=16 * len(steps) * count * blocks[0].shape[0] * latent_width,
            bytes_accessed=2 * len(blocks) * blocks[0].shape[0] * latent_width,
            transcendentals=0,
        ),
        name="down_project",
    )(*operands)


def latent_kernel(own_part, arrived, weights, piece):
    count = own_part.shape[0]
    total = own_part[...] + arrived[...].astype(jnp.float32)
    piece[:count] = total.astype(jnp.bfloat16)
    extra = piece.shape[0] - count
    piece[count:] = jnp.zeros((extra, piece.shape[1]), jnp.bfloat16)
    piece[count:, :count] = weights[...]


def finish_latent(own_part, arrived, weights):
    count, latent_width = own_part.shape
    return pl.pallas_call(
        latent_kernel,
        out_shape=jax.ShapeDtypeStruct((count + weights.shape[0], latent_width), jnp.bfloat16),
        in_specs=[in_vmem] * 3,
        out_specs=in_vmem,
        compiler_params=pltpu.CompilerParams(vmem_limit_bytes=4 * mebi),
        name="finish_latent",
    )(own_part, arrived, weights)


def expert_kernel(positions, count, where, *refs):
    pieces = refs[: 2 * positions]
    gate, up, out = refs[2 * positions : 2 * positions + 3]
    own_sums = refs[2 * positions + 3 : 3 * positions + 3]
    other_sums, rows, hidden, held, gate_block, up_block, out_block, sems = refs[-8:]
    width = 256
    blocks = gate.shape[2] // width

    def columns_at(start):
        return pl.ds(pl.multiple_of(start, width), width)

    def read(i, part):
        source, target = ((gate, gate_block), (up, up_block), (out, out_block))[part]
        columns = columns_at(i * width)
        return pltpu.make_async_copy(
            source.at[0, :, columns], target.at[:, columns], sems.at[part * blocks + i]
        )

    for i in range(blocks):
        read(i, 0).start()
        read(i, 1).start()
    for i in range(out.shape[2] // width):
        read(i, 2).start()
    for i, piece in enumerate(pieces):
        rows[i * count : (i + 1) * count] = piece[:count]

    def scale_of(piece):
        weights = piece[count:, :count].astype(jnp.float32)
        expert = lax.broadcasted_iota(jnp.int32, weights.shape, 0)
        line = jnp.sum(jnp.where(expert == where[0], weights, 0.0), axis=0, keepdims=True)
        row = lax.broadcasted_iota(jnp.int32, (count, count), 0)
        column = lax.broadcasted_iota(jnp.int32, (count, count), 1)
        return jnp.sum(jnp.where(row == column, line, 0.0), axis=1, keepdims=True)

    scales = [scale_of(piece) for piece in pieces]

    def arrive(i):
        read(i, 0).wait()
        read(i, 1).wait()

    def products(i):
        columns = columns_at(i * width)
        return (
            jnp.dot(rows[...], gate_block[:, columns], preferred_element_type=jnp.float32),
            jnp.dot(rows[...], up_block[:, columns], preferred_element_type=jnp.float32),
        )

    def activate(gate_value, up_value, i):
        value = gate_value / (1.0 + jnp.exp(-gate_value)) * up_value
        hidden[:, columns_at(i * width)] = value.astype(jnp.bfloat16)

    arrive(0)
    held[0], held[1] = products(0)

    def step(i, carry):
        arrive(2 * i + 1)
        arrive(2 * i + 2)
        first = products(2 * i + 1)
        activate(held[0], held[1], 2 * i)
        second = products(2 * i + 2)
        activate(*first, 2 * i + 1)
        held[0], held[1] = second
        return carry

    lax.fori_loop(0, blocks // 2 - 1, step, 0)
    arrive(blocks - 1)
    last = products(blocks - 1)
    activate(held[0], held[1], blocks - 2)
    activate(*last, blocks - 1)

    def finish(i, carry):
        columns = columns_at(i * width)
        read(i, 2).wait()
        value = jnp.dot(hidden[...], out_block[:, columns], preferred_element_type=jnp.float32)
        for j, scale in enumerate(scales):
            scaled = (value[j * count : (j + 1) * count] * scale).astype(jnp.bfloat16)
            if j < positions:
                own_sums[j][:, columns] = scaled
            else:
                other_sums[(j - positions) * count : (j - positions + 1) * count, columns] = scaled
        return carry

    lax.fori_loop(0, out.shape[2] // width, finish, 0)


def expert_apply(expert, owns, others, gate_weight, up_weight, out_weight, count):
    positions = len(owns)
    latent_width = owns[0].shape[1]
    hidden_width = gate_weight.shape[2]
    rows = 2 * positions * count
    own_sum = jax.ShapeDtypeStruct((count, latent_width), jnp.bfloat16)
    other_sums = jax.ShapeDtypeStruct((positions * count, latent_width), jnp.bfloat16)
    return pl.pallas_call(
        functools.partial(expert_kernel, positions, count),
        out_shape=(own_sum,) * positions + (other_sums,),
        in_specs=[in_smem] + [in_vmem] * (2 * positions) + [in_hbm] * 3,
        out_specs=(in_vmem,) * (positions + 1),
        scratch_shapes=[
            pltpu.VMEM((rows, latent_width), jnp.bfloat16),
            pltpu.VMEM((rows, hidden_width), jnp.bfloat16),
            pltpu.VMEM((2, rows, 256), jnp.float32),
            pltpu.VMEM((latent_width, hidden_width), jnp.bfloat16),
            pltpu.VMEM((latent_width, hidden_width), jnp.bfloat16),
            pltpu.VMEM((hidden_width, latent_width), jnp.bfloat16),
            pltpu.SemaphoreType.DMA(((2 * hidden_width + latent_width) // 256,)),
        ],
        compiler_params=pltpu.CompilerParams(vmem_limit_bytes=32 * mebi),
        cost_estimate=pl.CostEstimate(
            flops=6 * rows * latent_width * hidden_width,
            bytes_accessed=4 * rows * latent_width,
            transcendentals=rows * hidden_width,
        ),
        name="expert",
    )(expert, *owns, *others, gate_weight, up_weight, out_weight)


def project_kernel(where, *refs):
    terms, refs = refs[:-11], refs[-11:]
    mine, across, near_core, far_core, layer_out, combined, held, held_across, blocks = refs[:9]
    read_sems, sems = refs[9:]
    ep_count, inner, width = mine.shape

    def read(e, i):
        source, target = ((mine, held), (across, held_across))[i]
        return pltpu.make_async_copy(source.at[e], target.at[e], read_sems.at[2 * e + i])

    for e in range(ep_count):
        for i in range(2):
            read(e, i).start()
    total = terms[0][...].astype(jnp.float32)
    for term in terms[1:]:
        total += term[...].astype(jnp.float32)
    combined[...] = total.astype(jnp.bfloat16)

    def sent(e):
        columns = pl.ds(e * width, width)
        return pltpu.make_async_copy(blocks.at[:, columns], layer_out.at[:, columns], sems.at[e])

    for e in range(ep_count):
        value = 0.0
        for i, array in enumerate((near_core, far_core, held, held_across)):
            if i >= 2:
                read(e, i - 2).wait()
            columns = pl.ds(pl.multiple_of(where[i] * inner, inner), inner)
            value += jnp.dot(combined[:, columns], array[e], preferred_element_type=jnp.float32)
        blocks[:, e * width : (e + 1) * width] = value.astype(jnp.bfloat16)
        sent(e).start()
    for e in range(ep_count):
        sent(e).wait()


def project(where, terms, mine, across, near_core, far_core):
    count, latent_width = terms[0].shape
    ep_count, inner, width = mine.shape
    return pl.pallas_call(
        project_kernel,
        in_specs=[in_smem] + [in_vmem] * len(terms) + [in_hbm] * 2 + [in_vmem] * 2,
        out_specs=anywhere,
        out_shape=jax.ShapeDtypeStruct((count, ep_count * width), jnp.bfloat16),
        scratch_shapes=[
            pltpu.VMEM((count, latent_width), jnp.bfloat16),
            pltpu.VMEM(mine.shape, mine.dtype),
            pltpu.VMEM(mine.shape, mine.dtype),
            pltpu.VMEM((count, ep_count * width), jnp.bfloat16),
            pltpu.SemaphoreType.DMA((2 * ep_count,)),
            pltpu.SemaphoreType.DMA((ep_count,)),
        ],
        compiler_params=pltpu.CompilerParams(vmem_limit_bytes=16 * mebi),
        cost_estimate=pl.CostEstimate(
            flops=2 * count * latent_width * ep_count * width,
            bytes_accessed=2 * latent_width * ep_count * width,
            transcendentals=0,
        ),
        name="project",
    )(where, *terms, mine, across, near_core, far_core)


def body(
    tokens, expert_ids, route_scores, down_latent, gate_weight, up_weight, out_weight, up_latent
):
    group_count = lax.axis_size("grp")
    ep_count = lax.axis_size("ep")
    expert_count = group_count * ep_count * gate_weight.shape[0]
    rep, group, place = lax.axis_index("rep"), lax.axis_index("grp"), lax.axis_index("ep")
    side = rep % 2
    own_quarter = 2 * side + group
    token_count = tokens.shape[0]
    latent_width = down_latent.shape[1]
    steps = ep_count // 2
    last = steps - 1

    inner = latent_width // 4
    up_piece = lax.dynamic_slice_in_dim(up_latent, own_quarter * inner, inner, 0)
    mine = lax.all_gather(up_piece, "ep", axis=0)

    quarter = down_latent.shape[0] // 4

    def own_piece(core):
        return lax.dynamic_slice_in_dim(down_latent, (2 * side + core) * quarter, quarter, 0)

    kept, given = split_columns(tokens, ep_count, quarter, place, side, group)
    taken = swap_reps(given)
    near = first_steps(own_piece(group), steps)
    far = {0: swap_ep(near[0], 1)}
    near[1], kept = join(near[1], kept)
    far[1] = swap_ep(near[1], 1)
    weights = dense_weights(after(expert_ids, near[1]), route_scores, expert_count)
    others = {k: near[k] for k in near if k > 1}
    *arrived, weights = join(*others.values(), weights)
    near.update(zip(others, arrived))
    for k in range(2, steps):
        if k & (k - 1):
            low = k & -k
            near[k] = swap_ep(near[k ^ low], 2 * low)
        if k == last:
            near[k], far[1], taken = join(near[k], far[1], taken)
        far[k] = swap_ep(near[k], 1)
    blocks = []
    for k in range(steps):
        other = own_piece(1 - group) if k == 0 else swap_cores(near[k])
        blocks.append((near[k], far[k], other, swap_cores(far[k])))
    early = list(range(last))
    (partial,) = down_project(early, kept, taken, [b for k in early for b in blocks[k]])
    late = [after(blocks[-1][0], partial), *blocks[-1][1:]]
    own_part, sent_part = down_project([last], kept, taken, late, partial)
    latent = finish_latent(own_part, swap_reps(sent_part), weights.astype(jnp.bfloat16))

    gate_weight, up_weight, out_weight = [
        pltpu.with_memory_space_constraint(w, pltpu.HBM) for w in (gate_weight, up_weight, out_weight)
    ]
    expert = (group * ep_count + place).astype(jnp.int32).reshape(1)
    near = first_steps(latent, steps)
    far, away, sent, pairs, own_sums, swapped = {}, {}, {}, {}, {}, {}

    def run(which, coming, *waits):
        owns = [(near, far)[y][k] for k, y in which]
        operands = owns + [swap_cores(own) for own in owns]
        operands = join(*operands, *waits)[: len(operands)]
        count = len(which)
        sums = expert_apply(
            expert,
            operands[:count],
            operands[count:],
            gate_weight,
            up_weight,
            out_weight,
            token_count,
        )
        names = [(table, key) for table, keys in coming for key in keys]
        sums = join(*sums, *[table[key] for table, key in names])
        for (table, key), value in zip(names, sums[count + 1 :]):
            table[key] = value
        others = swap_cores(sums[count])
        for i, place_of in enumerate(which):
            own_sums[place_of] = sums[i]
            swapped[place_of] = others[i * token_count : (i + 1) * token_count]
        return sums[0]

    def chip_sum(k, y):
        return own_sums[k, y].astype(jnp.float32) + swapped[k, y].astype(jnp.float32)

    def send_far(k):
        sent[k] = chip_sum(k, 1).astype(jnp.bfloat16)
        away[k] = swap_ep(sent[k], 1)

    def pair_sum(k):
        pairs[k] = (chip_sum(k, 0) + away[k].astype(jnp.float32)).astype(jnp.bfloat16)

    def start_near(k):
        near[k] = swap_ep(near[k ^ (k & -k)], 2 * (k & -k))

    def start_far(k):
        far[k] = swap_ep(near[k], 1)

    gathered = {"mine": mine}
    powers = [k for k in near if k]
    run([(0, 0)], [(near, powers)])
    if last >= 3:
        start_near(3)
    start_far(2)
    run([(1, 0), (2, 0)], [(near, [3]), (far, [2]), (gathered, ["mine"])])
    mine = gathered["mine"]
    gathered["across"] = swap_reps(mine)
    returning = []
    for k in range(3, steps):
        start_far(k)
        if k == 3:
            start_far(0)
        coming = [(far, [0, k] if k == 3 else [k]), (away, returning)]
        if k + 1 < steps and k + 1 not in near:
            start_near(k + 1)
            coming.append((near, [k + 1]))
        run([(k, 0), (k - 1, 1)], coming, *pairs.values())
        for j in returning:
            pair_sum(j)
        send_far(k - 1)
        returning = [k - 1]
    start_far(1)
    near_home = chip_sum(1, 0).astype(jnp.bfloat16)
    run([(last, 1)], [(away, returning), (far, [1])], near_home, *sent.values(), *pairs.values())
    for j in returning:
        pair_sum(j)
    send_far(last)
    homeward = {"near": swap_ep(near_home, 2)}
    run(
        [(0, 1), (1, 1)],
        [(away, [last]), (gathered, ["across"]), (homeward, ["near"])],
        sent[last],
        *pairs.values(),
    )
    across = gathered["across"]
    pair_sum(last)
    send_far(0)
    far_home = chip_sum(1, 1).astype(jnp.bfloat16)
    pair_sum(0)
    terms = [pairs[0], homeward["near"], swap_ep(far_home, 3)]
    terms += [swap_ep(pairs[k], 2 * k) for k in range(2, steps)]

    where = [own_quarter ^ 1, own_quarter ^ 3, own_quarter, own_quarter ^ 2]
    where = jnp.stack(where).astype(jnp.int32)
    return project(where, terms, mine, across, swap_cores(mine), swap_cores(across))


def solution(mesh):
    in_specs = (
        P(("rep", "grp", "ep"), None),
        P(("rep", "grp", "ep"), None),
        P(("rep", "grp", "ep"), None),
        P("ep", None),
        P(("grp", "ep"), None, None),
        P(("grp", "ep"), None, None),
        P(("grp", "ep"), None, None),
        P(None, "ep"),
    )
    out_specs = P(("rep", "grp", "ep"), None)
    return jax.shard_map(body, mesh=mesh, in_specs=in_specs, out_specs=out_specs, check_vma=False)
```

```python
import functools

import jax
import jax.numpy as jnp
from jax import lax
from jax.experimental import pallas as pl
from jax.experimental.pallas import tpu as pltpu
from jax.sharding import PartitionSpec as P

route_scale = 2.5
mebi = 1024 * 1024
in_vmem = pl.BlockSpec(memory_space=pltpu.VMEM)
in_smem = pl.BlockSpec(memory_space=pltpu.SMEM)
in_hbm = pl.BlockSpec(memory_space=pltpu.HBM)
anywhere = pl.BlockSpec(memory_space=pl.ANY)


def after(value, *others):
    return lax.optimization_barrier((value, *others))[0]


def join(*values):
    return lax.optimization_barrier(values)


def swap_cores(array):
    return lax.ppermute(array, "grp", [(0, 1), (1, 0)])


def swap_reps(array):
    return lax.ppermute(array, "rep", [(i, i ^ 1) for i in range(lax.axis_size("rep"))])


def swap_ep(array, mask):
    return lax.ppermute(array, "ep", [(i, i ^ mask) for i in range(lax.axis_size("ep"))])


def first_steps(piece, steps):
    return {0: piece} | {k: swap_ep(piece, 2 * k) for k in range(1, steps) if k & (k - 1) == 0}


def dense_weights(expert_ids, route_scores, expert_count):
    sigmoids = jax.nn.sigmoid(route_scores)
    weights = (route_scale * sigmoids / jnp.sum(sigmoids, axis=1, keepdims=True)).astype(
        jnp.bfloat16
    )
    named = expert_ids[None, :, :] == jnp.arange(expert_count, dtype=jnp.int32)[:, None, None]
    return jnp.sum(jnp.where(named, weights.astype(jnp.float32)[None, :, :], 0.0), axis=2)


def columns_kernel(ep_count, quarter, where, tokens, kept, given):
    place, side, group = where[0], where[1], where[2]
    for offset in range(ep_count):
        for core in range(2):
            to = pl.ds(((offset // 2 * 2 + core) * 2 + offset % 2) * quarter, quarter)
            shard = (place ^ offset) * 4 + (group ^ core)
            for half, part in ((side, kept), (1 - side, given)):
                start = pl.multiple_of((shard + 2 * half) * quarter, quarter)
                part[:, to] = tokens[:, pl.ds(start, quarter)]


def split_columns(tokens, ep_count, quarter, place, side, group):
    count = tokens.shape[0]
    if quarter % 128 == 0:
        half = jax.ShapeDtypeStruct((count, 2 * ep_count * quarter), tokens.dtype)
        return pl.pallas_call(
            functools.partial(columns_kernel, ep_count, quarter),
            out_shape=(half, half),
            in_specs=[in_smem, in_vmem],
            out_specs=(in_vmem, in_vmem),
            compiler_params=pltpu.CompilerParams(vmem_limit_bytes=8 * mebi),
            name="split_columns",
        )(jnp.stack([place, side, group]).astype(jnp.int32), tokens)
    cut = tokens.reshape(count, ep_count, 2, 2, quarter)
    parts = [], []
    for step in range(ep_count // 2):
        for core in (group, 1 - group):
            for offset in (2 * step, 2 * step + 1):
                for half, part in zip((side, 1 - side), parts):
                    start = (0, place ^ offset, half, core, 0)
                    part.append(lax.dynamic_slice(cut, start, (count, 1, 1, 1, quarter)))
    kept, given = [jnp.stack(part, axis=1).reshape(count, -1) for part in parts]
    return kept, given


def down_kernel(steps, last, *refs):
    (kept, given), blocks = refs[:2], refs[2 : 2 + 4 * len(steps)]
    so_far, results = (refs[-3], refs[-2:]) if last else (None, refs[-1:])
    depth = 2 * blocks[0].shape[0]
    width = 256
    for start in range(0, blocks[0].shape[1], width):
        columns = slice(start, start + width)
        total = 0.0 if so_far is None else so_far[:, columns]
        for i, step in enumerate(steps):
            for core in range(2):
                inner = pl.ds((2 * step + core) * depth, depth)
                rows = jnp.concatenate([kept[:, inner], given[:, inner]], axis=0)
                near, far = blocks[4 * i + 2 * core], blocks[4 * i + 2 * core + 1]
                block = jnp.concatenate([near[:, columns], far[:, columns]], axis=0)
                total += jnp.dot(rows, block, preferred_element_type=jnp.float32)
        if last:
            count = kept.shape[0]
            results[0][:, columns] = total[:count]
            results[1][:, columns] = total[count:].astype(jnp.bfloat16)
        else:
            results[0][:, columns] = total


def down_project(steps, kept, given, blocks, so_far=None):
    count, inner = kept.shape
    latent_width = blocks[0].shape[1]
    operands = (kept, given, *blocks) + (() if so_far is None else (so_far,))
    if so_far is None:
        shapes = (jax.ShapeDtypeStruct((2 * count, latent_width), jnp.float32),)
    else:
        shapes = (
            jax.ShapeDtypeStruct((count, latent_width), jnp.float32),
            jax.ShapeDtypeStruct((count, latent_width), jnp.bfloat16),
        )
    return pl.pallas_call(
        functools.partial(down_kernel, steps, so_far is not None),
        out_shape=shapes,
        in_specs=[in_vmem] * len(operands),
        out_specs=(in_vmem,) * len(shapes),
        compiler_params=pltpu.CompilerParams(vmem_limit_bytes=16 * mebi),
        cost_estimate=pl.CostEstimate(
            flops=16 * len(steps) * count * blocks[0].shape[0] * latent_width,
            bytes_accessed=2 * len(blocks) * blocks[0].shape[0] * latent_width,
            transcendentals=0,
        ),
        name="down_project",
    )(*operands)


def latent_kernel(own_part, arrived, weights, piece):
    count = own_part.shape[0]
    total = own_part[...] + arrived[...].astype(jnp.float32)
    piece[:count] = total.astype(jnp.bfloat16)
    extra = piece.shape[0] - count
    piece[count:] = jnp.zeros((extra, piece.shape[1]), jnp.bfloat16)
    piece[count:, :count] = weights[...]


def finish_latent(own_part, arrived, weights):
    count, latent_width = own_part.shape
    return pl.pallas_call(
        latent_kernel,
        out_shape=jax.ShapeDtypeStruct((count + weights.shape[0], latent_width), jnp.bfloat16),
        in_specs=[in_vmem] * 3,
        out_specs=in_vmem,
        compiler_params=pltpu.CompilerParams(vmem_limit_bytes=4 * mebi),
        name="finish_latent",
    )(own_part, arrived, weights)


def expert_kernel(positions, count, stream, where, *refs):
    pieces = refs[: 2 * positions]
    gate, up, out = refs[2 * positions : 2 * positions + 3]
    own_sums = refs[2 * positions + 3 : 3 * positions + 3]
    other_sums, rows, hidden, held = refs[3 * positions + 3 : 3 * positions + 7]
    width = 256
    blocks = gate.shape[2] // width
    if stream:
        gate_block, up_block, out_block, sems = refs[-4:]
    else:
        gate_block, up_block, out_block = gate.at[0], up.at[0], out.at[0]

    def columns_at(start):
        return pl.ds(pl.multiple_of(start, width), width)

    def read(i, part):
        source, target = ((gate, gate_block), (up, up_block), (out, out_block))[part]
        columns = columns_at(i * width)
        return pltpu.make_async_copy(
            source.at[0, :, columns], target.at[:, columns], sems.at[part * blocks + i]
        )

    for i in range(blocks if stream else 0):
        read(i, 0).start()
        read(i, 1).start()
    for i in range(out.shape[2] // width if stream else 0):
        read(i, 2).start()
    for i, piece in enumerate(pieces):
        rows[i * count : (i + 1) * count] = piece[:count]

    def scale_of(piece):
        weights = piece[count:, :count].astype(jnp.float32)
        expert = lax.broadcasted_iota(jnp.int32, weights.shape, 0)
        line = jnp.sum(jnp.where(expert == where[0], weights, 0.0), axis=0, keepdims=True)
        row = lax.broadcasted_iota(jnp.int32, (count, count), 0)
        column = lax.broadcasted_iota(jnp.int32, (count, count), 1)
        return jnp.sum(jnp.where(row == column, line, 0.0), axis=1, keepdims=True)

    scales = [scale_of(piece) for piece in pieces]

    def arrive(i):
        if stream:
            read(i, 0).wait()
            read(i, 1).wait()

    def products(i):
        columns = columns_at(i * width)
        return (
            jnp.dot(rows[...], gate_block[:, columns], preferred_element_type=jnp.float32),
            jnp.dot(rows[...], up_block[:, columns], preferred_element_type=jnp.float32),
        )

    def activate(gate_value, up_value, i):
        value = gate_value / (1.0 + jnp.exp(-gate_value)) * up_value
        hidden[:, columns_at(i * width)] = value.astype(jnp.bfloat16)

    arrive(0)
    held[0], held[1] = products(0)

    def step(i, carry):
        arrive(2 * i + 1)
        arrive(2 * i + 2)
        first = products(2 * i + 1)
        activate(held[0], held[1], 2 * i)
        second = products(2 * i + 2)
        activate(*first, 2 * i + 1)
        held[0], held[1] = second
        return carry

    lax.fori_loop(0, blocks // 2 - 1, step, 0)
    arrive(blocks - 1)
    last = products(blocks - 1)
    activate(held[0], held[1], blocks - 2)
    activate(*last, blocks - 1)

    def finish(i, carry):
        columns = columns_at(i * width)
        if stream:
            read(i, 2).wait()
        value = jnp.dot(hidden[...], out_block[:, columns], preferred_element_type=jnp.float32)
        for j, scale in enumerate(scales):
            scaled = (value[j * count : (j + 1) * count] * scale).astype(jnp.bfloat16)
            if j < positions:
                own_sums[j][:, columns] = scaled
            else:
                other_sums[(j - positions) * count : (j - positions + 1) * count, columns] = scaled
        return carry

    lax.fori_loop(0, out.shape[2] // width, finish, 0)


def expert_apply(expert, owns, others, weights, count, stream):
    positions = len(owns)
    latent_width = owns[0].shape[1]
    hidden_width = weights[0].shape[2]
    rows = 2 * positions * count
    own_sum = jax.ShapeDtypeStruct((count, latent_width), jnp.bfloat16)
    other_sums = jax.ShapeDtypeStruct((positions * count, latent_width), jnp.bfloat16)
    scratch = [
        pltpu.VMEM((rows, latent_width), jnp.bfloat16),
        pltpu.VMEM((rows, hidden_width), jnp.bfloat16),
        pltpu.VMEM((2, rows, 256), jnp.float32),
    ]
    if stream:
        weights = [pltpu.with_memory_space_constraint(w, pltpu.HBM) for w in weights]
        scratch += [pltpu.VMEM(w.shape[1:], w.dtype) for w in weights]
        scratch += [pltpu.SemaphoreType.DMA(((2 * hidden_width + latent_width) // 256,))]
    return pl.pallas_call(
        functools.partial(expert_kernel, positions, count, stream),
        out_shape=(own_sum,) * positions + (other_sums,),
        in_specs=[in_smem]
        + [in_vmem] * (2 * positions)
        + [in_hbm if stream else in_vmem] * 3,
        out_specs=(in_vmem,) * (positions + 1),
        scratch_shapes=scratch,
        compiler_params=pltpu.CompilerParams(vmem_limit_bytes=(24 if stream else 14) * mebi),
        cost_estimate=pl.CostEstimate(
            flops=6 * rows * latent_width * hidden_width,
            bytes_accessed=4 * rows * latent_width,
            transcendentals=rows * hidden_width,
        ),
        name="expert",
    )(expert, *owns, *others, *weights)


def project_kernel(where, *refs):
    terms, refs = refs[:-11], refs[-11:]
    mine, across, near_core, far_core, layer_out, combined, held, held_across, blocks = refs[:9]
    read_sems, sems = refs[9:]
    ep_count, inner, width = mine.shape

    def read(e, i):
        source, target = ((mine, held), (across, held_across))[i]
        return pltpu.make_async_copy(source.at[e], target.at[e], read_sems.at[2 * e + i])

    for e in range(ep_count):
        for i in range(2):
            read(e, i).start()
    total = terms[0][...].astype(jnp.float32)
    for term in terms[1:]:
        total += term[...].astype(jnp.float32)
    combined[...] = total.astype(jnp.bfloat16)

    def sent(e):
        columns = pl.ds(e * width, width)
        return pltpu.make_async_copy(blocks.at[:, columns], layer_out.at[:, columns], sems.at[e])

    for e in range(ep_count):
        value = 0.0
        for i, array in enumerate((near_core, far_core, held, held_across)):
            if i >= 2:
                read(e, i - 2).wait()
            columns = pl.ds(pl.multiple_of(where[i] * inner, inner), inner)
            value += jnp.dot(combined[:, columns], array[e], preferred_element_type=jnp.float32)
        blocks[:, e * width : (e + 1) * width] = value.astype(jnp.bfloat16)
        sent(e).start()
    for e in range(ep_count):
        sent(e).wait()


def project(where, terms, mine, across, near_core, far_core):
    count, latent_width = terms[0].shape
    ep_count, inner, width = mine.shape
    return pl.pallas_call(
        project_kernel,
        in_specs=[in_smem] + [in_vmem] * len(terms) + [in_hbm] * 2 + [in_vmem] * 2,
        out_specs=anywhere,
        out_shape=jax.ShapeDtypeStruct((count, ep_count * width), jnp.bfloat16),
        scratch_shapes=[
            pltpu.VMEM((count, latent_width), jnp.bfloat16),
            pltpu.VMEM(mine.shape, mine.dtype),
            pltpu.VMEM(mine.shape, mine.dtype),
            pltpu.VMEM((count, ep_count * width), jnp.bfloat16),
            pltpu.SemaphoreType.DMA((2 * ep_count,)),
            pltpu.SemaphoreType.DMA((ep_count,)),
        ],
        compiler_params=pltpu.CompilerParams(vmem_limit_bytes=16 * mebi),
        cost_estimate=pl.CostEstimate(
            flops=2 * count * latent_width * ep_count * width,
            bytes_accessed=2 * latent_width * ep_count * width,
            transcendentals=0,
        ),
        name="project",
    )(where, *terms, mine, across, near_core, far_core)


def body(
    tokens, expert_ids, route_scores, down_latent, gate_weight, up_weight, out_weight, up_latent
):
    group_count = lax.axis_size("grp")
    ep_count = lax.axis_size("ep")
    expert_count = group_count * ep_count * gate_weight.shape[0]
    rep, group, place = lax.axis_index("rep"), lax.axis_index("grp"), lax.axis_index("ep")
    side = rep % 2
    own_quarter = 2 * side + group
    token_count = tokens.shape[0]
    latent_width = down_latent.shape[1]
    steps = ep_count // 2
    last = steps - 1

    inner = latent_width // 4
    up_piece = lax.dynamic_slice_in_dim(up_latent, own_quarter * inner, inner, 0)
    mine = lax.all_gather(up_piece, "ep", axis=0)

    quarter = down_latent.shape[0] // 4

    def own_piece(core):
        return lax.dynamic_slice_in_dim(down_latent, (2 * side + core) * quarter, quarter, 0)

    kept, given = split_columns(tokens, ep_count, quarter, place, side, group)
    taken = swap_reps(given)
    near = first_steps(own_piece(group), steps)
    far = {0: swap_ep(near[0], 1)}
    near[1], kept = join(near[1], kept)
    far[1] = swap_ep(near[1], 1)
    weights = dense_weights(after(expert_ids, near[1]), route_scores, expert_count)
    others = {k: near[k] for k in near if k > 1}
    far[1], weights, *arrived = join(far[1], weights, *others.values())
    near.update(zip(others, arrived))
    for k in range(2, steps):
        if k & (k - 1):
            low = k & -k
            near[k] = swap_ep(near[k ^ low], 2 * low)
        if k == last:
            near[k], far[0], taken = join(near[k], far[0], taken)
        far[k] = swap_ep(near[k], 1)
    blocks = []
    for k in range(steps):
        other = own_piece(1 - group) if k == 0 else swap_cores(near[k])
        blocks.append((near[k], far[k], other, swap_cores(far[k])))
    early = list(range(last))
    (partial,) = down_project(early, kept, taken, [b for k in early for b in blocks[k]])
    late = [after(blocks[-1][0], partial), *blocks[-1][1:]]
    own_part, sent_part = down_project([last], kept, taken, late, partial)
    arrived, mine = join(swap_reps(sent_part), mine)
    latent = finish_latent(own_part, arrived, weights.astype(jnp.bfloat16))

    sides = [[i, i + 1] for i in range(0, lax.axis_size("rep"), 2)]
    both_sides = lax.all_gather(mine, "rep", axis=0, axis_index_groups=sides)

    expert = (group * ep_count + place).astype(jnp.int32).reshape(1)
    near = first_steps(latent, steps)
    far, away, sent, pairs, own_sums, swapped = {}, {}, {}, {}, {}, {}

    def run(which, coming, *waits):
        owns = [(near, far)[y][k] for k, y in which]
        operands = owns + [swap_cores(own) for own in owns]
        operands = join(*operands, *waits)[: len(operands)]
        count = len(which)
        sums = expert_apply(
            expert,
            operands[:count],
            operands[count:],
            (gate_weight, up_weight, out_weight),
            token_count,
            len(own_sums) <= 1,
        )
        names = [(table, key) for table, keys in coming for key in keys]
        sums = join(*sums, *[table[key] for table, key in names])
        for (table, key), value in zip(names, sums[count + 1 :]):
            table[key] = value
        others = swap_cores(sums[count])
        for i, place_of in enumerate(which):
            own_sums[place_of] = sums[i]
            swapped[place_of] = others[i * token_count : (i + 1) * token_count]
        return sums[0]

    def chip_sum(k, y):
        return own_sums[k, y].astype(jnp.float32) + swapped[k, y].astype(jnp.float32)

    def send_far(k):
        sent[k] = chip_sum(k, 1).astype(jnp.bfloat16)
        away[k] = swap_ep(sent[k], 1)

    def pair_sum(k):
        pairs[k] = (chip_sum(k, 0) + away[k].astype(jnp.float32)).astype(jnp.bfloat16)

    def start_near(k):
        near[k] = swap_ep(near[k ^ (k & -k)], 2 * (k & -k))

    def start_far(k):
        far[k] = swap_ep(near[k], 1)

    powers = [k for k in near if k]
    run([(0, 0)], [(near, powers)])
    if last >= 3:
        start_near(3)
    start_far(2)
    run([(1, 0), (2, 0)], [(near, [3] if last >= 3 else []), (far, [2])])
    returning = []
    for k in range(3, steps):
        start_far(k)
        if k == 3:
            start_far(0)
        coming = [(far, [0, k] if k == 3 else [k]), (away, returning)]
        if k + 1 < steps and k + 1 not in near:
            start_near(k + 1)
            coming.append((near, [k + 1]))
        run([(k, 0), (k - 1, 1)], coming, *pairs.values())
        for j in returning:
            pair_sum(j)
        send_far(k - 1)
        returning = [k - 1]
    start_far(1)
    near_home = chip_sum(1, 0).astype(jnp.bfloat16)
    run([(last, 1)], [(away, returning), (far, [1])], near_home, *sent.values(), *pairs.values())
    for j in returning:
        pair_sum(j)
    send_far(last)
    homeward = {"near": swap_ep(near_home, 2)}
    run(
        [(0, 1), (1, 1)],
        [(away, [last]), (homeward, ["near"])],
        sent[last],
        *pairs.values(),
    )
    pair_sum(last)
    send_far(0)
    far_home = chip_sum(1, 1).astype(jnp.bfloat16)
    pair_sum(0)
    terms = [pairs[0], homeward["near"], swap_ep(far_home, 3)]
    terms += [swap_ep(pairs[k], 2 * k) for k in range(2, steps)]

    both_sides = after(both_sides, pairs[0])
    across = lax.dynamic_index_in_dim(both_sides, 1 - side, 0, keepdims=False)
    where = [own_quarter ^ 1, own_quarter ^ 3, own_quarter, own_quarter ^ 2]
    where = jnp.stack(where).astype(jnp.int32)
    return project(where, terms, mine, across, swap_cores(mine), swap_cores(across))


def solution(mesh):
    in_specs = (
        P(("rep", "grp", "ep"), None),
        P(("rep", "grp", "ep"), None),
        P(("rep", "grp", "ep"), None),
        P("ep", None),
        P(("grp", "ep"), None, None),
        P(("grp", "ep"), None, None),
        P(("grp", "ep"), None, None),
        P(None, "ep"),
    )
    out_specs = P(("rep", "grp", "ep"), None)
    return jax.shard_map(body, mesh=mesh, in_specs=in_specs, out_specs=out_specs, check_vma=False)
```

```python
import functools

import jax
import jax.numpy as jnp
from jax import lax
from jax.experimental import pallas as pl
from jax.experimental.pallas import tpu as pltpu
from jax.sharding import PartitionSpec as P

route_scale = 2.5
mebi = 1024 * 1024
in_vmem = pl.BlockSpec(memory_space=pltpu.VMEM)
in_smem = pl.BlockSpec(memory_space=pltpu.SMEM)
in_hbm = pl.BlockSpec(memory_space=pltpu.HBM)
anywhere = pl.BlockSpec(memory_space=pl.ANY)


def after(value, *others):
    return lax.optimization_barrier((value, *others))[0]


def join(*values):
    return lax.optimization_barrier(values)


def swap_cores(array):
    return lax.ppermute(array, "grp", [(0, 1), (1, 0)])


def swap_reps(array):
    return lax.ppermute(array, "rep", [(i, i ^ 1) for i in range(lax.axis_size("rep"))])


def swap_ep(array, mask):
    return lax.ppermute(array, "ep", [(i, i ^ mask) for i in range(lax.axis_size("ep"))])


def first_steps(piece, steps):
    return {0: piece} | {k: swap_ep(piece, 2 * k) for k in range(1, steps) if k & (k - 1) == 0}


def dense_weights(expert_ids, route_scores, expert_count):
    sigmoids = jax.nn.sigmoid(route_scores)
    weights = (route_scale * sigmoids / jnp.sum(sigmoids, axis=1, keepdims=True)).astype(
        jnp.bfloat16
    )
    named = expert_ids[None, :, :] == jnp.arange(expert_count, dtype=jnp.int32)[:, None, None]
    return jnp.sum(jnp.where(named, weights.astype(jnp.float32)[None, :, :], 0.0), axis=2)


def columns_kernel(ep_count, quarter, where, tokens, kept, given):
    place, side, group = where[0], where[1], where[2]
    for offset in range(ep_count):
        for core in range(2):
            to = pl.ds(((offset // 2 * 2 + core) * 2 + offset % 2) * quarter, quarter)
            shard = (place ^ offset) * 4 + (group ^ core)
            for half, part in ((side, kept), (1 - side, given)):
                start = pl.multiple_of((shard + 2 * half) * quarter, quarter)
                part[:, to] = tokens[:, pl.ds(start, quarter)]


def split_columns(tokens, ep_count, quarter, place, side, group):
    count = tokens.shape[0]
    if quarter % 128 == 0:
        half = jax.ShapeDtypeStruct((count, 2 * ep_count * quarter), tokens.dtype)
        return pl.pallas_call(
            functools.partial(columns_kernel, ep_count, quarter),
            out_shape=(half, half),
            in_specs=[in_smem, in_vmem],
            out_specs=(in_vmem, in_vmem),
            compiler_params=pltpu.CompilerParams(vmem_limit_bytes=8 * mebi),
            name="split_columns",
        )(jnp.stack([place, side, group]).astype(jnp.int32), tokens)
    cut = tokens.reshape(count, ep_count, 2, 2, quarter)
    parts = [], []
    for step in range(ep_count // 2):
        for core in (group, 1 - group):
            for offset in (2 * step, 2 * step + 1):
                for half, part in zip((side, 1 - side), parts):
                    start = (0, place ^ offset, half, core, 0)
                    part.append(lax.dynamic_slice(cut, start, (count, 1, 1, 1, quarter)))
    kept, given = [jnp.stack(part, axis=1).reshape(count, -1) for part in parts]
    return kept, given


def down_kernel(steps, last, *refs):
    (kept, given), blocks = refs[:2], refs[2 : 2 + 4 * len(steps)]
    so_far, results = (refs[-3], refs[-2:]) if last else (None, refs[-1:])
    depth = 2 * blocks[0].shape[0]
    width = 256
    for start in range(0, blocks[0].shape[1], width):
        columns = slice(start, start + width)
        total = 0.0 if so_far is None else so_far[:, columns]
        for i, step in enumerate(steps):
            for core in range(2):
                inner = pl.ds((2 * step + core) * depth, depth)
                rows = jnp.concatenate([kept[:, inner], given[:, inner]], axis=0)
                near, far = blocks[4 * i + 2 * core], blocks[4 * i + 2 * core + 1]
                block = jnp.concatenate([near[:, columns], far[:, columns]], axis=0)
                total += jnp.dot(rows, block, preferred_element_type=jnp.float32)
        if last:
            count = kept.shape[0]
            results[0][:, columns] = total[:count]
            results[1][:, columns] = total[count:].astype(jnp.bfloat16)
        else:
            results[0][:, columns] = total


def down_project(steps, kept, given, blocks, so_far=None):
    count, inner = kept.shape
    latent_width = blocks[0].shape[1]
    operands = (kept, given, *blocks) + (() if so_far is None else (so_far,))
    if so_far is None:
        shapes = (jax.ShapeDtypeStruct((2 * count, latent_width), jnp.float32),)
    else:
        shapes = (
            jax.ShapeDtypeStruct((count, latent_width), jnp.float32),
            jax.ShapeDtypeStruct((count, latent_width), jnp.bfloat16),
        )
    return pl.pallas_call(
        functools.partial(down_kernel, steps, so_far is not None),
        out_shape=shapes,
        in_specs=[in_vmem] * len(operands),
        out_specs=(in_vmem,) * len(shapes),
        compiler_params=pltpu.CompilerParams(vmem_limit_bytes=16 * mebi),
        cost_estimate=pl.CostEstimate(
            flops=16 * len(steps) * count * blocks[0].shape[0] * latent_width,
            bytes_accessed=2 * len(blocks) * blocks[0].shape[0] * latent_width,
            transcendentals=0,
        ),
        name="down_project",
    )(*operands)


def latent_kernel(own_part, arrived, weights, piece):
    count = own_part.shape[0]
    total = own_part[...] + arrived[...].astype(jnp.float32)
    piece[:count] = total.astype(jnp.bfloat16)
    extra = piece.shape[0] - count
    piece[count:] = jnp.zeros((extra, piece.shape[1]), jnp.bfloat16)
    piece[count:, :count] = weights[...]


def finish_latent(own_part, arrived, weights):
    count, latent_width = own_part.shape
    return pl.pallas_call(
        latent_kernel,
        out_shape=jax.ShapeDtypeStruct((count + weights.shape[0], latent_width), jnp.bfloat16),
        in_specs=[in_vmem] * 3,
        out_specs=in_vmem,
        compiler_params=pltpu.CompilerParams(vmem_limit_bytes=4 * mebi),
        name="finish_latent",
    )(own_part, arrived, weights)


def expert_kernel(positions, count, where, *refs):
    pieces = refs[: 2 * positions]
    gate_first, up_first, gate, up, out = refs[2 * positions : 2 * positions + 5]
    own_sums, refs = refs[2 * positions + 5 : 3 * positions + 5], refs[3 * positions + 5 :]
    other_sums, rows, hidden, held, gate_block, up_block, out_block, sems = refs
    width = gate_first.shape[1]
    blocks = gate.shape[2] // width

    def columns_at(start):
        return pl.ds(pl.multiple_of(start, width), width)

    def read(i, part):
        source, target = ((gate, gate_block), (up, up_block), (out, out_block))[part]
        columns = columns_at(i * width)
        return pltpu.make_async_copy(
            source.at[0, :, columns], target.at[:, columns], sems.at[part * blocks + i]
        )

    for i in range(1, blocks):
        read(i, 0).start()
        read(i, 1).start()
    for i in range(out.shape[2] // width):
        read(i, 2).start()
    for i, piece in enumerate(pieces):
        rows[i * count : (i + 1) * count] = piece[:count]

    def scale_of(piece):
        weights = piece[count:, :count].astype(jnp.float32)
        expert = lax.broadcasted_iota(jnp.int32, weights.shape, 0)
        line = jnp.sum(jnp.where(expert == where[0], weights, 0.0), axis=0, keepdims=True)
        row = lax.broadcasted_iota(jnp.int32, (count, count), 0)
        column = lax.broadcasted_iota(jnp.int32, (count, count), 1)
        return jnp.sum(jnp.where(row == column, line, 0.0), axis=1, keepdims=True)

    scales = [scale_of(piece) for piece in pieces]

    def arrive(i):
        read(i, 0).wait()
        read(i, 1).wait()

    def dots(*blocks):
        return [jnp.dot(rows[...], b, preferred_element_type=jnp.float32) for b in blocks]

    def products(i):
        columns = columns_at(i * width)
        return dots(gate_block[:, columns], up_block[:, columns])

    def activate(gate_value, up_value, i):
        value = gate_value / (1.0 + jnp.exp(-gate_value)) * up_value
        hidden[:, columns_at(i * width)] = value.astype(jnp.bfloat16)

    held[0], held[1] = dots(gate_first[...], up_first[...])

    def step(i, carry):
        arrive(2 * i + 1)
        arrive(2 * i + 2)
        first = products(2 * i + 1)
        activate(held[0], held[1], 2 * i)
        second = products(2 * i + 2)
        activate(*first, 2 * i + 1)
        held[0], held[1] = second
        return carry

    lax.fori_loop(0, blocks // 2 - 1, step, 0)
    arrive(blocks - 1)
    last = products(blocks - 1)
    activate(held[0], held[1], blocks - 2)
    activate(*last, blocks - 1)

    def finish(i, carry):
        columns = columns_at(i * width)
        read(i, 2).wait()
        value = jnp.dot(hidden[...], out_block[:, columns], preferred_element_type=jnp.float32)
        for j, scale in enumerate(scales):
            scaled = (value[j * count : (j + 1) * count] * scale).astype(jnp.bfloat16)
            if j < positions:
                own_sums[j][:, columns] = scaled
            else:
                other_sums[(j - positions) * count : (j - positions + 1) * count, columns] = scaled
        return carry

    lax.fori_loop(0, out.shape[2] // width, finish, 0)


def expert_apply(expert, owns, others, firsts, weights, count):
    positions = len(owns)
    latent_width = owns[0].shape[1]
    hidden_width = weights[0].shape[2]
    rows, width = 2 * positions * count, firsts[0].shape[1]
    own_sum = jax.ShapeDtypeStruct((count, latent_width), jnp.bfloat16)
    other_sums = jax.ShapeDtypeStruct((positions * count, latent_width), jnp.bfloat16)
    return pl.pallas_call(
        functools.partial(expert_kernel, positions, count),
        out_shape=(own_sum,) * positions + (other_sums,),
        in_specs=[in_smem] + [in_vmem] * (2 * positions + 2) + [in_hbm] * 3,
        out_specs=(in_vmem,) * (positions + 1),
        scratch_shapes=[
            pltpu.VMEM((rows, latent_width), jnp.bfloat16),
            pltpu.VMEM((rows, hidden_width), jnp.bfloat16),
            pltpu.VMEM((2, rows, width), jnp.float32),
        ]
        + [pltpu.VMEM(w.shape[1:], w.dtype) for w in weights]
        + [pltpu.SemaphoreType.DMA(((2 * hidden_width + latent_width) // width,))],
        compiler_params=pltpu.CompilerParams(vmem_limit_bytes=28 * mebi),
        cost_estimate=pl.CostEstimate(
            flops=6 * rows * latent_width * hidden_width,
            bytes_accessed=4 * rows * latent_width,
            transcendentals=rows * hidden_width,
        ),
        name="expert",
    )(expert, *owns, *others, *firsts, *weights)


def project_kernel(where, *refs):
    terms, refs = refs[:-8], refs[-8:]
    mine, swapped, layer_out, combined, held, blocks, read_sems, sems = refs
    sides, ep_count, inner, width = mine.shape

    def read(e, side):
        return pltpu.make_async_copy(
            mine.at[side, e], held.at[side, e], read_sems.at[sides * e + side]
        )

    for e in range(ep_count):
        for side in range(sides):
            read(e, side).start()
    total = terms[0][...].astype(jnp.float32)
    for term in terms[1:]:
        total += term[...].astype(jnp.float32)
    combined[...] = total.astype(jnp.bfloat16)

    def sent(e):
        columns = pl.ds(e * width, width)
        return pltpu.make_async_copy(blocks.at[:, columns], layer_out.at[:, columns], sems.at[e])

    for e in range(ep_count):
        value = 0.0
        for side in range(sides):
            read(e, side).wait()
            for core, array in ((1 - where[0], swapped), (where[0], held)):
                columns = pl.ds(pl.multiple_of((2 * side + core) * inner, inner), inner)
                value += jnp.dot(
                    combined[:, columns], array[side, e], preferred_element_type=jnp.float32
                )
        blocks[:, e * width : (e + 1) * width] = value.astype(jnp.bfloat16)
        sent(e).start()
    for e in range(ep_count):
        sent(e).wait()


def project(group, terms, mine, swapped):
    count, latent_width = terms[0].shape
    sides, ep_count, inner, width = mine.shape
    return pl.pallas_call(
        project_kernel,
        in_specs=[in_smem] + [in_vmem] * len(terms) + [in_hbm, in_vmem],
        out_specs=anywhere,
        out_shape=jax.ShapeDtypeStruct((count, ep_count * width), jnp.bfloat16),
        scratch_shapes=[
            pltpu.VMEM((count, latent_width), jnp.bfloat16),
            pltpu.VMEM(mine.shape, mine.dtype),
            pltpu.VMEM((count, ep_count * width), jnp.bfloat16),
            pltpu.SemaphoreType.DMA((sides * ep_count,)),
            pltpu.SemaphoreType.DMA((ep_count,)),
        ],
        compiler_params=pltpu.CompilerParams(vmem_limit_bytes=16 * mebi),
        cost_estimate=pl.CostEstimate(
            flops=2 * count * latent_width * ep_count * width,
            bytes_accessed=2 * latent_width * ep_count * width,
            transcendentals=0,
        ),
        name="project",
    )(group.reshape(1).astype(jnp.int32), *terms, mine, swapped)


def body(
    tokens, expert_ids, route_scores, down_latent, gate_weight, up_weight, out_weight, up_latent
):
    group_count = lax.axis_size("grp")
    ep_count = lax.axis_size("ep")
    expert_count = group_count * ep_count * gate_weight.shape[0]
    rep, group, place = lax.axis_index("rep"), lax.axis_index("grp"), lax.axis_index("ep")
    side = rep % 2
    own_quarter = 2 * side + group
    token_count = tokens.shape[0]
    latent_width = down_latent.shape[1]
    steps = ep_count // 2
    last = steps - 1

    inner = latent_width // 4
    up_piece = lax.dynamic_slice_in_dim(up_latent, own_quarter * inner, inner, 0)
    mine = lax.all_gather(up_piece, "ep", axis=0)

    quarter = down_latent.shape[0] // 4

    def own_piece(core):
        return lax.dynamic_slice_in_dim(down_latent, (2 * side + core) * quarter, quarter, 0)

    kept, given = split_columns(tokens, ep_count, quarter, place, side, group)
    taken = swap_reps(given)
    near = first_steps(own_piece(group), steps)
    far = {0: swap_ep(near[0], 1)}
    near[1], kept = join(near[1], kept)
    far[1] = swap_ep(near[1], 1)
    weights = dense_weights(after(expert_ids, near[1]), route_scores, expert_count)
    others = {k: near[k] for k in near if k > 1}
    far[1], weights, *arrived = join(far[1], weights, *others.values())
    near.update(zip(others, arrived))
    for k in range(2, steps):
        if k & (k - 1):
            low = k & -k
            near[k] = swap_ep(near[k ^ low], 2 * low)
        if k == last:
            near[k], far[0], taken = join(near[k], far[0], taken)
        far[k] = swap_ep(near[k], 1)
    blocks = []
    for k in range(steps):
        other = own_piece(1 - group) if k == 0 else swap_cores(near[k])
        blocks.append((near[k], far[k], other, swap_cores(far[k])))
    early = list(range(last))
    (partial,) = down_project(early, kept, taken, [b for k in early for b in blocks[k]])
    late = [after(blocks[-1][0], partial), *blocks[-1][1:]]
    own_part, sent_part = down_project([last], kept, taken, late, partial)
    arrived, mine = join(swap_reps(sent_part), mine)
    latent = finish_latent(own_part, arrived, weights.astype(jnp.bfloat16))

    sides = [[i, i + 1] for i in range(0, lax.axis_size("rep"), 2)]
    both_sides = lax.all_gather(mine, "rep", axis=0, axis_index_groups=sides)

    expert = (group * ep_count + place).astype(jnp.int32).reshape(1)
    firsts = [w[0, :, :256] for w in (gate_weight, up_weight)]
    expert_weights = [
        pltpu.with_memory_space_constraint(w, pltpu.HBM)
        for w in (gate_weight, up_weight, out_weight)
    ]
    near = first_steps(latent, steps)
    far, away, sent, pairs, own_sums, swapped = {}, {}, {}, {}, {}, {}

    def run(which, coming, *waits):
        owns = [(near, far)[y][k] for k, y in which]
        operands = owns + [swap_cores(own) for own in owns]
        operands = join(*operands, *waits)[: len(operands)]
        count = len(which)
        sums = expert_apply(
            expert,
            operands[:count],
            operands[count:],
            firsts,
            expert_weights,
            token_count,
        )
        names = [(table, key) for table, keys in coming for key in keys]
        sums = join(*sums, *[table[key] for table, key in names])
        for (table, key), value in zip(names, sums[count + 1 :]):
            table[key] = value
        others = swap_cores(sums[count])
        for i, place_of in enumerate(which):
            own_sums[place_of] = sums[i]
            swapped[place_of] = others[i * token_count : (i + 1) * token_count]
        return sums[0]

    def chip_sum(k, y):
        return own_sums[k, y].astype(jnp.float32) + swapped[k, y].astype(jnp.float32)

    def send_far(k):
        sent[k] = chip_sum(k, 1).astype(jnp.bfloat16)
        away[k] = swap_ep(sent[k], 1)

    def pair_sum(k):
        pairs[k] = (chip_sum(k, 0) + away[k].astype(jnp.float32)).astype(jnp.bfloat16)

    def start_near(k):
        near[k] = swap_ep(near[k ^ (k & -k)], 2 * (k & -k))

    def start_far(k):
        far[k] = swap_ep(near[k], 1)

    powers = [k for k in near if k]
    run([(0, 0)], [(near, powers)])
    if last >= 3:
        start_near(3)
    start_far(2)
    run([(1, 0), (2, 0)], [(near, [3] if last >= 3 else []), (far, [2])])
    returning = []
    for k in range(3, steps):
        start_far(k)
        if k == 3:
            start_far(0)
        coming = [(far, [0, k] if k == 3 else [k]), (away, returning)]
        if k + 1 < steps and k + 1 not in near:
            start_near(k + 1)
            coming.append((near, [k + 1]))
        run([(k, 0), (k - 1, 1)], coming, *pairs.values())
        for j in returning:
            pair_sum(j)
        send_far(k - 1)
        returning = [k - 1]
    start_far(1)
    near_home = chip_sum(1, 0).astype(jnp.bfloat16)
    run([(last, 1)], [(away, returning), (far, [1])], near_home, *sent.values(), *pairs.values())
    for j in returning:
        pair_sum(j)
    send_far(last)
    homeward = {("near", 1): swap_ep(near_home, 2)}
    for k in range(2, last):
        homeward["pair", k] = swap_ep(pairs[k], 2 * k)
    run(
        [(0, 1), (1, 1)],
        [(away, [last]), (homeward, list(homeward))],
        sent[last],
        *pairs.values(),
    )
    pair_sum(last)
    send_far(0)
    homeward["far", 1] = swap_ep(chip_sum(1, 1).astype(jnp.bfloat16), 3)
    homeward["pair", last] = swap_ep(pairs[last], 2 * last)
    both_sides = after(both_sides, sent[0])
    terms = [own_sums[0, 0], swapped[0, 0], away[0], *homeward.values()]
    *terms, swapped_sides = join(*terms, swap_cores(both_sides))
    both_sides = pltpu.with_memory_space_constraint(both_sides, pltpu.HBM)
    return project(group, terms, both_sides, swapped_sides)


def solution(mesh):
    in_specs = (
        P(("rep", "grp", "ep"), None),
        P(("rep", "grp", "ep"), None),
        P(("rep", "grp", "ep"), None),
        P("ep", None),
        P(("grp", "ep"), None, None),
        P(("grp", "ep"), None, None),
        P(("grp", "ep"), None, None),
        P(None, "ep"),
    )
    out_specs = P(("rep", "grp", "ep"), None)
    return jax.shard_map(body, mesh=mesh, in_specs=in_specs, out_specs=out_specs, check_vma=False)
```

```python
import functools

import jax
import jax.numpy as jnp
from jax import lax
from jax.experimental import pallas as pl
from jax.experimental.pallas import tpu as pltpu
from jax.sharding import PartitionSpec as P

route_scale = 2.5
mebi = 1024 * 1024
in_vmem = pl.BlockSpec(memory_space=pltpu.VMEM)
in_smem = pl.BlockSpec(memory_space=pltpu.SMEM)
in_hbm = pl.BlockSpec(memory_space=pltpu.HBM)
anywhere = pl.BlockSpec(memory_space=pl.ANY)


def after(value, *others):
    return lax.optimization_barrier((value, *others))[0]


def join(*values):
    return lax.optimization_barrier(values)


def swap_cores(array):
    return lax.ppermute(array, "grp", [(0, 1), (1, 0)])


def swap_reps(array):
    return lax.ppermute(array, "rep", [(i, i ^ 1) for i in range(lax.axis_size("rep"))])


def swap_ep(array, mask):
    return lax.ppermute(array, "ep", [(i, i ^ mask) for i in range(lax.axis_size("ep"))])


def first_steps(piece, steps):
    return {0: piece} | {k: swap_ep(piece, 2 * k) for k in range(1, steps) if k & (k - 1) == 0}


def dense_weights(expert_ids, route_scores, expert_count):
    sigmoids = jax.nn.sigmoid(route_scores)
    weights = (route_scale * sigmoids / jnp.sum(sigmoids, axis=1, keepdims=True)).astype(
        jnp.bfloat16
    )
    named = expert_ids[None, :, :] == jnp.arange(expert_count, dtype=jnp.int32)[:, None, None]
    return jnp.sum(jnp.where(named, weights.astype(jnp.float32)[None, :, :], 0.0), axis=2)


def columns_kernel(ep_count, quarter, where, tokens, kept, given):
    place, side, group = where[0], where[1], where[2]
    for offset in range(ep_count):
        for core in range(2):
            to = pl.ds(((offset // 2 * 2 + core) * 2 + offset % 2) * quarter, quarter)
            shard = (place ^ offset) * 4 + (group ^ core)
            for half, part in ((side, kept), (1 - side, given)):
                start = pl.multiple_of((shard + 2 * half) * quarter, quarter)
                part[:, to] = tokens[:, pl.ds(start, quarter)]


def split_columns(tokens, ep_count, quarter, place, side, group):
    count = tokens.shape[0]
    if quarter % 128 == 0:
        half = jax.ShapeDtypeStruct((count, 2 * ep_count * quarter), tokens.dtype)
        return pl.pallas_call(
            functools.partial(columns_kernel, ep_count, quarter),
            out_shape=(half, half),
            in_specs=[in_smem, in_vmem],
            out_specs=(in_vmem, in_vmem),
            compiler_params=pltpu.CompilerParams(vmem_limit_bytes=8 * mebi),
            name="split_columns",
        )(jnp.stack([place, side, group]).astype(jnp.int32), tokens)
    cut = tokens.reshape(count, ep_count, 2, 2, quarter)
    parts = [], []
    for step in range(ep_count // 2):
        for core in (group, 1 - group):
            for offset in (2 * step, 2 * step + 1):
                for half, part in zip((side, 1 - side), parts):
                    start = (0, place ^ offset, half, core, 0)
                    part.append(lax.dynamic_slice(cut, start, (count, 1, 1, 1, quarter)))
    kept, given = [jnp.stack(part, axis=1).reshape(count, -1) for part in parts]
    return kept, given


def down_kernel(steps, last, *refs):
    (kept, given), blocks = refs[:2], refs[2 : 2 + 4 * len(steps)]
    so_far, results = (refs[-3], refs[-2:]) if last else (None, refs[-1:])
    depth = 2 * blocks[0].shape[0]
    width = 256
    for start in range(0, blocks[0].shape[1], width):
        columns = slice(start, start + width)
        total = 0.0 if so_far is None else so_far[:, columns]
        for i, step in enumerate(steps):
            for core in range(2):
                inner = pl.ds((2 * step + core) * depth, depth)
                rows = jnp.concatenate([kept[:, inner], given[:, inner]], axis=0)
                near, far = blocks[4 * i + 2 * core], blocks[4 * i + 2 * core + 1]
                block = jnp.concatenate([near[:, columns], far[:, columns]], axis=0)
                total += jnp.dot(rows, block, preferred_element_type=jnp.float32)
        if last:
            count = kept.shape[0]
            results[0][:, columns] = total[:count]
            results[1][:, columns] = total[count:].astype(jnp.bfloat16)
        else:
            results[0][:, columns] = total


def down_project(steps, kept, given, blocks, so_far=None):
    count, inner = kept.shape
    latent_width = blocks[0].shape[1]
    operands = (kept, given, *blocks) + (() if so_far is None else (so_far,))
    if so_far is None:
        shapes = (jax.ShapeDtypeStruct((2 * count, latent_width), jnp.float32),)
    else:
        shapes = (
            jax.ShapeDtypeStruct((count, latent_width), jnp.float32),
            jax.ShapeDtypeStruct((count, latent_width), jnp.bfloat16),
        )
    return pl.pallas_call(
        functools.partial(down_kernel, steps, so_far is not None),
        out_shape=shapes,
        in_specs=[in_vmem] * len(operands),
        out_specs=(in_vmem,) * len(shapes),
        compiler_params=pltpu.CompilerParams(vmem_limit_bytes=16 * mebi),
        cost_estimate=pl.CostEstimate(
            flops=16 * len(steps) * count * blocks[0].shape[0] * latent_width,
            bytes_accessed=2 * len(blocks) * blocks[0].shape[0] * latent_width,
            transcendentals=0,
        ),
        name="down_project",
    )(*operands)


def latent_kernel(own_part, arrived, weights, piece):
    count = own_part.shape[0]
    total = own_part[...] + arrived[...].astype(jnp.float32)
    piece[:count] = total.astype(jnp.bfloat16)
    extra = piece.shape[0] - count
    piece[count:] = jnp.zeros((extra, piece.shape[1]), jnp.bfloat16)
    piece[count:, :count] = weights[...]


def finish_latent(own_part, arrived, weights):
    count, latent_width = own_part.shape
    return pl.pallas_call(
        latent_kernel,
        out_shape=jax.ShapeDtypeStruct((count + weights.shape[0], latent_width), jnp.bfloat16),
        in_specs=[in_vmem] * 3,
        out_specs=in_vmem,
        compiler_params=pltpu.CompilerParams(vmem_limit_bytes=4 * mebi),
        name="finish_latent",
    )(own_part, arrived, weights)


def expert_kernel(positions, count, where, *refs):
    pieces = refs[: 2 * positions]
    gate, up, out = refs[2 * positions : 2 * positions + 3]
    own_sums, refs = refs[2 * positions + 3 : 3 * positions + 3], refs[3 * positions + 3 :]
    other_sums, rows, hidden, held, gate_block, up_block, out_block, sems = refs
    width = 256
    blocks = gate.shape[2] // width

    def columns_at(start):
        return pl.ds(pl.multiple_of(start, width), width)

    def read(i, part):
        source, target = ((gate, gate_block), (up, up_block), (out, out_block))[part]
        columns = columns_at(i * width)
        return pltpu.make_async_copy(
            source.at[0, :, columns], target.at[:, columns], sems.at[part * blocks + i]
        )

    for i in range(blocks):
        read(i, 0).start()
        read(i, 1).start()
    for i in range(out.shape[2] // width):
        read(i, 2).start()
    for i, piece in enumerate(pieces):
        rows[i * count : (i + 1) * count] = piece[:count]

    def scale_of(piece):
        weights = piece[count:, :count].astype(jnp.float32)
        expert = lax.broadcasted_iota(jnp.int32, weights.shape, 0)
        line = jnp.sum(jnp.where(expert == where[0], weights, 0.0), axis=0, keepdims=True)
        row = lax.broadcasted_iota(jnp.int32, (count, count), 0)
        column = lax.broadcasted_iota(jnp.int32, (count, count), 1)
        return jnp.sum(jnp.where(row == column, line, 0.0), axis=1, keepdims=True)

    scales = [scale_of(piece) for piece in pieces]

    def arrive(i):
        read(i, 0).wait()
        read(i, 1).wait()

    def products(i):
        columns = columns_at(i * width)
        return [
            jnp.dot(rows[...], block[:, columns], preferred_element_type=jnp.float32)
            for block in (gate_block, up_block)
        ]

    def activate(gate_value, up_value, i):
        value = gate_value / (1.0 + jnp.exp(-gate_value)) * up_value
        hidden[:, columns_at(i * width)] = value.astype(jnp.bfloat16)

    arrive(0)
    held[0], held[1] = products(0)

    def step(i, carry):
        arrive(2 * i + 1)
        arrive(2 * i + 2)
        first = products(2 * i + 1)
        activate(held[0], held[1], 2 * i)
        second = products(2 * i + 2)
        activate(*first, 2 * i + 1)
        held[0], held[1] = second
        return carry

    lax.fori_loop(0, blocks // 2 - 1, step, 0)
    arrive(blocks - 1)
    last = products(blocks - 1)
    activate(held[0], held[1], blocks - 2)
    activate(*last, blocks - 1)

    def finish(i, carry):
        columns = columns_at(i * width)
        read(i, 2).wait()
        value = jnp.dot(hidden[...], out_block[:, columns], preferred_element_type=jnp.float32)
        for j, scale in enumerate(scales):
            scaled = (value[j * count : (j + 1) * count] * scale).astype(jnp.bfloat16)
            if j < positions:
                own_sums[j][:, columns] = scaled
            else:
                other_sums[(j - positions) * count : (j - positions + 1) * count, columns] = scaled
        return carry

    lax.fori_loop(0, out.shape[2] // width, finish, 0)


def expert_apply(expert, owns, others, weights, count):
    positions = len(owns)
    latent_width = owns[0].shape[1]
    hidden_width = weights[0].shape[2]
    rows, width = 2 * positions * count, 256
    own_sum = jax.ShapeDtypeStruct((count, latent_width), jnp.bfloat16)
    other_sums = jax.ShapeDtypeStruct((positions * count, latent_width), jnp.bfloat16)
    return pl.pallas_call(
        functools.partial(expert_kernel, positions, count),
        out_shape=(own_sum,) * positions + (other_sums,),
        in_specs=[in_smem] + [in_vmem] * (2 * positions) + [in_hbm] * 3,
        out_specs=(in_vmem,) * (positions + 1),
        scratch_shapes=[
            pltpu.VMEM((rows, latent_width), jnp.bfloat16),
            pltpu.VMEM((rows, hidden_width), jnp.bfloat16),
            pltpu.VMEM((2, rows, width), jnp.float32),
        ]
        + [pltpu.VMEM(w.shape[1:], w.dtype) for w in weights]
        + [pltpu.SemaphoreType.DMA(((2 * hidden_width + latent_width) // width,))],
        compiler_params=pltpu.CompilerParams(vmem_limit_bytes=28 * mebi),
        cost_estimate=pl.CostEstimate(
            flops=3 * rows * latent_width * hidden_width // 2,
            bytes_accessed=4 * rows * latent_width,
            transcendentals=0,
        ),
        name="expert",
    )(expert, *owns, *others, *weights)


def project_kernel(where, *refs):
    terms, refs = refs[:-8], refs[-8:]
    mine, swapped, layer_out, combined, held, blocks, read_sems, sems = refs
    sides, ep_count, inner, width = mine.shape

    def read(e, side):
        return pltpu.make_async_copy(
            mine.at[side, e], held.at[side, e], read_sems.at[sides * e + side]
        )

    for e in range(ep_count):
        for side in range(sides):
            read(e, side).start()
    total = terms[0][...].astype(jnp.float32)
    for term in terms[1:]:
        total += term[...].astype(jnp.float32)
    combined[...] = total.astype(jnp.bfloat16)

    def sent(e):
        columns = pl.ds(e * width, width)
        return pltpu.make_async_copy(blocks.at[:, columns], layer_out.at[:, columns], sems.at[e])

    for e in range(ep_count):
        value = 0.0
        for side in range(sides):
            read(e, side).wait()
            for core, array in ((1 - where[0], swapped), (where[0], held)):
                columns = pl.ds(pl.multiple_of((2 * side + core) * inner, inner), inner)
                value += jnp.dot(
                    combined[:, columns], array[side, e], preferred_element_type=jnp.float32
                )
        blocks[:, e * width : (e + 1) * width] = value.astype(jnp.bfloat16)
        sent(e).start()
    for e in range(ep_count):
        sent(e).wait()


def project(group, terms, mine, swapped):
    count, latent_width = terms[0].shape
    sides, ep_count, inner, width = mine.shape
    return pl.pallas_call(
        project_kernel,
        in_specs=[in_smem] + [in_vmem] * len(terms) + [in_hbm, in_vmem],
        out_specs=anywhere,
        out_shape=jax.ShapeDtypeStruct((count, ep_count * width), jnp.bfloat16),
        scratch_shapes=[
            pltpu.VMEM((count, latent_width), jnp.bfloat16),
            pltpu.VMEM(mine.shape, mine.dtype),
            pltpu.VMEM((count, ep_count * width), jnp.bfloat16),
            pltpu.SemaphoreType.DMA((sides * ep_count,)),
            pltpu.SemaphoreType.DMA((ep_count,)),
        ],
        compiler_params=pltpu.CompilerParams(vmem_limit_bytes=16 * mebi),
        cost_estimate=pl.CostEstimate(
            flops=2 * count * latent_width * ep_count * width,
            bytes_accessed=2 * latent_width * ep_count * width,
            transcendentals=0,
        ),
        name="project",
    )(group.reshape(1).astype(jnp.int32), *terms, mine, swapped)


def body(
    tokens, expert_ids, route_scores, down_latent, gate_weight, up_weight, out_weight, up_latent
):
    group_count = lax.axis_size("grp")
    ep_count = lax.axis_size("ep")
    expert_count = group_count * ep_count * gate_weight.shape[0]
    rep, group, place = lax.axis_index("rep"), lax.axis_index("grp"), lax.axis_index("ep")
    side = rep % 2
    own_quarter = 2 * side + group
    token_count = tokens.shape[0]
    latent_width = down_latent.shape[1]
    steps = ep_count // 2
    last = steps - 1

    quarter = down_latent.shape[0] // 4

    def own_piece(core):
        return lax.dynamic_slice_in_dim(down_latent, (2 * side + core) * quarter, quarter, 0)

    kept, given = split_columns(tokens, ep_count, quarter, place, side, group)
    taken = swap_reps(given)
    near = first_steps(own_piece(group), steps)
    far = {0: swap_ep(near[0], 1)}
    near[1], kept = join(near[1], kept)
    far[1] = swap_ep(near[1], 1)

    inner = latent_width // 4
    up_piece = lax.dynamic_slice_in_dim(up_latent, own_quarter * inner, inner, 0)
    mine = lax.all_gather(up_piece, "ep", axis=0)
    weights = dense_weights(after(expert_ids, near[1]), route_scores, expert_count)
    others = {k: near[k] for k in near if k > 1}
    far[1], weights, *arrived = join(far[1], weights, *others.values())
    near.update(zip(others, arrived))
    for k in range(2, steps):
        if k & (k - 1):
            low = k & -k
            near[k] = swap_ep(near[k ^ low], 2 * low)
        if k == last:
            near[k], far[0], taken = join(near[k], far[0], taken)
        far[k] = swap_ep(near[k], 1)
    blocks = []
    for k in range(steps):
        other = own_piece(1 - group) if k == 0 else swap_cores(near[k])
        blocks.append((near[k], far[k], other, swap_cores(far[k])))
    early = list(range(last))
    (partial,) = down_project(early, kept, taken, [b for k in early for b in blocks[k]])
    late = [after(blocks[-1][0], partial), *blocks[-1][1:]]
    own_part, sent_part = down_project([last], kept, taken, late, partial)
    latent = finish_latent(own_part, swap_reps(sent_part), weights.astype(jnp.bfloat16))

    expert = (group * ep_count + place).astype(jnp.int32).reshape(1)
    expert_weights = [
        pltpu.with_memory_space_constraint(w, pltpu.HBM)
        for w in (gate_weight, up_weight, out_weight)
    ]
    near = first_steps(latent, steps)
    far = {0: swap_ep(latent, 1)}
    sums, travel, taken_in = {}, {"up": mine}, set()

    def start_near(k):
        near[k] = swap_ep(near[k ^ (k & -k)], 2 * (k & -k))
        return near, k

    def start_far(k):
        far[k] = swap_ep(near[k], 1)
        return far, k

    def send(name, value, mask):
        travel[name] = swap_ep(value.astype(jnp.bfloat16), mask)
        return travel, name

    def run(which, *coming):
        owns = [(near, far)[y][k] for k, y in which]
        operands = join(*owns, *[swap_cores(own) for own in owns])
        count = len(which)
        out = expert_apply(expert, operands[:count], operands[count:], expert_weights, token_count)
        out = join(*out, *[table[key] for table, key in coming])
        for (table, key), value in zip(coming, out[count + 1 :]):
            table[key] = value
        from_core = swap_cores(out[count])
        for i, place_of in enumerate(which):
            swapped = from_core[i * token_count : (i + 1) * token_count]
            sums[place_of] = out[i].astype(jnp.float32) + swapped.astype(jnp.float32)

    run([(0, 0)], (near, 1), (far, 0), (travel, "up"))
    sides = [[i, i + 1] for i in range(0, lax.axis_size("rep"), 2)]
    both_sides = lax.all_gather(travel.pop("up"), "rep", axis=0, axis_index_groups=sides)
    run([(1, 0), (0, 1)], *[(near, k) for k in near if k > 1], start_far(1))
    for k in range(2, steps):
        coming = [start_far(k)]
        for j in range(3, steps):
            if j not in near and j ^ (j & -j) == k:
                coming.append(start_near(j))
        previous = [(k - 2, 1)] if k == last else [(k - 2, 1), (k - 1, 0)]
        coming += [send(p, sums[p], 2 * p[0] + p[1]) for p in previous]
        run([(k, 0), (k - 1, 1)], *coming)
    run(
        [(last, 1)],
        send((last - 1, 1), sums[last - 1, 1], 1),
        send((last, 0), sums[last, 0], 2),
    )
    shared = sums[last - 1, 0]
    for name in ((last - 1, 1), (last, 0)):
        shared += travel.pop(name).astype(jnp.float32)
    send("shared", shared, 2 * last - 2)
    final = sums[last, 1].astype(jnp.bfloat16)
    both_sides = after(both_sides, final)
    send((last, 1), final, 2 * last + 1)
    *terms, swapped_sides = join(sums[0, 0], *travel.values(), swap_cores(both_sides))
    both_sides = pltpu.with_memory_space_constraint(both_sides, pltpu.HBM)
    return project(group, terms, both_sides, swapped_sides)


def solution(mesh):
    in_specs = (
        P(("rep", "grp", "ep"), None),
        P(("rep", "grp", "ep"), None),
        P(("rep", "grp", "ep"), None),
        P("ep", None),
        P(("grp", "ep"), None, None),
        P(("grp", "ep"), None, None),
        P(("grp", "ep"), None, None),
        P(None, "ep"),
    )
    out_specs = P(("rep", "grp", "ep"), None)
    return jax.shard_map(body, mesh=mesh, in_specs=in_specs, out_specs=out_specs, check_vma=False)
```

```python
import functools

import jax
import jax.numpy as jnp
from jax import lax
from jax.experimental import pallas as pl
from jax.experimental.pallas import tpu as pltpu
from jax.sharding import PartitionSpec as P

route_scale = 2.5
mebi = 1024 * 1024
in_vmem = pl.BlockSpec(memory_space=pltpu.VMEM)
in_smem = pl.BlockSpec(memory_space=pltpu.SMEM)
in_hbm = pl.BlockSpec(memory_space=pltpu.HBM)
anywhere = pl.BlockSpec(memory_space=pl.ANY)


def after(value, *others):
    return lax.optimization_barrier((value, *others))[0]


def join(*values):
    return lax.optimization_barrier(values)


def swap_cores(array):
    return lax.ppermute(array, "grp", [(0, 1), (1, 0)])


def swap_reps(array):
    return lax.ppermute(array, "rep", [(i, i ^ 1) for i in range(lax.axis_size("rep"))])


def swap_ep(array, mask):
    return lax.ppermute(array, "ep", [(i, i ^ mask) for i in range(lax.axis_size("ep"))])


def first_steps(piece, steps):
    return {0: piece} | {k: swap_ep(piece, 2 * k) for k in range(1, steps) if k & (k - 1) == 0}


def dense_weights(expert_ids, route_scores, expert_count):
    sigmoids = jax.nn.sigmoid(route_scores)
    weights = (route_scale * sigmoids / jnp.sum(sigmoids, axis=1, keepdims=True)).astype(
        jnp.bfloat16
    )
    named = expert_ids[None, :, :] == jnp.arange(expert_count, dtype=jnp.int32)[:, None, None]
    return jnp.sum(jnp.where(named, weights.astype(jnp.float32)[None, :, :], 0.0), axis=2)


def columns_kernel(ep_count, quarter, where, tokens, kept, given):
    place, side, group = where[0], where[1], where[2]
    for offset in range(ep_count):
        for core in range(2):
            to = pl.ds(((offset // 2 * 2 + core) * 2 + offset % 2) * quarter, quarter)
            shard = (place ^ offset) * 4 + (group ^ core)
            for half, part in ((side, kept), (1 - side, given)):
                start = pl.multiple_of((shard + 2 * half) * quarter, quarter)
                part[:, to] = tokens[:, pl.ds(start, quarter)]


def split_columns(tokens, ep_count, quarter, place, side, group):
    count = tokens.shape[0]
    if quarter % 128 == 0:
        half = jax.ShapeDtypeStruct((count, 2 * ep_count * quarter), tokens.dtype)
        return pl.pallas_call(
            functools.partial(columns_kernel, ep_count, quarter),
            out_shape=(half, half),
            in_specs=[in_smem, in_vmem],
            out_specs=(in_vmem, in_vmem),
            compiler_params=pltpu.CompilerParams(vmem_limit_bytes=8 * mebi),
            name="split_columns",
        )(jnp.stack([place, side, group]).astype(jnp.int32), tokens)
    cut = tokens.reshape(count, ep_count, 2, 2, quarter)
    parts = [], []
    for step in range(ep_count // 2):
        for core in (group, 1 - group):
            for offset in (2 * step, 2 * step + 1):
                for half, part in zip((side, 1 - side), parts):
                    start = (0, place ^ offset, half, core, 0)
                    part.append(lax.dynamic_slice(cut, start, (count, 1, 1, 1, quarter)))
    kept, given = [jnp.stack(part, axis=1).reshape(count, -1) for part in parts]
    return kept, given


def down_kernel(steps, last, *refs):
    (kept, given), blocks = refs[:2], refs[2 : 2 + 4 * len(steps)]
    so_far, results = (refs[-3], refs[-2:]) if last else (None, refs[-1:])
    depth = 2 * blocks[0].shape[0]
    width = 256
    for start in range(0, blocks[0].shape[1], width):
        columns = slice(start, start + width)
        total = 0.0 if so_far is None else so_far[:, columns]
        for i, step in enumerate(steps):
            for core in range(2):
                inner = pl.ds((2 * step + core) * depth, depth)
                rows = jnp.concatenate([kept[:, inner], given[:, inner]], axis=0)
                near, far = blocks[4 * i + 2 * core], blocks[4 * i + 2 * core + 1]
                block = jnp.concatenate([near[:, columns], far[:, columns]], axis=0)
                total += jnp.dot(rows, block, preferred_element_type=jnp.float32)
        if last:
            count = kept.shape[0]
            results[0][:, columns] = total[:count]
            results[1][:, columns] = total[count:].astype(jnp.bfloat16)
        else:
            results[0][:, columns] = total


def down_project(steps, kept, given, blocks, so_far=None):
    count, inner = kept.shape
    latent_width = blocks[0].shape[1]
    operands = (kept, given, *blocks) + (() if so_far is None else (so_far,))
    if so_far is None:
        shapes = (jax.ShapeDtypeStruct((2 * count, latent_width), jnp.float32),)
    else:
        shapes = (
            jax.ShapeDtypeStruct((count, latent_width), jnp.float32),
            jax.ShapeDtypeStruct((count, latent_width), jnp.bfloat16),
        )
    return pl.pallas_call(
        functools.partial(down_kernel, steps, so_far is not None),
        out_shape=shapes,
        in_specs=[in_vmem] * len(operands),
        out_specs=(in_vmem,) * len(shapes),
        compiler_params=pltpu.CompilerParams(vmem_limit_bytes=16 * mebi),
        cost_estimate=pl.CostEstimate(
            flops=16 * len(steps) * count * blocks[0].shape[0] * latent_width,
            bytes_accessed=2 * len(blocks) * blocks[0].shape[0] * latent_width,
            transcendentals=0,
        ),
        name="down_project",
    )(*operands)


def latent_kernel(own_part, arrived, weights, piece):
    count = own_part.shape[0]
    total = own_part[...] + arrived[...].astype(jnp.float32)
    piece[:count] = total.astype(jnp.bfloat16)
    extra = piece.shape[0] - count
    piece[count:] = jnp.zeros((extra, piece.shape[1]), jnp.bfloat16)
    piece[count:, :count] = weights[...]


def finish_latent(own_part, arrived, weights):
    count, latent_width = own_part.shape
    return pl.pallas_call(
        latent_kernel,
        out_shape=jax.ShapeDtypeStruct((count + weights.shape[0], latent_width), jnp.bfloat16),
        in_specs=[in_vmem] * 3,
        out_specs=in_vmem,
        compiler_params=pltpu.CompilerParams(vmem_limit_bytes=4 * mebi),
        name="finish_latent",
    )(own_part, arrived, weights)


def expert_kernel(positions, count, where, *refs):
    pieces = refs[: 2 * positions]
    gate, up, out = refs[2 * positions : 2 * positions + 3]
    own_sums, refs = refs[2 * positions + 3 : 3 * positions + 3], refs[3 * positions + 3 :]
    other_sums, rows, hidden, held, gate_block, up_block, out_block, sems = refs
    width = 256
    blocks = gate.shape[2] // width

    def columns_at(start):
        return pl.ds(pl.multiple_of(start, width), width)

    def read(i, part):
        source, target = ((gate, gate_block), (up, up_block), (out, out_block))[part]
        columns = columns_at(i * width)
        return pltpu.make_async_copy(
            source.at[0, :, columns], target.at[:, columns], sems.at[part * blocks + i]
        )

    for i in range(blocks):
        read(i, 0).start()
        read(i, 1).start()
    for i in range(out.shape[2] // width):
        read(i, 2).start()
    for i, piece in enumerate(pieces):
        rows[i * count : (i + 1) * count] = piece[:count]

    def scale_of(piece):
        weights = piece[count:, :count].astype(jnp.float32)
        expert = lax.broadcasted_iota(jnp.int32, weights.shape, 0)
        line = jnp.sum(jnp.where(expert == where[0], weights, 0.0), axis=0, keepdims=True)
        row = lax.broadcasted_iota(jnp.int32, (count, count), 0)
        column = lax.broadcasted_iota(jnp.int32, (count, count), 1)
        return jnp.sum(jnp.where(row == column, line, 0.0), axis=1, keepdims=True)

    scales = [scale_of(piece) for piece in pieces]

    def arrive(i):
        read(i, 0).wait()
        read(i, 1).wait()

    def products(i):
        columns = columns_at(i * width)
        return [
            jnp.dot(rows[...], block[:, columns], preferred_element_type=jnp.float32)
            for block in (gate_block, up_block)
        ]

    def activate(gate_value, up_value, i):
        value = gate_value / (1.0 + jnp.exp(-gate_value)) * up_value
        hidden[:, columns_at(i * width)] = value.astype(jnp.bfloat16)

    arrive(0)
    held[0], held[1] = products(0)

    def step(i, carry):
        arrive(2 * i + 1)
        arrive(2 * i + 2)
        first = products(2 * i + 1)
        activate(held[0], held[1], 2 * i)
        second = products(2 * i + 2)
        activate(*first, 2 * i + 1)
        held[0], held[1] = second
        return carry

    lax.fori_loop(0, blocks // 2 - 1, step, 0)
    arrive(blocks - 1)
    last = products(blocks - 1)
    activate(held[0], held[1], blocks - 2)
    activate(*last, blocks - 1)

    def finish(i, carry):
        columns = columns_at(i * width)
        read(i, 2).wait()
        value = jnp.dot(hidden[...], out_block[:, columns], preferred_element_type=jnp.float32)
        for j, scale in enumerate(scales):
            scaled = (value[j * count : (j + 1) * count] * scale).astype(jnp.bfloat16)
            if j < positions:
                own_sums[j][:, columns] = scaled
            else:
                other_sums[(j - positions) * count : (j - positions + 1) * count, columns] = scaled
        return carry

    lax.fori_loop(0, out.shape[2] // width, finish, 0)


def expert_apply(expert, owns, others, weights, count):
    positions = len(owns)
    latent_width = owns[0].shape[1]
    hidden_width = weights[0].shape[2]
    rows, width = 2 * positions * count, 256
    own_sum = jax.ShapeDtypeStruct((count, latent_width), jnp.bfloat16)
    other_sums = jax.ShapeDtypeStruct((positions * count, latent_width), jnp.bfloat16)
    return pl.pallas_call(
        functools.partial(expert_kernel, positions, count),
        out_shape=(own_sum,) * positions + (other_sums,),
        in_specs=[in_smem] + [in_vmem] * (2 * positions) + [in_hbm] * 3,
        out_specs=(in_vmem,) * (positions + 1),
        scratch_shapes=[
            pltpu.VMEM((rows, latent_width), jnp.bfloat16),
            pltpu.VMEM((rows, hidden_width), jnp.bfloat16),
            pltpu.VMEM((2, rows, width), jnp.float32),
        ]
        + [pltpu.VMEM(w.shape[1:], w.dtype) for w in weights]
        + [pltpu.SemaphoreType.DMA(((2 * hidden_width + latent_width) // width,))],
        compiler_params=pltpu.CompilerParams(vmem_limit_bytes=28 * mebi),
        cost_estimate=pl.CostEstimate(
            flops=3 * rows * latent_width * hidden_width // 2,
            bytes_accessed=4 * rows * latent_width,
            transcendentals=0,
        ),
        name="expert",
    )(expert, *owns, *others, *weights)


def project_kernel(where, *refs):
    terms, refs = refs[:-8], refs[-8:]
    mine, swapped, layer_out, combined, held, blocks, read_sems, sems = refs
    sides, ep_count, inner, width = mine.shape

    def read(e, side):
        return pltpu.make_async_copy(
            mine.at[side, e], held.at[side, e], read_sems.at[sides * e + side]
        )

    for e in range(ep_count):
        for side in range(sides):
            read(e, side).start()
    total = terms[0][...].astype(jnp.float32)
    for term in terms[1:]:
        total += term[...].astype(jnp.float32)
    combined[...] = total.astype(jnp.bfloat16)

    def sent(e):
        columns = pl.ds(e * width, width)
        return pltpu.make_async_copy(blocks.at[:, columns], layer_out.at[:, columns], sems.at[e])

    for e in range(ep_count):
        value = 0.0
        for side in range(sides):
            read(e, side).wait()
            for core, array in ((1 - where[0], swapped), (where[0], held)):
                columns = pl.ds(pl.multiple_of((2 * side + core) * inner, inner), inner)
                value += jnp.dot(
                    combined[:, columns], array[side, e], preferred_element_type=jnp.float32
                )
        blocks[:, e * width : (e + 1) * width] = value.astype(jnp.bfloat16)
        sent(e).start()
    for e in range(ep_count):
        sent(e).wait()


def project(group, terms, mine, swapped):
    count, latent_width = terms[0].shape
    sides, ep_count, inner, width = mine.shape
    return pl.pallas_call(
        project_kernel,
        in_specs=[in_smem] + [in_vmem] * len(terms) + [in_hbm, in_vmem],
        out_specs=anywhere,
        out_shape=jax.ShapeDtypeStruct((count, ep_count * width), jnp.bfloat16),
        scratch_shapes=[
            pltpu.VMEM((count, latent_width), jnp.bfloat16),
            pltpu.VMEM(mine.shape, mine.dtype),
            pltpu.VMEM((count, ep_count * width), jnp.bfloat16),
            pltpu.SemaphoreType.DMA((sides * ep_count,)),
            pltpu.SemaphoreType.DMA((ep_count,)),
        ],
        compiler_params=pltpu.CompilerParams(vmem_limit_bytes=16 * mebi),
        cost_estimate=pl.CostEstimate(
            flops=2 * count * latent_width * ep_count * width,
            bytes_accessed=2 * latent_width * ep_count * width,
            transcendentals=0,
        ),
        name="project",
    )(group.reshape(1).astype(jnp.int32), *terms, mine, swapped)


def body(
    tokens, expert_ids, route_scores, down_latent, gate_weight, up_weight, out_weight, up_latent
):
    group_count = lax.axis_size("grp")
    ep_count = lax.axis_size("ep")
    expert_count = group_count * ep_count * gate_weight.shape[0]
    rep, group, place = lax.axis_index("rep"), lax.axis_index("grp"), lax.axis_index("ep")
    side = rep % 2
    own_quarter = 2 * side + group
    token_count = tokens.shape[0]
    latent_width = down_latent.shape[1]
    steps = ep_count // 2
    last = steps - 1

    quarter = down_latent.shape[0] // 4

    def own_piece(core):
        return lax.dynamic_slice_in_dim(down_latent, (2 * side + core) * quarter, quarter, 0)

    kept, given = split_columns(tokens, ep_count, quarter, place, side, group)
    taken = swap_reps(given)
    near = first_steps(own_piece(group), steps)
    far = {0: swap_ep(near[0], 1)}
    near[1], kept = join(near[1], kept)
    far[1] = swap_ep(near[1], 1)
    weights = dense_weights(after(expert_ids, near[1]), route_scores, expert_count)
    others = {k: near[k] for k in near if k > 1}
    far[0], far[1], taken, weights, *arrived = join(
        far[0], far[1], taken, weights, *others.values()
    )
    near.update(zip(others, arrived))

    inner = latent_width // 4
    up_piece = lax.dynamic_slice_in_dim(up_latent, own_quarter * inner, inner, 0)
    mine = lax.all_gather(after(up_piece, weights), "ep", axis=0)

    for k in range(2, steps):
        if k & (k - 1):
            low = k & -k
            near[k] = swap_ep(near[k ^ low], 2 * low)
        far[k] = swap_ep(near[k], 1)
    blocks = []
    for k in range(steps):
        other = own_piece(1 - group) if k == 0 else swap_cores(near[k])
        blocks.append((near[k], far[k], other, swap_cores(far[k])))
    early = list(range(last))
    (partial,) = down_project(early, kept, taken, [b for k in early for b in blocks[k]])
    late = [after(blocks[-1][0], partial), *blocks[-1][1:]]
    own_part, sent_part = down_project([last], kept, taken, late, partial)
    latent = finish_latent(own_part, swap_reps(sent_part), weights.astype(jnp.bfloat16))

    expert = (group * ep_count + place).astype(jnp.int32).reshape(1)
    expert_weights = [
        pltpu.with_memory_space_constraint(w, pltpu.HBM)
        for w in (gate_weight, up_weight, out_weight)
    ]
    near = first_steps(latent, steps)
    far = {0: swap_ep(latent, 1)}
    sums, travel, taken_in = {}, {"up": mine}, set()

    def start_near(k):
        near[k] = swap_ep(near[k ^ (k & -k)], 2 * (k & -k))
        return near, k

    def start_far(k):
        far[k] = swap_ep(near[k], 1)
        return far, k

    def send(name, value, mask):
        travel[name] = swap_ep(value.astype(jnp.bfloat16), mask)
        return travel, name

    def run(which, *coming):
        owns = [(near, far)[y][k] for k, y in which]
        operands = join(*owns, *[swap_cores(own) for own in owns])
        count = len(which)
        out = expert_apply(expert, operands[:count], operands[count:], expert_weights, token_count)
        out = join(*out, *[table[key] for table, key in coming])
        for (table, key), value in zip(coming, out[count + 1 :]):
            table[key] = value
        from_core = swap_cores(out[count])
        for i, place_of in enumerate(which):
            swapped = from_core[i * token_count : (i + 1) * token_count]
            sums[place_of] = out[i].astype(jnp.float32) + swapped.astype(jnp.float32)

    run([(0, 0)], (near, 1), (far, 0))
    run([(1, 0), (0, 1)], *[(near, k) for k in near if k > 1], start_far(1), (travel, "up"))
    sides = [[i, i + 1] for i in range(0, lax.axis_size("rep"), 2)]
    both_sides = lax.all_gather(travel.pop("up"), "rep", axis=0, axis_index_groups=sides)
    for k in range(2, steps):
        coming = [start_far(k)]
        for j in range(3, steps):
            if j not in near and j ^ (j & -j) == k:
                coming.append(start_near(j))
        previous = [(k - 2, 1)] if k == last else [(k - 2, 1), (k - 1, 0)]
        coming += [send(p, sums[p], 2 * p[0] + p[1]) for p in previous]
        run([(k, 0), (k - 1, 1)], *coming)
    run(
        [(last, 1)],
        send((last - 1, 1), sums[last - 1, 1], 1),
        send((last, 0), sums[last, 0], 2),
    )
    send((last, 1), sums[last, 1], 3)
    shared = sums[last - 1, 0]
    for name in ((last - 1, 1), (last, 0), (last, 1)):
        shared += travel.pop(name).astype(jnp.float32)
    shared = shared.astype(jnp.bfloat16)
    both_sides = after(both_sides, shared)
    send("shared", shared, 2 * last - 2)
    *terms, swapped_sides = join(sums[0, 0], *travel.values(), swap_cores(both_sides))
    both_sides = pltpu.with_memory_space_constraint(both_sides, pltpu.HBM)
    return project(group, terms, both_sides, swapped_sides)


def solution(mesh):
    in_specs = (
        P(("rep", "grp", "ep"), None),
        P(("rep", "grp", "ep"), None),
        P(("rep", "grp", "ep"), None),
        P("ep", None),
        P(("grp", "ep"), None, None),
        P(("grp", "ep"), None, None),
        P(("grp", "ep"), None, None),
        P(None, "ep"),
    )
    out_specs = P(("rep", "grp", "ep"), None)
    return jax.shard_map(body, mesh=mesh, in_specs=in_specs, out_specs=out_specs, check_vma=False)
```

```python
import functools

import jax
import jax.numpy as jnp
from jax import lax
from jax.experimental import pallas as pl
from jax.experimental.pallas import tpu as pltpu
from jax.sharding import PartitionSpec as P

route_scale = 2.5
mebi = 1024 * 1024
in_vmem = pl.BlockSpec(memory_space=pltpu.VMEM)
in_smem = pl.BlockSpec(memory_space=pltpu.SMEM)
in_hbm = pl.BlockSpec(memory_space=pltpu.HBM)
anywhere = pl.BlockSpec(memory_space=pl.ANY)


def after(value, *others):
    return lax.optimization_barrier((value, *others))[0]


def join(*values):
    return lax.optimization_barrier(values)


def swap_cores(array):
    return lax.ppermute(array, "grp", [(0, 1), (1, 0)])


def swap_reps(array):
    return lax.ppermute(array, "rep", [(i, i ^ 1) for i in range(lax.axis_size("rep"))])


def swap_ep(array, mask):
    return lax.ppermute(array, "ep", [(i, i ^ mask) for i in range(lax.axis_size("ep"))])


def swap_both(array):
    names, sizes = ("rep", "ep"), (lax.axis_size("rep"), lax.axis_size("ep"))
    pairs = [(i, i ^ (sizes[1] + 1)) for i in range(sizes[0] * sizes[1])]
    return lax.ppermute(array, names, pairs)


def first_steps(piece, steps):
    return {0: piece} | {k: swap_ep(piece, 2 * k) for k in range(1, steps) if k & (k - 1) == 0}


def dense_weights(expert_ids, route_scores, expert_count):
    sigmoids = jax.nn.sigmoid(route_scores)
    weights = (route_scale * sigmoids / jnp.sum(sigmoids, axis=1, keepdims=True)).astype(
        jnp.bfloat16
    )
    named = expert_ids[None, :, :] == jnp.arange(expert_count, dtype=jnp.int32)[:, None, None]
    return jnp.sum(jnp.where(named, weights.astype(jnp.float32)[None, :, :], 0.0), axis=2)


def columns_kernel(steps, quarter, where, tokens, *parts):
    place, side, group = where[0], where[1], where[2]
    for k in range(steps):
        for core in range(2):
            to = pl.ds((2 * k + core) * quarter, quarter)
            for i, part in enumerate(parts):
                shard = (place ^ (2 * k + i % 2)) * 4 + 2 * (side ^ (i // 2)) + (group ^ core)
                start = pl.multiple_of(shard * quarter, quarter)
                part[:, to] = tokens[:, pl.ds(start, quarter)]


def split_columns(tokens, ep_count, quarter, place, side, group):
    count = tokens.shape[0]
    steps = ep_count // 2
    if quarter % 128 == 0:
        part = jax.ShapeDtypeStruct((count, 2 * steps * quarter), tokens.dtype)
        return pl.pallas_call(
            functools.partial(columns_kernel, steps, quarter),
            out_shape=(part,) * 4,
            in_specs=[in_smem, in_vmem],
            out_specs=(in_vmem,) * 4,
            compiler_params=pltpu.CompilerParams(vmem_limit_bytes=8 * mebi),
            name="split_columns",
        )(jnp.stack([place, side, group]).astype(jnp.int32), tokens)
    cut = tokens.reshape(count, ep_count, 2, 2, quarter)
    parts = []
    for i in range(4):
        columns = []
        for k in range(steps):
            for core in (group, 1 - group):
                start = (0, place ^ (2 * k + i % 2), side ^ (i // 2), core, 0)
                columns.append(lax.dynamic_slice(cut, start, (count, 1, 1, 1, quarter)))
        parts.append(jnp.stack(columns, axis=1).reshape(count, -1))
    return parts


def down_kernel(steps, last, *refs):
    parts, blocks = refs[:4], refs[4 : 4 + 2 * len(steps)]
    so_far, results = (refs[-5], refs[-4:]) if last else (None, refs[-1:])
    depth = 2 * blocks[0].shape[0]
    width = 256
    for start in range(0, blocks[0].shape[1], width):
        columns = slice(start, start + width)
        total = 0.0 if so_far is None else so_far[:, columns]
        for i, step in enumerate(steps):
            inner = pl.ds(step * depth, depth)
            rows = jnp.concatenate([part[:, inner] for part in parts], axis=0)
            block = [core[:, columns] for core in blocks[2 * i : 2 * i + 2]]
            block = jnp.concatenate(block, axis=0)
            total += jnp.dot(rows, block, preferred_element_type=jnp.float32)
        if last:
            count = parts[0].shape[0]
            for i, result in enumerate(results):
                rows = total[i * count : (i + 1) * count]
                result[:, columns] = rows.astype(result.dtype)
        else:
            results[0][:, columns] = total


def down_project(steps, parts, blocks, so_far=None):
    count = parts[0].shape[0]
    latent_width = blocks[0].shape[1]
    operands = (*parts, *blocks) + (() if so_far is None else (so_far,))
    if so_far is None:
        shapes = (jax.ShapeDtypeStruct((4 * count, latent_width), jnp.float32),)
    else:
        types = (jnp.float32, jnp.bfloat16, jnp.bfloat16, jnp.bfloat16)
        shapes = tuple(jax.ShapeDtypeStruct((count, latent_width), t) for t in types)
    return pl.pallas_call(
        functools.partial(down_kernel, steps, so_far is not None),
        out_shape=shapes,
        in_specs=[in_vmem] * len(operands),
        out_specs=(in_vmem,) * len(shapes),
        compiler_params=pltpu.CompilerParams(vmem_limit_bytes=16 * mebi),
        cost_estimate=pl.CostEstimate(
            flops=16 * len(steps) * count * blocks[0].shape[0] * latent_width,
            bytes_accessed=2 * len(blocks) * blocks[0].shape[0] * latent_width,
            transcendentals=0,
        ),
        name="down_project",
    )(*operands)


def latent_kernel(own_part, *refs):
    arrived, (weights, piece) = refs[:-2], refs[-2:]
    count = own_part.shape[0]
    total = own_part[...]
    for part in arrived:
        total += part[...].astype(jnp.float32)
    piece[:count] = total.astype(jnp.bfloat16)
    extra = piece.shape[0] - count
    piece[count:] = jnp.zeros((extra, piece.shape[1]), jnp.bfloat16)
    piece[count:, :count] = weights[...]


def finish_latent(own_part, weights, *arrived):
    count, latent_width = own_part.shape
    return pl.pallas_call(
        latent_kernel,
        out_shape=jax.ShapeDtypeStruct((count + weights.shape[0], latent_width), jnp.bfloat16),
        in_specs=[in_vmem] * (2 + len(arrived)),
        out_specs=in_vmem,
        compiler_params=pltpu.CompilerParams(vmem_limit_bytes=4 * mebi),
        name="finish_latent",
    )(own_part, *arrived, weights)


def expert_kernel(positions, count, where, *refs):
    pieces = refs[: 2 * positions]
    gate, up, out = refs[2 * positions : 2 * positions + 3]
    own_sums, refs = refs[2 * positions + 3 : 3 * positions + 3], refs[3 * positions + 3 :]
    other_sums, rows, hidden, held, gate_block, up_block, out_block, sems = refs
    width = 256
    blocks = gate.shape[2] // width

    def columns_at(start):
        return pl.ds(pl.multiple_of(start, width), width)

    def read(i, part):
        source, target = ((gate, gate_block), (up, up_block), (out, out_block))[part]
        columns = columns_at(i * width)
        return pltpu.make_async_copy(
            source.at[0, :, columns], target.at[:, columns], sems.at[part * blocks + i]
        )

    for i in range(blocks):
        read(i, 0).start()
        read(i, 1).start()
    for i in range(out.shape[2] // width):
        read(i, 2).start()
    for i, piece in enumerate(pieces):
        rows[i * count : (i + 1) * count] = piece[:count]

    def scale_of(piece):
        weights = piece[count:, :count].astype(jnp.float32)
        expert = lax.broadcasted_iota(jnp.int32, weights.shape, 0)
        line = jnp.sum(jnp.where(expert == where[0], weights, 0.0), axis=0, keepdims=True)
        row = lax.broadcasted_iota(jnp.int32, (count, count), 0)
        column = lax.broadcasted_iota(jnp.int32, (count, count), 1)
        return jnp.sum(jnp.where(row == column, line, 0.0), axis=1, keepdims=True)

    scales = [scale_of(piece) for piece in pieces]

    def arrive(i):
        read(i, 0).wait()
        read(i, 1).wait()

    def products(i):
        columns = columns_at(i * width)
        return [
            jnp.dot(rows[...], block[:, columns], preferred_element_type=jnp.float32)
            for block in (gate_block, up_block)
        ]

    def activate(gate_value, up_value, i):
        value = gate_value / (1.0 + jnp.exp(-gate_value)) * up_value
        hidden[:, columns_at(i * width)] = value.astype(jnp.bfloat16)

    arrive(0)
    held[0], held[1] = products(0)

    def step(i, carry):
        arrive(2 * i + 1)
        arrive(2 * i + 2)
        first = products(2 * i + 1)
        activate(held[0], held[1], 2 * i)
        second = products(2 * i + 2)
        activate(*first, 2 * i + 1)
        held[0], held[1] = second
        return carry

    lax.fori_loop(0, blocks // 2 - 1, step, 0)
    arrive(blocks - 1)
    last = products(blocks - 1)
    activate(held[0], held[1], blocks - 2)
    activate(*last, blocks - 1)

    def finish(i, carry):
        columns = columns_at(i * width)
        read(i, 2).wait()
        value = jnp.dot(hidden[...], out_block[:, columns], preferred_element_type=jnp.float32)
        for j, scale in enumerate(scales):
            scaled = (value[j * count : (j + 1) * count] * scale).astype(jnp.bfloat16)
            if j < positions:
                own_sums[j][:, columns] = scaled
            else:
                other_sums[(j - positions) * count : (j - positions + 1) * count, columns] = scaled
        return carry

    lax.fori_loop(0, out.shape[2] // width, finish, 0)


def expert_apply(expert, owns, others, weights, count):
    positions = len(owns)
    latent_width = owns[0].shape[1]
    hidden_width = weights[0].shape[2]
    rows, width = 2 * positions * count, 256
    own_sum = jax.ShapeDtypeStruct((count, latent_width), jnp.bfloat16)
    other_sums = jax.ShapeDtypeStruct((positions * count, latent_width), jnp.bfloat16)
    return pl.pallas_call(
        functools.partial(expert_kernel, positions, count),
        out_shape=(own_sum,) * positions + (other_sums,),
        in_specs=[in_smem] + [in_vmem] * (2 * positions) + [in_hbm] * 3,
        out_specs=(in_vmem,) * (positions + 1),
        scratch_shapes=[
            pltpu.VMEM((rows, latent_width), jnp.bfloat16),
            pltpu.VMEM((rows, hidden_width), jnp.bfloat16),
            pltpu.VMEM((2, rows, width), jnp.float32),
        ]
        + [pltpu.VMEM(w.shape[1:], w.dtype) for w in weights]
        + [pltpu.SemaphoreType.DMA(((2 * hidden_width + latent_width) // width,))],
        compiler_params=pltpu.CompilerParams(vmem_limit_bytes=28 * mebi),
        cost_estimate=pl.CostEstimate(
            flops=3 * rows * latent_width * hidden_width // 2,
            bytes_accessed=4 * rows * latent_width,
            transcendentals=0,
        ),
        name="expert",
    )(expert, *owns, *others, *weights)


def project_kernel(where, *refs):
    terms, refs = refs[:-8], refs[-8:]
    mine, swapped, layer_out, combined, held, blocks, read_sems, sems = refs
    sides, ep_count, inner, width = mine.shape

    def read(e, side):
        return pltpu.make_async_copy(
            mine.at[side, e], held.at[side, e], read_sems.at[sides * e + side]
        )

    for e in range(ep_count):
        for side in range(sides):
            read(e, side).start()
    total = terms[0][...].astype(jnp.float32)
    for term in terms[1:]:
        total += term[...].astype(jnp.float32)
    combined[...] = total.astype(jnp.bfloat16)

    def sent(e):
        columns = pl.ds(e * width, width)
        return pltpu.make_async_copy(blocks.at[:, columns], layer_out.at[:, columns], sems.at[e])

    for e in range(ep_count):
        value = 0.0
        for side in range(sides):
            read(e, side).wait()
            for core, array in ((1 - where[0], swapped), (where[0], held)):
                columns = pl.ds(pl.multiple_of((2 * side + core) * inner, inner), inner)
                value += jnp.dot(
                    combined[:, columns], array[side, e], preferred_element_type=jnp.float32
                )
        blocks[:, e * width : (e + 1) * width] = value.astype(jnp.bfloat16)
        sent(e).start()
    for e in range(ep_count):
        sent(e).wait()


def project(group, terms, mine, swapped):
    count, latent_width = terms[0].shape
    sides, ep_count, inner, width = mine.shape
    return pl.pallas_call(
        project_kernel,
        in_specs=[in_smem] + [in_vmem] * len(terms) + [in_hbm, in_vmem],
        out_specs=anywhere,
        out_shape=jax.ShapeDtypeStruct((count, ep_count * width), jnp.bfloat16),
        scratch_shapes=[
            pltpu.VMEM((count, latent_width), jnp.bfloat16),
            pltpu.VMEM(mine.shape, mine.dtype),
            pltpu.VMEM((count, ep_count * width), jnp.bfloat16),
            pltpu.SemaphoreType.DMA((sides * ep_count,)),
            pltpu.SemaphoreType.DMA((ep_count,)),
        ],
        compiler_params=pltpu.CompilerParams(vmem_limit_bytes=16 * mebi),
        cost_estimate=pl.CostEstimate(
            flops=2 * count * latent_width * ep_count * width,
            bytes_accessed=2 * latent_width * ep_count * width,
            transcendentals=0,
        ),
        name="project",
    )(group.reshape(1).astype(jnp.int32), *terms, mine, swapped)


def body(
    tokens, expert_ids, route_scores, down_latent, gate_weight, up_weight, out_weight, up_latent
):
    group_count = lax.axis_size("grp")
    ep_count = lax.axis_size("ep")
    expert_count = group_count * ep_count * gate_weight.shape[0]
    rep, group, place = lax.axis_index("rep"), lax.axis_index("grp"), lax.axis_index("ep")
    side = rep % 2
    own_quarter = 2 * side + group
    token_count = tokens.shape[0]
    latent_width = down_latent.shape[1]
    steps = ep_count // 2
    last = steps - 1

    quarter = down_latent.shape[0] // 4

    def own_piece(core):
        return lax.dynamic_slice_in_dim(down_latent, (2 * side + core) * quarter, quarter, 0)

    near = first_steps(own_piece(group), steps)

    inner = latent_width // 4
    up_piece = lax.dynamic_slice_in_dim(up_latent, own_quarter * inner, inner, 0)
    mine = lax.all_gather(after(up_piece, near[0]), "ep", axis=0)

    parts = split_columns(tokens, ep_count, quarter, place, side, group)
    parts = [parts[0], swap_ep(parts[1], 1), swap_reps(parts[2]), swap_both(parts[3])]
    weights = dense_weights(after(expert_ids, parts[0]), route_scores, expert_count)
    others = {k: near[k] for k in near if k}
    weights, *arrived = join(weights, *parts[1:], *others.values())
    parts[1:] = arrived[:3]
    near.update(zip(others, arrived[3:]))
    for k in range(3, steps):
        if k not in near:
            near[k] = swap_ep(near[k ^ (k & -k)], 2 * (k & -k))
    blocks = []
    for k in range(steps):
        blocks += [near[k], swap_cores(near[k]) if k else own_piece(1 - group)]
    (partial,) = down_project(list(range(last)), parts, blocks[:-2])
    late = [after(blocks[-2], partial), blocks[-1]]
    own_part, *sent_parts = down_project([last], parts, late, partial)
    arrived = [swap(part) for swap, part in zip((lambda a: swap_ep(a, 1), swap_reps, swap_both), sent_parts)]
    latent = finish_latent(own_part, weights.astype(jnp.bfloat16), *arrived)

    expert = (group * ep_count + place).astype(jnp.int32).reshape(1)
    expert_weights = [
        pltpu.with_memory_space_constraint(w, pltpu.HBM)
        for w in (gate_weight, up_weight, out_weight)
    ]
    near = first_steps(latent, steps)
    far = {0: swap_ep(latent, 1)}
    sums, travel, taken_in = {}, {"up": mine}, set()

    def start_near(k):
        near[k] = swap_ep(near[k ^ (k & -k)], 2 * (k & -k))
        return near, k

    def start_far(k):
        far[k] = swap_ep(near[k], 1)
        return far, k

    def send(name, value, mask):
        travel[name] = swap_ep(value.astype(jnp.bfloat16), mask)
        return travel, name

    def run(which, *coming):
        owns = [(near, far)[y][k] for k, y in which]
        operands = join(*owns, *[swap_cores(own) for own in owns])
        count = len(which)
        out = expert_apply(expert, operands[:count], operands[count:], expert_weights, token_count)
        out = join(*out, *[table[key] for table, key in coming])
        for (table, key), value in zip(coming, out[count + 1 :]):
            table[key] = value
        from_core = swap_cores(out[count])
        for i, place_of in enumerate(which):
            swapped = from_core[i * token_count : (i + 1) * token_count]
            sums[place_of] = out[i].astype(jnp.float32) + swapped.astype(jnp.float32)

    run([(0, 0)], (near, 1), (far, 0))
    run([(1, 0), (0, 1)], *[(near, k) for k in near if k > 1], start_far(1), (travel, "up"))
    sides = [[i, i + 1] for i in range(0, lax.axis_size("rep"), 2)]
    both_sides = lax.all_gather(travel.pop("up"), "rep", axis=0, axis_index_groups=sides)
    for k in range(2, steps):
        coming = [start_far(k)]
        for j in range(3, steps):
            if j not in near and j ^ (j & -j) == k:
                coming.append(start_near(j))
        previous = [(k - 2, 1)] if k == last else [(k - 2, 1), (k - 1, 0)]
        coming += [send(p, sums[p], 2 * p[0] + p[1]) for p in previous]
        run([(k, 0), (k - 1, 1)], *coming)
    run(
        [(last, 1)],
        send((last - 1, 1), sums[last - 1, 1], 1),
        send((last, 0), sums[last, 0], 2),
    )
    send((last, 1), sums[last, 1], 3)
    shared = sums[last - 1, 0]
    for name in ((last - 1, 1), (last, 0), (last, 1)):
        shared += travel.pop(name).astype(jnp.float32)
    shared = shared.astype(jnp.bfloat16)
    both_sides = after(both_sides, shared)
    send("shared", shared, 2 * last - 2)
    *terms, swapped_sides = join(sums[0, 0], *travel.values(), swap_cores(both_sides))
    both_sides = pltpu.with_memory_space_constraint(both_sides, pltpu.HBM)
    return project(group, terms, both_sides, swapped_sides)


def solution(mesh):
    in_specs = (
        P(("rep", "grp", "ep"), None),
        P(("rep", "grp", "ep"), None),
        P(("rep", "grp", "ep"), None),
        P("ep", None),
        P(("grp", "ep"), None, None),
        P(("grp", "ep"), None, None),
        P(("grp", "ep"), None, None),
        P(None, "ep"),
    )
    out_specs = P(("rep", "grp", "ep"), None)
    return jax.shard_map(body, mesh=mesh, in_specs=in_specs, out_specs=out_specs, check_vma=False)
```

```python
import functools

import jax
import jax.numpy as jnp
from jax import lax
from jax.experimental import pallas as pl
from jax.experimental.pallas import tpu as pltpu
from jax.sharding import PartitionSpec as P

route_scale = 2.5
mebi = 1024 * 1024
in_vmem = pl.BlockSpec(memory_space=pltpu.VMEM)
in_smem = pl.BlockSpec(memory_space=pltpu.SMEM)
in_hbm = pl.BlockSpec(memory_space=pltpu.HBM)
anywhere = pl.BlockSpec(memory_space=pl.ANY)


def after(value, *others):
    return lax.optimization_barrier((value, *others))[0]


def join(*values):
    return lax.optimization_barrier(values)


def swap_cores(array):
    return lax.ppermute(array, "grp", [(0, 1), (1, 0)])


def swap_reps(array):
    return lax.ppermute(array, "rep", [(i, i ^ 1) for i in range(lax.axis_size("rep"))])


def swap_ep(array, mask):
    return lax.ppermute(array, "ep", [(i, i ^ mask) for i in range(lax.axis_size("ep"))])


def first_steps(piece, steps):
    return {0: piece} | {k: swap_ep(piece, 2 * k) for k in range(1, steps) if k & (k - 1) == 0}


def dense_weights(expert_ids, route_scores, expert_count):
    sigmoids = jax.nn.sigmoid(route_scores)
    weights = (route_scale * sigmoids / jnp.sum(sigmoids, axis=1, keepdims=True)).astype(
        jnp.bfloat16
    )
    named = expert_ids[None, :, :] == jnp.arange(expert_count, dtype=jnp.int32)[:, None, None]
    return jnp.sum(jnp.where(named, weights.astype(jnp.float32)[None, :, :], 0.0), axis=2)


def columns_kernel(ep_count, quarter, where, tokens, kept, given):
    place, side, group = where[0], where[1], where[2]
    for offset in range(ep_count):
        for core in range(2):
            to = pl.ds(((offset // 2 * 2 + core) * 2 + offset % 2) * quarter, quarter)
            shard = (place ^ offset) * 4 + (group ^ core)
            for half, part in ((side, kept), (1 - side, given)):
                start = pl.multiple_of((shard + 2 * half) * quarter, quarter)
                part[:, to] = tokens[:, pl.ds(start, quarter)]


def split_columns(tokens, ep_count, quarter, place, side, group):
    count = tokens.shape[0]
    if quarter % 128 == 0:
        half = jax.ShapeDtypeStruct((count, 2 * ep_count * quarter), tokens.dtype)
        return pl.pallas_call(
            functools.partial(columns_kernel, ep_count, quarter),
            out_shape=(half, half),
            in_specs=[in_smem, in_vmem],
            out_specs=(in_vmem, in_vmem),
            compiler_params=pltpu.CompilerParams(vmem_limit_bytes=8 * mebi),
            name="split_columns",
        )(jnp.stack([place, side, group]).astype(jnp.int32), tokens)
    cut = tokens.reshape(count, ep_count, 2, 2, quarter)
    parts = [], []
    for step in range(ep_count // 2):
        for core in (group, 1 - group):
            for offset in (2 * step, 2 * step + 1):
                for half, part in zip((side, 1 - side), parts):
                    start = (0, place ^ offset, half, core, 0)
                    part.append(lax.dynamic_slice(cut, start, (count, 1, 1, 1, quarter)))
    kept, given = [jnp.stack(part, axis=1).reshape(count, -1) for part in parts]
    return kept, given


def down_kernel(steps, last, *refs):
    (kept, given), blocks = refs[:2], refs[2 : 2 + 4 * len(steps)]
    so_far, results = (refs[-3], refs[-2:]) if last else (None, refs[-1:])
    depth = 2 * blocks[0].shape[0]
    width = 256
    for start in range(0, blocks[0].shape[1], width):
        columns = slice(start, start + width)
        total = 0.0 if so_far is None else so_far[:, columns]
        for i, step in enumerate(steps):
            for core in range(2):
                inner = pl.ds((2 * step + core) * depth, depth)
                rows = jnp.concatenate([kept[:, inner], given[:, inner]], axis=0)
                near, far = blocks[4 * i + 2 * core], blocks[4 * i + 2 * core + 1]
                block = jnp.concatenate([near[:, columns], far[:, columns]], axis=0)
                total += jnp.dot(rows, block, preferred_element_type=jnp.float32)
        if last:
            count = kept.shape[0]
            results[0][:, columns] = total[:count]
            results[1][:, columns] = total[count:].astype(jnp.bfloat16)
        else:
            results[0][:, columns] = total


def down_project(steps, kept, given, blocks, so_far=None):
    count, inner = kept.shape
    latent_width = blocks[0].shape[1]
    operands = (kept, given, *blocks) + (() if so_far is None else (so_far,))
    if so_far is None:
        shapes = (jax.ShapeDtypeStruct((2 * count, latent_width), jnp.float32),)
    else:
        shapes = (
            jax.ShapeDtypeStruct((count, latent_width), jnp.float32),
            jax.ShapeDtypeStruct((count, latent_width), jnp.bfloat16),
        )
    return pl.pallas_call(
        functools.partial(down_kernel, steps, so_far is not None),
        out_shape=shapes,
        in_specs=[in_vmem] * len(operands),
        out_specs=(in_vmem,) * len(shapes),
        compiler_params=pltpu.CompilerParams(vmem_limit_bytes=16 * mebi),
        cost_estimate=pl.CostEstimate(
            flops=16 * len(steps) * count * blocks[0].shape[0] * latent_width,
            bytes_accessed=2 * len(blocks) * blocks[0].shape[0] * latent_width,
            transcendentals=0,
        ),
        name="down_project",
    )(*operands)


def latent_kernel(own_part, arrived, weights, piece):
    count = own_part.shape[0]
    total = own_part[...] + arrived[...].astype(jnp.float32)
    piece[:count] = total.astype(jnp.bfloat16)
    extra = piece.shape[0] - count
    piece[count:] = jnp.zeros((extra, piece.shape[1]), jnp.bfloat16)
    piece[count:, :count] = weights[...]


def finish_latent(own_part, arrived, weights):
    count, latent_width = own_part.shape
    return pl.pallas_call(
        latent_kernel,
        out_shape=jax.ShapeDtypeStruct((count + weights.shape[0], latent_width), jnp.bfloat16),
        in_specs=[in_vmem] * 3,
        out_specs=in_vmem,
        compiler_params=pltpu.CompilerParams(vmem_limit_bytes=4 * mebi),
        name="finish_latent",
    )(own_part, arrived, weights)


def expert_kernel(positions, count, where, *refs):
    pieces = refs[: 2 * positions]
    gate, up, out = refs[2 * positions : 2 * positions + 3]
    own_sums, refs = refs[2 * positions + 3 : 3 * positions + 3], refs[3 * positions + 3 :]
    other_sums, rows, hidden, held, gate_block, up_block, out_block, sems = refs
    width = 256
    blocks = gate.shape[2] // width

    def columns_at(start):
        return pl.ds(pl.multiple_of(start, width), width)

    def read(i, part):
        source, target = ((gate, gate_block), (up, up_block), (out, out_block))[part]
        columns = columns_at(i * width)
        return pltpu.make_async_copy(
            source.at[0, :, columns], target.at[:, columns], sems.at[part * blocks + i]
        )

    for i in range(blocks):
        read(i, 0).start()
        read(i, 1).start()
    for i in range(out.shape[2] // width):
        read(i, 2).start()
    for i, piece in enumerate(pieces):
        rows[i * count : (i + 1) * count] = piece[:count]

    def scale_of(piece):
        weights = piece[count:, :count].astype(jnp.float32)
        expert = lax.broadcasted_iota(jnp.int32, weights.shape, 0)
        line = jnp.sum(jnp.where(expert == where[0], weights, 0.0), axis=0, keepdims=True)
        row = lax.broadcasted_iota(jnp.int32, (count, count), 0)
        column = lax.broadcasted_iota(jnp.int32, (count, count), 1)
        return jnp.sum(jnp.where(row == column, line, 0.0), axis=1, keepdims=True)

    scales = [scale_of(piece) for piece in pieces]

    def arrive(i):
        read(i, 0).wait()
        read(i, 1).wait()

    def products(i):
        columns = columns_at(i * width)
        return [
            jnp.dot(rows[...], block[:, columns], preferred_element_type=jnp.float32)
            for block in (gate_block, up_block)
        ]

    def activate(gate_value, up_value, i):
        value = gate_value / (1.0 + jnp.exp(-gate_value)) * up_value
        hidden[:, columns_at(i * width)] = value.astype(jnp.bfloat16)

    arrive(0)
    held[0], held[1] = products(0)

    def step(i, carry):
        arrive(2 * i + 1)
        arrive(2 * i + 2)
        first = products(2 * i + 1)
        activate(held[0], held[1], 2 * i)
        second = products(2 * i + 2)
        activate(*first, 2 * i + 1)
        held[0], held[1] = second
        return carry

    lax.fori_loop(0, blocks // 2 - 1, step, 0)
    arrive(blocks - 1)
    last = products(blocks - 1)
    activate(held[0], held[1], blocks - 2)
    activate(*last, blocks - 1)

    def finish(i, carry):
        columns = columns_at(i * width)
        read(i, 2).wait()
        value = jnp.dot(hidden[...], out_block[:, columns], preferred_element_type=jnp.float32)
        for j, scale in enumerate(scales):
            scaled = (value[j * count : (j + 1) * count] * scale).astype(jnp.bfloat16)
            if j < positions:
                own_sums[j][:, columns] = scaled
            else:
                other_sums[(j - positions) * count : (j - positions + 1) * count, columns] = scaled
        return carry

    lax.fori_loop(0, out.shape[2] // width, finish, 0)


def expert_apply(expert, owns, others, weights, count):
    positions = len(owns)
    latent_width = owns[0].shape[1]
    hidden_width = weights[0].shape[2]
    rows, width = 2 * positions * count, 256
    own_sum = jax.ShapeDtypeStruct((count, latent_width), jnp.bfloat16)
    other_sums = jax.ShapeDtypeStruct((positions * count, latent_width), jnp.bfloat16)
    return pl.pallas_call(
        functools.partial(expert_kernel, positions, count),
        out_shape=(own_sum,) * positions + (other_sums,),
        in_specs=[in_smem] + [in_vmem] * (2 * positions) + [in_hbm] * 3,
        out_specs=(in_vmem,) * (positions + 1),
        scratch_shapes=[
            pltpu.VMEM((rows, latent_width), jnp.bfloat16),
            pltpu.VMEM((rows, hidden_width), jnp.bfloat16),
            pltpu.VMEM((2, rows, width), jnp.float32),
        ]
        + [pltpu.VMEM(w.shape[1:], w.dtype) for w in weights]
        + [pltpu.SemaphoreType.DMA(((2 * hidden_width + latent_width) // width,))],
        compiler_params=pltpu.CompilerParams(vmem_limit_bytes=28 * mebi),
        cost_estimate=pl.CostEstimate(
            flops=3 * rows * latent_width * hidden_width // 2,
            bytes_accessed=4 * rows * latent_width,
            transcendentals=0,
        ),
        name="expert",
    )(expert, *owns, *others, *weights)


def project_kernel(where, *refs):
    terms, refs = refs[:-8], refs[-8:]
    mine, swapped, layer_out, combined, held, blocks, read_sems, sems = refs
    sides, ep_count, inner, width = mine.shape

    def read(e, side):
        return pltpu.make_async_copy(
            mine.at[side, e], held.at[side, e], read_sems.at[sides * e + side]
        )

    for e in range(ep_count):
        for side in range(sides):
            read(e, side).start()
    total = terms[0][...].astype(jnp.float32)
    for term in terms[1:]:
        total += term[...].astype(jnp.float32)
    combined[...] = total.astype(jnp.bfloat16)

    def sent(e):
        columns = pl.ds(e * width, width)
        return pltpu.make_async_copy(blocks.at[:, columns], layer_out.at[:, columns], sems.at[e])

    for e in range(ep_count):
        value = 0.0
        for side in range(sides):
            read(e, side).wait()
            for core, array in ((1 - where[0], swapped), (where[0], held)):
                columns = pl.ds(pl.multiple_of((2 * side + core) * inner, inner), inner)
                value += jnp.dot(
                    combined[:, columns], array[side, e], preferred_element_type=jnp.float32
                )
        blocks[:, e * width : (e + 1) * width] = value.astype(jnp.bfloat16)
        sent(e).start()
    for e in range(ep_count):
        sent(e).wait()


def project(group, terms, mine, swapped):
    count, latent_width = terms[0].shape
    sides, ep_count, inner, width = mine.shape
    return pl.pallas_call(
        project_kernel,
        in_specs=[in_smem] + [in_vmem] * len(terms) + [in_hbm, in_vmem],
        out_specs=anywhere,
        out_shape=jax.ShapeDtypeStruct((count, ep_count * width), jnp.bfloat16),
        scratch_shapes=[
            pltpu.VMEM((count, latent_width), jnp.bfloat16),
            pltpu.VMEM(mine.shape, mine.dtype),
            pltpu.VMEM((count, ep_count * width), jnp.bfloat16),
            pltpu.SemaphoreType.DMA((sides * ep_count,)),
            pltpu.SemaphoreType.DMA((ep_count,)),
        ],
        compiler_params=pltpu.CompilerParams(vmem_limit_bytes=16 * mebi),
        cost_estimate=pl.CostEstimate(
            flops=2 * count * latent_width * ep_count * width,
            bytes_accessed=2 * latent_width * ep_count * width,
            transcendentals=0,
        ),
        name="project",
    )(group.reshape(1).astype(jnp.int32), *terms, mine, swapped)


def body(
    tokens, expert_ids, route_scores, down_latent, gate_weight, up_weight, out_weight, up_latent
):
    group_count = lax.axis_size("grp")
    ep_count = lax.axis_size("ep")
    expert_count = group_count * ep_count * gate_weight.shape[0]
    rep, group, place = lax.axis_index("rep"), lax.axis_index("grp"), lax.axis_index("ep")
    side = rep % 2
    own_quarter = 2 * side + group
    token_count = tokens.shape[0]
    latent_width = down_latent.shape[1]
    steps = ep_count // 2
    last = steps - 1

    quarter = down_latent.shape[0] // 4

    def own_piece(core):
        return lax.dynamic_slice_in_dim(down_latent, (2 * side + core) * quarter, quarter, 0)

    kept, given = split_columns(tokens, ep_count, quarter, place, side, group)
    taken = swap_reps(given)
    near = first_steps(own_piece(group), steps)
    far = {0: swap_ep(near[0], 1)}
    near[1], kept = join(near[1], kept)
    far[1] = swap_ep(near[1], 1)

    inner = latent_width // 4
    up_piece = lax.dynamic_slice_in_dim(up_latent, own_quarter * inner, inner, 0)
    mine = lax.all_gather(up_piece, "ep", axis=0)
    weights = dense_weights(after(expert_ids, near[1]), route_scores, expert_count)
    others = {k: near[k] for k in near if k > 1}
    far[1], weights, *arrived = join(far[1], weights, *others.values())
    near.update(zip(others, arrived))
    for k in range(2, steps):
        if k & (k - 1):
            low = k & -k
            near[k] = swap_ep(near[k ^ low], 2 * low)
        if k == last:
            near[k], far[0], taken = join(near[k], far[0], taken)
        far[k] = swap_ep(near[k], 1)
    blocks = []
    for k in range(steps):
        other = own_piece(1 - group) if k == 0 else swap_cores(near[k])
        blocks.append((near[k], far[k], other, swap_cores(far[k])))
    early = list(range(last))
    (partial,) = down_project(early, kept, taken, [b for k in early for b in blocks[k]])
    late = [after(blocks[-1][0], partial), *blocks[-1][1:]]
    own_part, sent_part = down_project([last], kept, taken, late, partial)
    latent = finish_latent(own_part, swap_reps(sent_part), weights.astype(jnp.bfloat16))

    expert = (group * ep_count + place).astype(jnp.int32).reshape(1)
    expert_weights = [
        pltpu.with_memory_space_constraint(w, pltpu.HBM)
        for w in (gate_weight, up_weight, out_weight)
    ]
    near = first_steps(latent, steps)
    far = {0: swap_ep(latent, 1)}
    sums, travel, taken_in = {}, {"up": mine}, set()

    def start_near(k):
        near[k] = swap_ep(near[k ^ (k & -k)], 2 * (k & -k))
        return near, k

    def start_far(k):
        far[k] = swap_ep(near[k], 1)
        return far, k

    def send(name, value, mask):
        travel[name] = swap_ep(value.astype(jnp.bfloat16), mask)
        return travel, name

    def run(which, *coming):
        owns = [(near, far)[y][k] for k, y in which]
        operands = join(*owns, *[swap_cores(own) for own in owns])
        count = len(which)
        out = expert_apply(expert, operands[:count], operands[count:], expert_weights, token_count)
        out = join(*out, *[table[key] for table, key in coming])
        for (table, key), value in zip(coming, out[count + 1 :]):
            table[key] = value
        from_core = swap_cores(out[count])
        for i, place_of in enumerate(which):
            swapped = from_core[i * token_count : (i + 1) * token_count]
            sums[place_of] = out[i].astype(jnp.float32) + swapped.astype(jnp.float32)

    run([(0, 0)], (near, 1), (far, 0), (travel, "up"))
    sides = [[i, i + 1] for i in range(0, lax.axis_size("rep"), 2)]
    both_sides = lax.all_gather(travel.pop("up"), "rep", axis=0, axis_index_groups=sides)
    run([(1, 0), (0, 1)], *[(near, k) for k in near if k > 1], start_far(1))
    for k in range(2, steps):
        coming = [start_far(k)]
        for j in range(3, steps):
            if j not in near and j ^ (j & -j) == k:
                coming.append(start_near(j))
        previous = [(k - 2, 1)] if k == last else [(k - 2, 1), (k - 1, 0)]
        coming += [send(p, sums[p], 2 * p[0] + p[1]) for p in previous]
        run([(k, 0), (k - 1, 1)], *coming)
    run(
        [(last, 1)],
        send((last - 1, 1), sums[last - 1, 1], 1),
        send((last, 0), sums[last, 0], 2),
    )
    send((last, 1), sums[last, 1], 3)
    shared = sums[last - 1, 0]
    for name in ((last - 1, 1), (last, 0), (last, 1)):
        shared += travel.pop(name).astype(jnp.float32)
    shared = shared.astype(jnp.bfloat16)
    both_sides = after(both_sides, sums[last, 1])
    send("shared", shared, 2 * last - 2)
    *terms, swapped_sides = join(sums[0, 0], *travel.values(), swap_cores(both_sides))
    both_sides = pltpu.with_memory_space_constraint(both_sides, pltpu.HBM)
    return project(group, terms, both_sides, swapped_sides)


def solution(mesh):
    in_specs = (
        P(("rep", "grp", "ep"), None),
        P(("rep", "grp", "ep"), None),
        P(("rep", "grp", "ep"), None),
        P("ep", None),
        P(("grp", "ep"), None, None),
        P(("grp", "ep"), None, None),
        P(("grp", "ep"), None, None),
        P(None, "ep"),
    )
    out_specs = P(("rep", "grp", "ep"), None)
    return jax.shard_map(body, mesh=mesh, in_specs=in_specs, out_specs=out_specs, check_vma=False)
```

```python
import functools

import jax
import jax.numpy as jnp
from jax import lax
from jax.experimental import pallas as pl
from jax.experimental.pallas import tpu as pltpu
from jax.sharding import PartitionSpec as P

route_scale = 2.5
mebi = 1024 * 1024
in_vmem = pl.BlockSpec(memory_space=pltpu.VMEM)
in_smem = pl.BlockSpec(memory_space=pltpu.SMEM)
in_hbm = pl.BlockSpec(memory_space=pltpu.HBM)
anywhere = pl.BlockSpec(memory_space=pl.ANY)


def after(value, *others):
    return lax.optimization_barrier((value, *others))[0]


def join(*values):
    return lax.optimization_barrier(values)


def swap_cores(array):
    return lax.ppermute(array, "grp", [(0, 1), (1, 0)])


def swap_reps(array):
    return lax.ppermute(array, "rep", [(i, i ^ 1) for i in range(lax.axis_size("rep"))])


def swap_ep(array, mask):
    return lax.ppermute(array, "ep", [(i, i ^ mask) for i in range(lax.axis_size("ep"))])


def first_steps(piece, steps):
    return {0: piece} | {k: swap_ep(piece, 2 * k) for k in range(1, steps) if k & (k - 1) == 0}


def dense_weights(expert_ids, route_scores, expert_count):
    sigmoids = jax.nn.sigmoid(route_scores)
    weights = (route_scale * sigmoids / jnp.sum(sigmoids, axis=1, keepdims=True)).astype(
        jnp.bfloat16
    )
    named = expert_ids[None, :, :] == jnp.arange(expert_count, dtype=jnp.int32)[:, None, None]
    return jnp.sum(jnp.where(named, weights.astype(jnp.float32)[None, :, :], 0.0), axis=2)


def columns_kernel(ep_count, quarter, where, tokens, kept, given):
    place, side, group = where[0], where[1], where[2]
    for offset in range(ep_count):
        for core in range(2):
            to = pl.ds(((offset // 2 * 2 + core) * 2 + offset % 2) * quarter, quarter)
            shard = (place ^ offset) * 4 + (group ^ core)
            for half, part in ((side, kept), (1 - side, given)):
                start = pl.multiple_of((shard + 2 * half) * quarter, quarter)
                part[:, to] = tokens[:, pl.ds(start, quarter)]


def split_columns(tokens, ep_count, quarter, place, side, group):
    count = tokens.shape[0]
    if quarter % 128 == 0:
        half = jax.ShapeDtypeStruct((count, 2 * ep_count * quarter), tokens.dtype)
        return pl.pallas_call(
            functools.partial(columns_kernel, ep_count, quarter),
            out_shape=(half, half),
            in_specs=[in_smem, in_vmem],
            out_specs=(in_vmem, in_vmem),
            compiler_params=pltpu.CompilerParams(vmem_limit_bytes=8 * mebi),
            name="split_columns",
        )(jnp.stack([place, side, group]).astype(jnp.int32), tokens)
    cut = tokens.reshape(count, ep_count, 2, 2, quarter)
    parts = [], []
    for step in range(ep_count // 2):
        for core in (group, 1 - group):
            for offset in (2 * step, 2 * step + 1):
                for half, part in zip((side, 1 - side), parts):
                    start = (0, place ^ offset, half, core, 0)
                    part.append(lax.dynamic_slice(cut, start, (count, 1, 1, 1, quarter)))
    kept, given = [jnp.stack(part, axis=1).reshape(count, -1) for part in parts]
    return kept, given


def down_kernel(steps, last, *refs):
    (kept, given), blocks = refs[:2], refs[2 : 2 + 4 * len(steps)]
    so_far, results = (refs[-3], refs[-2:]) if last else (None, refs[-1:])
    depth = 2 * blocks[0].shape[0]
    width = 256
    for start in range(0, blocks[0].shape[1], width):
        columns = slice(start, start + width)
        total = 0.0 if so_far is None else so_far[:, columns]
        for i, step in enumerate(steps):
            for core in range(2):
                inner = pl.ds((2 * step + core) * depth, depth)
                rows = jnp.concatenate([kept[:, inner], given[:, inner]], axis=0)
                near, far = blocks[4 * i + 2 * core], blocks[4 * i + 2 * core + 1]
                block = jnp.concatenate([near[:, columns], far[:, columns]], axis=0)
                total += jnp.dot(rows, block, preferred_element_type=jnp.float32)
        if last:
            count = kept.shape[0]
            results[0][:, columns] = total[:count]
            results[1][:, columns] = total[count:].astype(jnp.bfloat16)
        else:
            results[0][:, columns] = total


def down_project(steps, kept, given, blocks, so_far=None):
    count, inner = kept.shape
    latent_width = blocks[0].shape[1]
    operands = (kept, given, *blocks) + (() if so_far is None else (so_far,))
    if so_far is None:
        shapes = (jax.ShapeDtypeStruct((2 * count, latent_width), jnp.float32),)
    else:
        shapes = (
            jax.ShapeDtypeStruct((count, latent_width), jnp.float32),
            jax.ShapeDtypeStruct((count, latent_width), jnp.bfloat16),
        )
    return pl.pallas_call(
        functools.partial(down_kernel, steps, so_far is not None),
        out_shape=shapes,
        in_specs=[in_vmem] * len(operands),
        out_specs=(in_vmem,) * len(shapes),
        compiler_params=pltpu.CompilerParams(vmem_limit_bytes=16 * mebi),
        cost_estimate=pl.CostEstimate(
            flops=16 * len(steps) * count * blocks[0].shape[0] * latent_width,
            bytes_accessed=2 * len(blocks) * blocks[0].shape[0] * latent_width,
            transcendentals=0,
        ),
        name="down_project",
    )(*operands)


def latent_kernel(own_part, arrived, weights, piece):
    count = own_part.shape[0]
    total = own_part[...] + arrived[...].astype(jnp.float32)
    piece[:count] = total.astype(jnp.bfloat16)
    extra = piece.shape[0] - count
    piece[count:] = jnp.zeros((extra, piece.shape[1]), jnp.bfloat16)
    piece[count:, :count] = weights[...]


def finish_latent(own_part, arrived, weights):
    count, latent_width = own_part.shape
    return pl.pallas_call(
        latent_kernel,
        out_shape=jax.ShapeDtypeStruct((count + weights.shape[0], latent_width), jnp.bfloat16),
        in_specs=[in_vmem] * 3,
        out_specs=in_vmem,
        compiler_params=pltpu.CompilerParams(vmem_limit_bytes=4 * mebi),
        name="finish_latent",
    )(own_part, arrived, weights)


def expert_kernel(positions, count, where, *refs):
    pieces = refs[: 2 * positions]
    gate, up, out = refs[2 * positions : 2 * positions + 3]
    own_sums, refs = refs[2 * positions + 3 : 3 * positions + 3], refs[3 * positions + 3 :]
    other_sums, rows, hidden, held, gate_block, up_block, out_block, sems = refs
    width = 256
    blocks = gate.shape[2] // width

    def columns_at(start):
        return pl.ds(pl.multiple_of(start, width), width)

    def read(i, part):
        source, target = ((gate, gate_block), (up, up_block), (out, out_block))[part]
        columns = columns_at(i * width)
        return pltpu.make_async_copy(
            source.at[0, :, columns], target.at[:, columns], sems.at[part * blocks + i]
        )

    for i in range(blocks):
        read(i, 0).start()
        read(i, 1).start()
    for i in range(out.shape[2] // width):
        read(i, 2).start()
    for i, piece in enumerate(pieces):
        rows[i * count : (i + 1) * count] = piece[:count]

    def scale_of(piece):
        weights = piece[count:, :count].astype(jnp.float32)
        expert = lax.broadcasted_iota(jnp.int32, weights.shape, 0)
        line = jnp.sum(jnp.where(expert == where[0], weights, 0.0), axis=0, keepdims=True)
        row = lax.broadcasted_iota(jnp.int32, (count, count), 0)
        column = lax.broadcasted_iota(jnp.int32, (count, count), 1)
        return jnp.sum(jnp.where(row == column, line, 0.0), axis=1, keepdims=True)

    scales = [scale_of(piece) for piece in pieces]

    def arrive(i):
        read(i, 0).wait()
        read(i, 1).wait()

    def products(i):
        columns = columns_at(i * width)
        return [
            jnp.dot(rows[...], block[:, columns], preferred_element_type=jnp.float32)
            for block in (gate_block, up_block)
        ]

    def activate(gate_value, up_value, i):
        value = gate_value / (1.0 + jnp.exp(-gate_value)) * up_value
        hidden[:, columns_at(i * width)] = value.astype(jnp.bfloat16)

    arrive(0)
    held[0], held[1] = products(0)

    def step(i, carry):
        arrive(2 * i + 1)
        arrive(2 * i + 2)
        first = products(2 * i + 1)
        activate(held[0], held[1], 2 * i)
        second = products(2 * i + 2)
        activate(*first, 2 * i + 1)
        held[0], held[1] = second
        return carry

    lax.fori_loop(0, blocks // 2 - 1, step, 0)
    arrive(blocks - 1)
    last = products(blocks - 1)
    activate(held[0], held[1], blocks - 2)
    activate(*last, blocks - 1)

    def finish(i, carry):
        columns = columns_at(i * width)
        read(i, 2).wait()
        value = jnp.dot(hidden[...], out_block[:, columns], preferred_element_type=jnp.float32)
        for j, scale in enumerate(scales):
            scaled = (value[j * count : (j + 1) * count] * scale).astype(jnp.bfloat16)
            if j < positions:
                own_sums[j][:, columns] = scaled
            else:
                other_sums[(j - positions) * count : (j - positions + 1) * count, columns] = scaled
        return carry

    lax.fori_loop(0, out.shape[2] // width, finish, 0)


def expert_apply(expert, owns, others, weights, count):
    positions = len(owns)
    latent_width = owns[0].shape[1]
    hidden_width = weights[0].shape[2]
    rows, width = 2 * positions * count, 256
    own_sum = jax.ShapeDtypeStruct((count, latent_width), jnp.bfloat16)
    other_sums = jax.ShapeDtypeStruct((positions * count, latent_width), jnp.bfloat16)
    return pl.pallas_call(
        functools.partial(expert_kernel, positions, count),
        out_shape=(own_sum,) * positions + (other_sums,),
        in_specs=[in_smem] + [in_vmem] * (2 * positions) + [in_hbm] * 3,
        out_specs=(in_vmem,) * (positions + 1),
        scratch_shapes=[
            pltpu.VMEM((rows, latent_width), jnp.bfloat16),
            pltpu.VMEM((rows, hidden_width), jnp.bfloat16),
            pltpu.VMEM((2, rows, width), jnp.float32),
        ]
        + [pltpu.VMEM(w.shape[1:], w.dtype) for w in weights]
        + [pltpu.SemaphoreType.DMA(((2 * hidden_width + latent_width) // width,))],
        compiler_params=pltpu.CompilerParams(vmem_limit_bytes=28 * mebi),
        cost_estimate=pl.CostEstimate(
            flops=3 * rows * latent_width * hidden_width // 2,
            bytes_accessed=4 * rows * latent_width,
            transcendentals=0,
        ),
        name="expert",
    )(expert, *owns, *others, *weights)


def project_kernel(where, *refs):
    terms, refs = refs[:-8], refs[-8:]
    mine, swapped, layer_out, combined, held, blocks, read_sems, sems = refs
    sides, ep_count, inner, width = mine.shape

    def read(e, side):
        return pltpu.make_async_copy(
            mine.at[side, e], held.at[side, e], read_sems.at[sides * e + side]
        )

    for e in range(ep_count):
        for side in range(sides):
            read(e, side).start()
    total = terms[0][...].astype(jnp.float32)
    for term in terms[1:]:
        total += term[...].astype(jnp.float32)
    combined[...] = total.astype(jnp.bfloat16)

    def sent(e):
        columns = pl.ds(e * width, width)
        return pltpu.make_async_copy(blocks.at[:, columns], layer_out.at[:, columns], sems.at[e])

    for e in range(ep_count):
        value = 0.0
        for side in range(sides):
            read(e, side).wait()
            for core, array in ((1 - where[0], swapped), (where[0], held)):
                columns = pl.ds(pl.multiple_of((2 * side + core) * inner, inner), inner)
                value += jnp.dot(
                    combined[:, columns], array[side, e], preferred_element_type=jnp.float32
                )
        blocks[:, e * width : (e + 1) * width] = value.astype(jnp.bfloat16)
        sent(e).start()
    for e in range(ep_count):
        sent(e).wait()


def project(group, terms, mine, swapped):
    count, latent_width = terms[0].shape
    sides, ep_count, inner, width = mine.shape
    return pl.pallas_call(
        project_kernel,
        in_specs=[in_smem] + [in_vmem] * len(terms) + [in_hbm, in_vmem],
        out_specs=anywhere,
        out_shape=jax.ShapeDtypeStruct((count, ep_count * width), jnp.bfloat16),
        scratch_shapes=[
            pltpu.VMEM((count, latent_width), jnp.bfloat16),
            pltpu.VMEM(mine.shape, mine.dtype),
            pltpu.VMEM((count, ep_count * width), jnp.bfloat16),
            pltpu.SemaphoreType.DMA((sides * ep_count,)),
            pltpu.SemaphoreType.DMA((ep_count,)),
        ],
        compiler_params=pltpu.CompilerParams(vmem_limit_bytes=16 * mebi),
        cost_estimate=pl.CostEstimate(
            flops=2 * count * latent_width * ep_count * width,
            bytes_accessed=2 * latent_width * ep_count * width,
            transcendentals=0,
        ),
        name="project",
    )(group.reshape(1).astype(jnp.int32), *terms, mine, swapped)


def body(
    tokens, expert_ids, route_scores, down_latent, gate_weight, up_weight, out_weight, up_latent
):
    group_count = lax.axis_size("grp")
    ep_count = lax.axis_size("ep")
    expert_count = group_count * ep_count * gate_weight.shape[0]
    rep, group, place = lax.axis_index("rep"), lax.axis_index("grp"), lax.axis_index("ep")
    side = rep % 2
    own_quarter = 2 * side + group
    token_count = tokens.shape[0]
    latent_width = down_latent.shape[1]
    steps = ep_count // 2
    last = steps - 1

    quarter = down_latent.shape[0] // 4

    def own_piece(core):
        return lax.dynamic_slice_in_dim(down_latent, (2 * side + core) * quarter, quarter, 0)

    kept, given = split_columns(tokens, ep_count, quarter, place, side, group)
    taken = swap_reps(given)
    near = first_steps(own_piece(group), steps)
    far = {0: swap_ep(near[0], 1)}
    near[1], kept = join(near[1], kept)
    far[1] = swap_ep(near[1], 1)

    inner = latent_width // 4
    up_piece = lax.dynamic_slice_in_dim(up_latent, own_quarter * inner, inner, 0)
    mine = lax.all_gather(up_piece, "ep", axis=0)
    weights = dense_weights(after(expert_ids, near[1]), route_scores, expert_count)
    others = {k: near[k] for k in near if k > 1}
    far[1], weights, *arrived = join(far[1], weights, *others.values())
    near.update(zip(others, arrived))
    for k in range(2, steps):
        if k & (k - 1):
            low = k & -k
            near[k] = swap_ep(near[k ^ low], 2 * low)
        if k == last:
            near[k], far[0], taken = join(near[k], far[0], taken)
        far[k] = swap_ep(near[k], 1)
    blocks = []
    for k in range(steps):
        other = own_piece(1 - group) if k == 0 else swap_cores(near[k])
        blocks.append((near[k], far[k], other, swap_cores(far[k])))
    early = list(range(last))
    (partial,) = down_project(early, kept, taken, [b for k in early for b in blocks[k]])
    late = [after(blocks[-1][0], partial), *blocks[-1][1:]]
    own_part, sent_part = down_project([last], kept, taken, late, partial)
    latent = finish_latent(own_part, swap_reps(sent_part), weights.astype(jnp.bfloat16))

    expert = (group * ep_count + place).astype(jnp.int32).reshape(1)
    expert_weights = [
        pltpu.with_memory_space_constraint(w, pltpu.HBM)
        for w in (gate_weight, up_weight, out_weight)
    ]
    near = first_steps(latent, steps)
    far = {0: swap_ep(latent, 1)}
    sums, travel, taken_in = {}, {"up": mine}, set()

    def start_near(k):
        near[k] = swap_ep(near[k ^ (k & -k)], 2 * (k & -k))
        return near, k

    def start_far(k):
        far[k] = swap_ep(near[k], 1)
        return far, k

    def send(name, value, mask):
        travel[name] = swap_ep(value.astype(jnp.bfloat16), mask)
        return travel, name

    def run(which, *coming):
        owns = [(near, far)[y][k] for k, y in which]
        operands = join(*owns, *[swap_cores(own) for own in owns])
        count = len(which)
        out = expert_apply(expert, operands[:count], operands[count:], expert_weights, token_count)
        out = join(*out, *[table[key] for table, key in coming])
        for (table, key), value in zip(coming, out[count + 1 :]):
            table[key] = value
        from_core = swap_cores(out[count])
        for i, place_of in enumerate(which):
            swapped = from_core[i * token_count : (i + 1) * token_count]
            sums[place_of] = out[i].astype(jnp.float32) + swapped.astype(jnp.float32)

    run([(0, 0)], (near, 1), (far, 0), (travel, "up"))
    sides = [[i, i + 1] for i in range(0, lax.axis_size("rep"), 2)]
    both_sides = lax.all_gather(travel.pop("up"), "rep", axis=0, axis_index_groups=sides)
    run([(1, 0), (0, 1)], *[(near, k) for k in near if k > 1], start_far(1))
    for k in range(2, steps):
        coming = [start_far(k)]
        for j in range(3, steps):
            if j not in near and j ^ (j & -j) == k:
                coming.append(start_near(j))
        previous = [(k - 2, 1)] if k == last else [(k - 2, 1), (k - 1, 0)]
        coming += [send(p, sums[p], 2 * p[0] + p[1]) for p in previous]
        run([(k, 0), (k - 1, 1)], *coming)
    run(
        [(last, 1)],
        send((last - 1, 1), sums[last - 1, 1], 1),
        send((last, 0), sums[last, 0], 2),
    )
    send((last, 1), sums[last, 1], 3)
    shared = sums[last - 1, 0]
    for name in ((last - 1, 1), (last, 0), (last, 1)):
        shared += travel.pop(name).astype(jnp.float32)
    shared = shared.astype(jnp.bfloat16)
    both_sides = after(both_sides, shared)
    send("shared", shared, 2 * last - 2)
    *terms, swapped_sides = join(sums[0, 0], *travel.values(), swap_cores(both_sides))
    both_sides = pltpu.with_memory_space_constraint(both_sides, pltpu.HBM)
    return project(group, terms, both_sides, swapped_sides)


def solution(mesh):
    in_specs = (
        P(("rep", "grp", "ep"), None),
        P(("rep", "grp", "ep"), None),
        P(("rep", "grp", "ep"), None),
        P("ep", None),
        P(("grp", "ep"), None, None),
        P(("grp", "ep"), None, None),
        P(("grp", "ep"), None, None),
        P(None, "ep"),
    )
    out_specs = P(("rep", "grp", "ep"), None)
    return jax.shard_map(body, mesh=mesh, in_specs=in_specs, out_specs=out_specs, check_vma=False)
```

```python
import functools

import jax
import jax.numpy as jnp
from jax import lax
from jax.experimental import pallas as pl
from jax.experimental.pallas import tpu as pltpu
from jax.sharding import PartitionSpec as P

route_scale = 2.5
mebi = 1024 * 1024
in_vmem = pl.BlockSpec(memory_space=pltpu.VMEM)
in_smem = pl.BlockSpec(memory_space=pltpu.SMEM)
in_hbm = pl.BlockSpec(memory_space=pltpu.HBM)
anywhere = pl.BlockSpec(memory_space=pl.ANY)


def after(value, *others):
    return lax.optimization_barrier((value, *others))[0]


def join(*values):
    return lax.optimization_barrier(values)


def swap_cores(array):
    return lax.ppermute(array, "grp", [(0, 1), (1, 0)])


def swap_reps(array):
    return lax.ppermute(array, "rep", [(i, i ^ 1) for i in range(lax.axis_size("rep"))])


def swap_ep(array, mask):
    return lax.ppermute(array, "ep", [(i, i ^ mask) for i in range(lax.axis_size("ep"))])


def first_steps(piece, steps):
    return {0: piece} | {k: swap_ep(piece, 2 * k) for k in range(1, steps) if k & (k - 1) == 0}


def dense_weights(expert_ids, route_scores, expert_count):
    sigmoids = jax.nn.sigmoid(route_scores)
    weights = (route_scale * sigmoids / jnp.sum(sigmoids, axis=1, keepdims=True)).astype(
        jnp.bfloat16
    )
    named = expert_ids[None, :, :] == jnp.arange(expert_count, dtype=jnp.int32)[:, None, None]
    return jnp.sum(jnp.where(named, weights.astype(jnp.float32)[None, :, :], 0.0), axis=2)


def columns_kernel(ep_count, quarter, where, tokens, kept, given):
    place, side, group = where[0], where[1], where[2]
    for offset in range(ep_count):
        for core in range(2):
            to = pl.ds(((offset // 2 * 2 + core) * 2 + offset % 2) * quarter, quarter)
            shard = (place ^ offset) * 4 + (group ^ core)
            for half, part in ((side, kept), (1 - side, given)):
                start = pl.multiple_of((shard + 2 * half) * quarter, quarter)
                part[:, to] = tokens[:, pl.ds(start, quarter)]


def split_columns(tokens, ep_count, quarter, place, side, group):
    count = tokens.shape[0]
    if quarter % 128 == 0:
        half = jax.ShapeDtypeStruct((count, 2 * ep_count * quarter), tokens.dtype)
        return pl.pallas_call(
            functools.partial(columns_kernel, ep_count, quarter),
            out_shape=(half, half),
            in_specs=[in_smem, in_vmem],
            out_specs=(in_vmem, in_vmem),
            compiler_params=pltpu.CompilerParams(vmem_limit_bytes=8 * mebi),
            name="split_columns",
        )(jnp.stack([place, side, group]).astype(jnp.int32), tokens)
    cut = tokens.reshape(count, ep_count, 2, 2, quarter)
    parts = [], []
    for step in range(ep_count // 2):
        for core in (group, 1 - group):
            for offset in (2 * step, 2 * step + 1):
                for half, part in zip((side, 1 - side), parts):
                    start = (0, place ^ offset, half, core, 0)
                    part.append(lax.dynamic_slice(cut, start, (count, 1, 1, 1, quarter)))
    kept, given = [jnp.stack(part, axis=1).reshape(count, -1) for part in parts]
    return kept, given


def down_kernel(steps, last, *refs):
    (kept, given), blocks = refs[:2], refs[2 : 2 + 4 * len(steps)]
    so_far, results = (refs[-3], refs[-2:]) if last else (None, refs[-1:])
    depth = 2 * blocks[0].shape[0]
    width = 256
    for start in range(0, blocks[0].shape[1], width):
        columns = slice(start, start + width)
        total = 0.0 if so_far is None else so_far[:, columns]
        for i, step in enumerate(steps):
            for core in range(2):
                inner = pl.ds((2 * step + core) * depth, depth)
                rows = jnp.concatenate([kept[:, inner], given[:, inner]], axis=0)
                near, far = blocks[4 * i + 2 * core], blocks[4 * i + 2 * core + 1]
                block = jnp.concatenate([near[:, columns], far[:, columns]], axis=0)
                total += jnp.dot(rows, block, preferred_element_type=jnp.float32)
        if last:
            count = kept.shape[0]
            results[0][:, columns] = total[:count]
            results[1][:, columns] = total[count:].astype(jnp.bfloat16)
        else:
            results[0][:, columns] = total


def down_project(steps, kept, given, blocks, so_far=None):
    count, inner = kept.shape
    latent_width = blocks[0].shape[1]
    operands = (kept, given, *blocks) + (() if so_far is None else (so_far,))
    if so_far is None:
        shapes = (jax.ShapeDtypeStruct((2 * count, latent_width), jnp.float32),)
    else:
        shapes = (
            jax.ShapeDtypeStruct((count, latent_width), jnp.float32),
            jax.ShapeDtypeStruct((count, latent_width), jnp.bfloat16),
        )
    return pl.pallas_call(
        functools.partial(down_kernel, steps, so_far is not None),
        out_shape=shapes,
        in_specs=[in_vmem] * len(operands),
        out_specs=(in_vmem,) * len(shapes),
        compiler_params=pltpu.CompilerParams(vmem_limit_bytes=16 * mebi),
        cost_estimate=pl.CostEstimate(
            flops=16 * len(steps) * count * blocks[0].shape[0] * latent_width,
            bytes_accessed=2 * len(blocks) * blocks[0].shape[0] * latent_width,
            transcendentals=0,
        ),
        name="down_project",
    )(*operands)


def latent_kernel(own_part, arrived, weights, piece):
    count = own_part.shape[0]
    total = own_part[...] + arrived[...].astype(jnp.float32)
    piece[:count] = total.astype(jnp.bfloat16)
    extra = piece.shape[0] - count
    piece[count:] = jnp.zeros((extra, piece.shape[1]), jnp.bfloat16)
    piece[count:, :count] = weights[...]


def finish_latent(own_part, arrived, weights):
    count, latent_width = own_part.shape
    return pl.pallas_call(
        latent_kernel,
        out_shape=jax.ShapeDtypeStruct((count + weights.shape[0], latent_width), jnp.bfloat16),
        in_specs=[in_vmem] * 3,
        out_specs=in_vmem,
        compiler_params=pltpu.CompilerParams(vmem_limit_bytes=4 * mebi),
        name="finish_latent",
    )(own_part, arrived, weights)


def expert_kernel(positions, count, where, *refs):
    pieces = refs[: 2 * positions]
    gate, up, out = refs[2 * positions : 2 * positions + 3]
    own_sums, refs = refs[2 * positions + 3 : 3 * positions + 3], refs[3 * positions + 3 :]
    other_sums, rows, hidden, held, gate_block, up_block, out_block, sems = refs
    width = 256
    blocks = gate.shape[2] // width

    def columns_at(start):
        return pl.ds(pl.multiple_of(start, width), width)

    chunks = blocks // 2 + 1

    def read(j, part, size):
        source, target = ((gate, gate_block), (up, up_block), (out, out_block))[part]
        start = 2 * j * width if part == 2 else max(2 * j - 1, 0) * width
        return copy_columns(source, target, start, size, sems.at[part * chunks + j])

    def copy_columns(source, target, start, size, sem):
        columns = pl.ds(pl.multiple_of(start, width), size)
        return pltpu.make_async_copy(source.at[0, :, columns], target.at[:, columns], sem)

    def size_of(j):
        return width if j in (0, chunks - 1) else 2 * width

    out_chunks = out.shape[2] // (2 * width)
    for j in range(chunks):
        read(j, 0, size_of(j)).start()
        read(j, 1, size_of(j)).start()
    for j in range(out_chunks):
        read(j, 2, 2 * width).start()
    for i, piece in enumerate(pieces):
        rows[i * count : (i + 1) * count] = piece[:count]

    def scale_of(piece):
        weights = piece[count:, :count].astype(jnp.float32)
        expert = lax.broadcasted_iota(jnp.int32, weights.shape, 0)
        line = jnp.sum(jnp.where(expert == where[0], weights, 0.0), axis=0, keepdims=True)
        row = lax.broadcasted_iota(jnp.int32, (count, count), 0)
        column = lax.broadcasted_iota(jnp.int32, (count, count), 1)
        return jnp.sum(jnp.where(row == column, line, 0.0), axis=1, keepdims=True)

    scales = [scale_of(piece) for piece in pieces]

    def arrive(j, start, size):
        copy_columns(gate, gate_block, start, size, sems.at[j]).wait()
        copy_columns(up, up_block, start, size, sems.at[chunks + j]).wait()

    def products(i):
        columns = columns_at(i * width)
        return [
            jnp.dot(rows[...], block[:, columns], preferred_element_type=jnp.float32)
            for block in (gate_block, up_block)
        ]

    def activate(gate_value, up_value, i):
        value = gate_value / (1.0 + jnp.exp(-gate_value)) * up_value
        hidden[:, columns_at(i * width)] = value.astype(jnp.bfloat16)

    arrive(0, 0, width)
    held[0], held[1] = products(0)

    def step(i, carry):
        arrive(i + 1, (2 * i + 1) * width, 2 * width)
        first = products(2 * i + 1)
        activate(held[0], held[1], 2 * i)
        second = products(2 * i + 2)
        activate(*first, 2 * i + 1)
        held[0], held[1] = second
        return carry

    lax.fori_loop(0, blocks // 2 - 1, step, 0)
    arrive(chunks - 1, (blocks - 1) * width, width)
    last = products(blocks - 1)
    activate(held[0], held[1], blocks - 2)
    activate(*last, blocks - 1)

    def finish(i, carry):
        copy_columns(out, out_block, 2 * i * width, 2 * width, sems.at[2 * chunks + i]).wait()
        for half in range(2):
            columns = columns_at((2 * i + half) * width)
            value = jnp.dot(hidden[...], out_block[:, columns], preferred_element_type=jnp.float32)
            for j, scale in enumerate(scales):
                scaled = (value[j * count : (j + 1) * count] * scale).astype(jnp.bfloat16)
                if j < positions:
                    own_sums[j][:, columns] = scaled
                else:
                    start = (j - positions) * count
                    other_sums[start : start + count, columns] = scaled
        return carry

    lax.fori_loop(0, out_chunks, finish, 0)


def expert_apply(expert, owns, others, weights, count):
    positions = len(owns)
    latent_width = owns[0].shape[1]
    hidden_width = weights[0].shape[2]
    rows, width = 2 * positions * count, 256
    own_sum = jax.ShapeDtypeStruct((count, latent_width), jnp.bfloat16)
    other_sums = jax.ShapeDtypeStruct((positions * count, latent_width), jnp.bfloat16)
    return pl.pallas_call(
        functools.partial(expert_kernel, positions, count),
        out_shape=(own_sum,) * positions + (other_sums,),
        in_specs=[in_smem] + [in_vmem] * (2 * positions) + [in_hbm] * 3,
        out_specs=(in_vmem,) * (positions + 1),
        scratch_shapes=[
            pltpu.VMEM((rows, latent_width), jnp.bfloat16),
            pltpu.VMEM((rows, hidden_width), jnp.bfloat16),
            pltpu.VMEM((2, rows, width), jnp.float32),
        ]
        + [pltpu.VMEM(w.shape[1:], w.dtype) for w in weights]
        + [pltpu.SemaphoreType.DMA((hidden_width // width + 2 + latent_width // (2 * width),))],
        compiler_params=pltpu.CompilerParams(vmem_limit_bytes=28 * mebi),
        cost_estimate=pl.CostEstimate(
            flops=3 * rows * latent_width * hidden_width // 2,
            bytes_accessed=4 * rows * latent_width,
            transcendentals=0,
        ),
        name="expert",
    )(expert, *owns, *others, *weights)


def project_kernel(where, *refs):
    terms, refs = refs[:-8], refs[-8:]
    mine, swapped, layer_out, combined, held, blocks, read_sems, sems = refs
    sides, ep_count, inner, width = mine.shape

    def read(e, side):
        return pltpu.make_async_copy(
            mine.at[side, e], held.at[side, e], read_sems.at[sides * e + side]
        )

    for e in range(ep_count):
        for side in range(sides):
            read(e, side).start()
    total = terms[0][...].astype(jnp.float32)
    for term in terms[1:]:
        total += term[...].astype(jnp.float32)
    combined[...] = total.astype(jnp.bfloat16)

    def sent(e):
        columns = pl.ds(e * width, width)
        return pltpu.make_async_copy(blocks.at[:, columns], layer_out.at[:, columns], sems.at[e])

    for e in range(ep_count):
        value = 0.0
        for side in range(sides):
            read(e, side).wait()
            for core, array in ((1 - where[0], swapped), (where[0], held)):
                columns = pl.ds(pl.multiple_of((2 * side + core) * inner, inner), inner)
                value += jnp.dot(
                    combined[:, columns], array[side, e], preferred_element_type=jnp.float32
                )
        blocks[:, e * width : (e + 1) * width] = value.astype(jnp.bfloat16)
        sent(e).start()
    for e in range(ep_count):
        sent(e).wait()


def project(group, terms, mine, swapped):
    count, latent_width = terms[0].shape
    sides, ep_count, inner, width = mine.shape
    return pl.pallas_call(
        project_kernel,
        in_specs=[in_smem] + [in_vmem] * len(terms) + [in_hbm, in_vmem],
        out_specs=anywhere,
        out_shape=jax.ShapeDtypeStruct((count, ep_count * width), jnp.bfloat16),
        scratch_shapes=[
            pltpu.VMEM((count, latent_width), jnp.bfloat16),
            pltpu.VMEM(mine.shape, mine.dtype),
            pltpu.VMEM((count, ep_count * width), jnp.bfloat16),
            pltpu.SemaphoreType.DMA((sides * ep_count,)),
            pltpu.SemaphoreType.DMA((ep_count,)),
        ],
        compiler_params=pltpu.CompilerParams(vmem_limit_bytes=16 * mebi),
        cost_estimate=pl.CostEstimate(
            flops=2 * count * latent_width * ep_count * width,
            bytes_accessed=2 * latent_width * ep_count * width,
            transcendentals=0,
        ),
        name="project",
    )(group.reshape(1).astype(jnp.int32), *terms, mine, swapped)


def body(
    tokens, expert_ids, route_scores, down_latent, gate_weight, up_weight, out_weight, up_latent
):
    group_count = lax.axis_size("grp")
    ep_count = lax.axis_size("ep")
    expert_count = group_count * ep_count * gate_weight.shape[0]
    rep, group, place = lax.axis_index("rep"), lax.axis_index("grp"), lax.axis_index("ep")
    side = rep % 2
    own_quarter = 2 * side + group
    token_count = tokens.shape[0]
    latent_width = down_latent.shape[1]
    steps = ep_count // 2
    last = steps - 1

    quarter = down_latent.shape[0] // 4

    def own_piece(core):
        return lax.dynamic_slice_in_dim(down_latent, (2 * side + core) * quarter, quarter, 0)

    kept, given = split_columns(tokens, ep_count, quarter, place, side, group)
    taken = swap_reps(given)
    near = first_steps(own_piece(group), steps)
    far = {0: swap_ep(near[0], 1)}
    near[1], kept = join(near[1], kept)
    far[1] = swap_ep(near[1], 1)

    inner = latent_width // 4
    up_piece = lax.dynamic_slice_in_dim(up_latent, own_quarter * inner, inner, 0)
    mine = lax.all_gather(up_piece, "ep", axis=0)
    weights = dense_weights(after(expert_ids, near[1]), route_scores, expert_count)
    others = {k: near[k] for k in near if k > 1}
    far[1], weights, *arrived = join(far[1], weights, *others.values())
    near.update(zip(others, arrived))
    for k in range(2, steps):
        if k & (k - 1):
            low = k & -k
            near[k] = swap_ep(near[k ^ low], 2 * low)
        if k == last:
            near[k], far[0], taken = join(near[k], far[0], taken)
        far[k] = swap_ep(near[k], 1)
    blocks = []
    for k in range(steps):
        other = own_piece(1 - group) if k == 0 else swap_cores(near[k])
        blocks.append((near[k], far[k], other, swap_cores(far[k])))
    early = list(range(last))
    (partial,) = down_project(early, kept, taken, [b for k in early for b in blocks[k]])
    late = [after(blocks[-1][0], partial), *blocks[-1][1:]]
    own_part, sent_part = down_project([last], kept, taken, late, partial)
    latent = finish_latent(own_part, swap_reps(sent_part), weights.astype(jnp.bfloat16))

    expert = (group * ep_count + place).astype(jnp.int32).reshape(1)
    expert_weights = [
        pltpu.with_memory_space_constraint(w, pltpu.HBM)
        for w in (gate_weight, up_weight, out_weight)
    ]
    near = first_steps(latent, steps)
    far = {0: swap_ep(latent, 1)}
    sums, travel, taken_in = {}, {"up": mine}, set()

    def start_near(k):
        near[k] = swap_ep(near[k ^ (k & -k)], 2 * (k & -k))
        return near, k

    def start_far(k):
        far[k] = swap_ep(near[k], 1)
        return far, k

    def send(name, value, mask):
        travel[name] = swap_ep(value.astype(jnp.bfloat16), mask)
        return travel, name

    def run(which, *coming):
        owns = [(near, far)[y][k] for k, y in which]
        operands = join(*owns, *[swap_cores(own) for own in owns])
        count = len(which)
        out = expert_apply(expert, operands[:count], operands[count:], expert_weights, token_count)
        out = join(*out, *[table[key] for table, key in coming])
        for (table, key), value in zip(coming, out[count + 1 :]):
            table[key] = value
        from_core = swap_cores(out[count])
        for i, place_of in enumerate(which):
            swapped = from_core[i * token_count : (i + 1) * token_count]
            sums[place_of] = out[i].astype(jnp.float32) + swapped.astype(jnp.float32)

    special = [(0, 0), (last - 1, 0), (last - 1, 1), (last, 0)]

    def homeward(*previous):
        return [send(p, sums[p], 2 * p[0] + p[1]) for p in previous if p not in special]

    run([(0, 0)], *[(near, k) for k in near if k], (travel, "up"))
    sides = [[i, i + 1] for i in range(0, lax.axis_size("rep"), 2)]
    both_sides = lax.all_gather(travel.pop("up"), "rep", axis=0, axis_index_groups=sides)
    previous = [(2, 0), (1, 0)]
    run(previous, *[start_near(3)] * (last >= 3), start_far(2))
    for k in range(3, steps):
        coming = homeward(*previous) + [start_far(k)] + [(far, 0)] * (k == last)
        if k + 1 < steps and k + 1 not in near:
            coming.append(start_near(k + 1))
        previous = [(k, 0), (k - 1, 1)]
        run(previous, *coming)
    run(
        [(last, 1), (0, 1)],
        send((last - 1, 1), sums[last - 1, 1], 1),
        send((last, 0), sums[last, 0], 2),
        start_far(1),
    )
    run([(1, 1)], send((last, 1), sums[last, 1], 3), *homeward((0, 1)))
    shared = sums[last - 1, 0]
    for name in ((last - 1, 1), (last, 0), (last, 1)):
        shared += travel.pop(name).astype(jnp.float32)
    shared = shared.astype(jnp.bfloat16)
    send("shared", shared, 2 * last - 2)
    sums[1, 1] = sums[1, 1].astype(jnp.bfloat16)
    both_sides = after(both_sides, sums[1, 1], shared)
    homeward((1, 1))
    *terms, swapped_sides = join(sums[0, 0], *travel.values(), swap_cores(both_sides))
    both_sides = pltpu.with_memory_space_constraint(both_sides, pltpu.HBM)
    return project(group, terms, both_sides, swapped_sides)


def solution(mesh):
    in_specs = (
        P(("rep", "grp", "ep"), None),
        P(("rep", "grp", "ep"), None),
        P(("rep", "grp", "ep"), None),
        P("ep", None),
        P(("grp", "ep"), None, None),
        P(("grp", "ep"), None, None),
        P(("grp", "ep"), None, None),
        P(None, "ep"),
    )
    out_specs = P(("rep", "grp", "ep"), None)
    return jax.shard_map(body, mesh=mesh, in_specs=in_specs, out_specs=out_specs, check_vma=False)
```

```python
import functools

import jax
import jax.numpy as jnp
from jax import lax
from jax.experimental import pallas as pl
from jax.experimental.pallas import tpu as pltpu
from jax.sharding import PartitionSpec as P

route_scale = 2.5
mebi = 1024 * 1024
in_vmem = pl.BlockSpec(memory_space=pltpu.VMEM)
in_smem = pl.BlockSpec(memory_space=pltpu.SMEM)
in_hbm = pl.BlockSpec(memory_space=pltpu.HBM)
anywhere = pl.BlockSpec(memory_space=pl.ANY)


def after(value, *others):
    return lax.optimization_barrier((value, *others))[0]


def join(*values):
    return lax.optimization_barrier(values)


def swap_cores(array):
    return lax.ppermute(array, "grp", [(0, 1), (1, 0)])


def swap_reps(array):
    return lax.ppermute(array, "rep", [(i, i ^ 1) for i in range(lax.axis_size("rep"))])


def swap_ep(array, mask):
    return lax.ppermute(array, "ep", [(i, i ^ mask) for i in range(lax.axis_size("ep"))])


def first_steps(piece, steps):
    return {0: piece} | {k: swap_ep(piece, 2 * k) for k in range(1, steps) if k & (k - 1) == 0}


def dense_weights(expert_ids, route_scores, expert_count):
    sigmoids = jax.nn.sigmoid(route_scores)
    weights = (route_scale * sigmoids / jnp.sum(sigmoids, axis=1, keepdims=True)).astype(
        jnp.bfloat16
    )
    named = expert_ids[None, :, :] == jnp.arange(expert_count, dtype=jnp.int32)[:, None, None]
    return jnp.sum(jnp.where(named, weights.astype(jnp.float32)[None, :, :], 0.0), axis=2)


def cut_kernel(where, down, up, own, other, up_piece, sems):
    pairs = []
    for core, piece, shard in ((0, own, down), (1, other, down), (0, up_piece, up)):
        rows = piece.shape[0]
        start = pl.multiple_of((where[0] ^ core) * rows, rows)
        pairs.append((shard.at[pl.ds(start, rows)], piece))
    copies = [pltpu.make_async_copy(*pair, sems.at[i]) for i, pair in enumerate(pairs)]
    for copy in copies:
        copy.start()
    for copy in copies:
        copy.wait()


def cut_quarters(quarter, down, up):
    shapes = [
        jax.ShapeDtypeStruct((array.shape[0] // 4, array.shape[1]), array.dtype)
        for array in (down, down, up)
    ]
    return pl.pallas_call(
        cut_kernel,
        out_shape=shapes,
        in_specs=[in_smem] + [in_hbm] * 2,
        out_specs=[anywhere] * 3,
        scratch_shapes=[pltpu.SemaphoreType.DMA((3,))],
        compiler_params=pltpu.CompilerParams(vmem_limit_bytes=mebi),
        name="cut_quarters",
    )(
        quarter.reshape(1).astype(jnp.int32),
        *[pltpu.with_memory_space_constraint(array, pltpu.HBM) for array in (down, up)],
    )


def columns_kernel(ep_count, quarter, where, tokens, kept, given):
    place, side, group = where[0], where[1], where[2]
    for offset in range(ep_count):
        for core in range(2):
            to = pl.ds(((offset // 2 * 2 + core) * 2 + offset % 2) * quarter, quarter)
            shard = (place ^ offset) * 4 + (group ^ core)
            for half, part in ((side, kept), (1 - side, given)):
                start = pl.multiple_of((shard + 2 * half) * quarter, quarter)
                part[:, to] = tokens[:, pl.ds(start, quarter)]


def split_columns(tokens, ep_count, quarter, place, side, group):
    count = tokens.shape[0]
    if quarter % 128 == 0:
        half = jax.ShapeDtypeStruct((count, 2 * ep_count * quarter), tokens.dtype)
        return pl.pallas_call(
            functools.partial(columns_kernel, ep_count, quarter),
            out_shape=(half, half),
            in_specs=[in_smem, in_vmem],
            out_specs=(in_vmem, in_vmem),
            compiler_params=pltpu.CompilerParams(vmem_limit_bytes=8 * mebi),
            name="split_columns",
        )(jnp.stack([place, side, group]).astype(jnp.int32), tokens)
    cut = tokens.reshape(count, ep_count, 2, 2, quarter)
    parts = [], []
    for step in range(ep_count // 2):
        for core in (group, 1 - group):
            for offset in (2 * step, 2 * step + 1):
                for half, part in zip((side, 1 - side), parts):
                    start = (0, place ^ offset, half, core, 0)
                    part.append(lax.dynamic_slice(cut, start, (count, 1, 1, 1, quarter)))
    kept, given = [jnp.stack(part, axis=1).reshape(count, -1) for part in parts]
    return kept, given


def down_kernel(steps, last, *refs):
    (kept, given), blocks = refs[:2], refs[2 : 2 + 4 * len(steps)]
    so_far, results = (refs[-3], refs[-2:]) if last else (None, refs[-1:])
    depth = 2 * blocks[0].shape[0]
    width = 256
    for start in range(0, blocks[0].shape[1], width):
        columns = slice(start, start + width)
        total = 0.0 if so_far is None else so_far[:, columns]
        for i, step in enumerate(steps):
            for core in range(2):
                inner = pl.ds((2 * step + core) * depth, depth)
                rows = jnp.concatenate([kept[:, inner], given[:, inner]], axis=0)
                near, far = blocks[4 * i + 2 * core], blocks[4 * i + 2 * core + 1]
                block = jnp.concatenate([near[:, columns], far[:, columns]], axis=0)
                total += jnp.dot(rows, block, preferred_element_type=jnp.float32)
        if last:
            count = kept.shape[0]
            results[0][:, columns] = total[:count]
            results[1][:, columns] = total[count:].astype(jnp.bfloat16)
        else:
            results[0][:, columns] = total


def down_project(steps, kept, given, blocks, so_far=None):
    count, inner = kept.shape
    latent_width = blocks[0].shape[1]
    operands = (kept, given, *blocks) + (() if so_far is None else (so_far,))
    if so_far is None:
        shapes = (jax.ShapeDtypeStruct((2 * count, latent_width), jnp.float32),)
    else:
        shapes = (
            jax.ShapeDtypeStruct((count, latent_width), jnp.float32),
            jax.ShapeDtypeStruct((count, latent_width), jnp.bfloat16),
        )
    return pl.pallas_call(
        functools.partial(down_kernel, steps, so_far is not None),
        out_shape=shapes,
        in_specs=[in_vmem] * len(operands),
        out_specs=(in_vmem,) * len(shapes),
        compiler_params=pltpu.CompilerParams(vmem_limit_bytes=16 * mebi),
        cost_estimate=pl.CostEstimate(
            flops=16 * len(steps) * count * blocks[0].shape[0] * latent_width,
            bytes_accessed=2 * len(blocks) * blocks[0].shape[0] * latent_width,
            transcendentals=0,
        ),
        name="down_project",
    )(*operands)


def latent_kernel(own_part, arrived, weights, piece):
    count = own_part.shape[0]
    total = own_part[...] + arrived[...].astype(jnp.float32)
    piece[:count] = total.astype(jnp.bfloat16)
    extra = piece.shape[0] - count
    piece[count:] = jnp.zeros((extra, piece.shape[1]), jnp.bfloat16)
    piece[count:, :count] = weights[...]


def finish_latent(own_part, arrived, weights):
    count, latent_width = own_part.shape
    return pl.pallas_call(
        latent_kernel,
        out_shape=jax.ShapeDtypeStruct((count + weights.shape[0], latent_width), jnp.bfloat16),
        in_specs=[in_vmem] * 3,
        out_specs=in_vmem,
        compiler_params=pltpu.CompilerParams(vmem_limit_bytes=4 * mebi),
        name="finish_latent",
    )(own_part, arrived, weights)


def expert_kernel(positions, count, where, *refs):
    pieces = refs[: 2 * positions]
    gate, up, out = refs[2 * positions : 2 * positions + 3]
    own_sums, refs = refs[2 * positions + 3 : 3 * positions + 3], refs[3 * positions + 3 :]
    other_sums, rows, hidden, held, gate_block, up_block, out_block, sems = refs
    width = 256
    blocks = gate.shape[2] // width

    def columns_at(start):
        return pl.ds(pl.multiple_of(start, width), width)

    chunks = blocks // 2 + 1

    def read(j, part, size):
        source, target = ((gate, gate_block), (up, up_block), (out, out_block))[part]
        start = 2 * j * width if part == 2 else max(2 * j - 1, 0) * width
        return copy_columns(source, target, start, size, sems.at[part * chunks + j])

    def copy_columns(source, target, start, size, sem):
        columns = pl.ds(pl.multiple_of(start, width), size)
        return pltpu.make_async_copy(source.at[0, :, columns], target.at[:, columns], sem)

    def size_of(j):
        return width if j in (0, chunks - 1) else 2 * width

    out_chunks = out.shape[2] // (2 * width)
    for j in range(chunks):
        read(j, 0, size_of(j)).start()
        read(j, 1, size_of(j)).start()
    for j in range(out_chunks):
        read(j, 2, 2 * width).start()
    for i, piece in enumerate(pieces):
        rows[i * count : (i + 1) * count] = piece[:count]

    def scale_of(piece):
        weights = piece[count:, :count].astype(jnp.float32)
        expert = lax.broadcasted_iota(jnp.int32, weights.shape, 0)
        line = jnp.sum(jnp.where(expert == where[0], weights, 0.0), axis=0, keepdims=True)
        row = lax.broadcasted_iota(jnp.int32, (count, count), 0)
        column = lax.broadcasted_iota(jnp.int32, (count, count), 1)
        return jnp.sum(jnp.where(row == column, line, 0.0), axis=1, keepdims=True)

    scales = [scale_of(piece) for piece in pieces]

    def arrive(j, start, size):
        copy_columns(gate, gate_block, start, size, sems.at[j]).wait()
        copy_columns(up, up_block, start, size, sems.at[chunks + j]).wait()

    def products(i):
        columns = columns_at(i * width)
        return [
            jnp.dot(rows[...], block[:, columns], preferred_element_type=jnp.float32)
            for block in (gate_block, up_block)
        ]

    def activate(gate_value, up_value, i):
        value = gate_value / (1.0 + jnp.exp(-gate_value)) * up_value
        hidden[:, columns_at(i * width)] = value.astype(jnp.bfloat16)

    arrive(0, 0, width)
    held[0], held[1] = products(0)

    def step(i, carry):
        arrive(i + 1, (2 * i + 1) * width, 2 * width)
        first = products(2 * i + 1)
        activate(held[0], held[1], 2 * i)
        second = products(2 * i + 2)
        activate(*first, 2 * i + 1)
        held[0], held[1] = second
        return carry

    lax.fori_loop(0, blocks // 2 - 1, step, 0)
    arrive(chunks - 1, (blocks - 1) * width, width)
    last = products(blocks - 1)
    activate(held[0], held[1], blocks - 2)
    activate(*last, blocks - 1)

    def finish(i, carry):
        copy_columns(out, out_block, 2 * i * width, 2 * width, sems.at[2 * chunks + i]).wait()
        for half in range(2):
            columns = columns_at((2 * i + half) * width)
            value = jnp.dot(hidden[...], out_block[:, columns], preferred_element_type=jnp.float32)
            for j, scale in enumerate(scales):
                scaled = (value[j * count : (j + 1) * count] * scale).astype(jnp.bfloat16)
                if j < positions:
                    own_sums[j][:, columns] = scaled
                else:
                    start = (j - positions) * count
                    other_sums[start : start + count, columns] = scaled
        return carry

    lax.fori_loop(0, out_chunks, finish, 0)


def expert_apply(expert, owns, others, weights, count):
    positions = len(owns)
    latent_width = owns[0].shape[1]
    hidden_width = weights[0].shape[2]
    rows, width = 2 * positions * count, 256
    own_sum = jax.ShapeDtypeStruct((count, latent_width), jnp.bfloat16)
    other_sums = jax.ShapeDtypeStruct((positions * count, latent_width), jnp.bfloat16)
    return pl.pallas_call(
        functools.partial(expert_kernel, positions, count),
        out_shape=(own_sum,) * positions + (other_sums,),
        in_specs=[in_smem] + [in_vmem] * (2 * positions) + [in_hbm] * 3,
        out_specs=(in_vmem,) * (positions + 1),
        scratch_shapes=[
            pltpu.VMEM((rows, latent_width), jnp.bfloat16),
            pltpu.VMEM((rows, hidden_width), jnp.bfloat16),
            pltpu.VMEM((2, rows, width), jnp.float32),
        ]
        + [pltpu.VMEM(w.shape[1:], w.dtype) for w in weights]
        + [pltpu.SemaphoreType.DMA((hidden_width // width + 2 + latent_width // (2 * width),))],
        compiler_params=pltpu.CompilerParams(vmem_limit_bytes=28 * mebi),
        cost_estimate=pl.CostEstimate(
            flops=3 * rows * latent_width * hidden_width // 2,
            bytes_accessed=4 * rows * latent_width,
            transcendentals=0,
        ),
        name="expert",
    )(expert, *owns, *others, *weights)


def project_kernel(where, *refs):
    terms, refs = refs[:-8], refs[-8:]
    mine, swapped, layer_out, combined, held, blocks, read_sems, sems = refs
    sides, ep_count, inner, width = mine.shape

    def read(e, side):
        return pltpu.make_async_copy(
            mine.at[side, e], held.at[side, e], read_sems.at[sides * e + side]
        )

    for e in range(ep_count):
        for side in range(sides):
            read(e, side).start()
    total = terms[0][...].astype(jnp.float32)
    for term in terms[1:]:
        total += term[...].astype(jnp.float32)
    combined[...] = total.astype(jnp.bfloat16)

    def sent(e):
        columns = pl.ds(e * width, width)
        return pltpu.make_async_copy(blocks.at[:, columns], layer_out.at[:, columns], sems.at[e])

    for e in range(ep_count):
        value = 0.0
        for side in range(sides):
            read(e, side).wait()
            for core, array in ((1 - where[0], swapped), (where[0], held)):
                columns = pl.ds(pl.multiple_of((2 * side + core) * inner, inner), inner)
                value += jnp.dot(
                    combined[:, columns], array[side, e], preferred_element_type=jnp.float32
                )
        blocks[:, e * width : (e + 1) * width] = value.astype(jnp.bfloat16)
        sent(e).start()
    for e in range(ep_count):
        sent(e).wait()


def project(group, terms, mine, swapped):
    count, latent_width = terms[0].shape
    sides, ep_count, inner, width = mine.shape
    return pl.pallas_call(
        project_kernel,
        in_specs=[in_smem] + [in_vmem] * len(terms) + [in_hbm, in_vmem],
        out_specs=anywhere,
        out_shape=jax.ShapeDtypeStruct((count, ep_count * width), jnp.bfloat16),
        scratch_shapes=[
            pltpu.VMEM((count, latent_width), jnp.bfloat16),
            pltpu.VMEM(mine.shape, mine.dtype),
            pltpu.VMEM((count, ep_count * width), jnp.bfloat16),
            pltpu.SemaphoreType.DMA((sides * ep_count,)),
            pltpu.SemaphoreType.DMA((ep_count,)),
        ],
        compiler_params=pltpu.CompilerParams(vmem_limit_bytes=16 * mebi),
        cost_estimate=pl.CostEstimate(
            flops=2 * count * latent_width * ep_count * width,
            bytes_accessed=2 * latent_width * ep_count * width,
            transcendentals=0,
        ),
        name="project",
    )(group.reshape(1).astype(jnp.int32), *terms, mine, swapped)


def body(
    tokens, expert_ids, route_scores, down_latent, gate_weight, up_weight, out_weight, up_latent
):
    group_count = lax.axis_size("grp")
    ep_count = lax.axis_size("ep")
    expert_count = group_count * ep_count * gate_weight.shape[0]
    rep, group, place = lax.axis_index("rep"), lax.axis_index("grp"), lax.axis_index("ep")
    side = rep % 2
    own_quarter = 2 * side + group
    token_count = tokens.shape[0]
    latent_width = down_latent.shape[1]
    steps = ep_count // 2
    last = steps - 1

    quarter = down_latent.shape[0] // 4

    own_piece, other_piece, up_piece = cut_quarters(own_quarter, down_latent, up_latent)
    kept, given = split_columns(tokens, ep_count, quarter, place, side, group)
    taken = swap_reps(given)
    near = first_steps(own_piece, steps)
    far = {0: swap_ep(near[0], 1)}
    near[1], kept = join(near[1], kept)
    far[1] = swap_ep(near[1], 1)

    mine = lax.all_gather(up_piece, "ep", axis=0)
    weights = dense_weights(after(expert_ids, near[1]), route_scores, expert_count)
    others = {k: near[k] for k in near if k > 1}
    far[1], weights, *arrived = join(far[1], weights, *others.values())
    near.update(zip(others, arrived))
    for k in range(2, steps):
        if k & (k - 1):
            low = k & -k
            near[k] = swap_ep(near[k ^ low], 2 * low)
        if k == last:
            near[k], far[0], taken = join(near[k], far[0], taken)
        far[k] = swap_ep(near[k], 1)
    blocks = []
    for k in range(steps):
        other = other_piece if k == 0 else swap_cores(near[k])
        blocks.append((near[k], far[k], other, swap_cores(far[k])))
    early = list(range(last))
    (partial,) = down_project(early, kept, taken, [b for k in early for b in blocks[k]])
    late = [after(blocks[-1][0], partial), *blocks[-1][1:]]
    own_part, sent_part = down_project([last], kept, taken, late, partial)
    latent = finish_latent(own_part, swap_reps(sent_part), weights.astype(jnp.bfloat16))

    expert = (group * ep_count + place).astype(jnp.int32).reshape(1)
    expert_weights = [
        pltpu.with_memory_space_constraint(w, pltpu.HBM)
        for w in (gate_weight, up_weight, out_weight)
    ]
    near = first_steps(latent, steps)
    far = {0: swap_ep(latent, 1)}
    sums, travel, taken_in = {}, {"up": mine}, set()

    def start_near(k):
        near[k] = swap_ep(near[k ^ (k & -k)], 2 * (k & -k))
        return near, k

    def start_far(k):
        far[k] = swap_ep(near[k], 1)
        return far, k

    def send(name, value, mask):
        travel[name] = swap_ep(value.astype(jnp.bfloat16), mask)
        return travel, name

    def run(which, *coming):
        owns = [(near, far)[y][k] for k, y in which]
        operands = join(*owns, *[swap_cores(own) for own in owns])
        count = len(which)
        out = expert_apply(expert, operands[:count], operands[count:], expert_weights, token_count)
        out = join(*out, *[table[key] for table, key in coming])
        for (table, key), value in zip(coming, out[count + 1 :]):
            table[key] = value
        from_core = swap_cores(out[count])
        for i, place_of in enumerate(which):
            swapped = from_core[i * token_count : (i + 1) * token_count]
            sums[place_of] = out[i].astype(jnp.float32) + swapped.astype(jnp.float32)

    special = [(0, 0), (last - 1, 0), (last - 1, 1), (last, 0)]

    def homeward(*previous):
        return [send(p, sums[p], 2 * p[0] + p[1]) for p in previous if p not in special]

    run([(0, 0)], *[(near, k) for k in near if k], (travel, "up"))
    sides = [[i, i + 1] for i in range(0, lax.axis_size("rep"), 2)]
    both_sides = lax.all_gather(travel.pop("up"), "rep", axis=0, axis_index_groups=sides)
    previous = [(2, 0), (1, 0)]
    run(previous, *[start_near(3)] * (last >= 3), start_far(2))
    for k in range(3, steps):
        coming = homeward(*previous) + [start_far(k)] + [(far, 0)] * (k == last)
        if k + 1 < steps and k + 1 not in near:
            coming.append(start_near(k + 1))
        previous = [(k, 0), (k - 1, 1)]
        run(previous, *coming)
    run(
        [(last, 1), (0, 1)],
        send((last - 1, 1), sums[last - 1, 1], 1),
        send((last, 0), sums[last, 0], 2),
        start_far(1),
    )
    run([(1, 1)], send((last, 1), sums[last, 1], 3))
    shared = sums[last - 1, 0]
    for name in ((last - 1, 1), (last, 0), (last, 1)):
        shared += travel.pop(name).astype(jnp.float32)
    shared = shared.astype(jnp.bfloat16)
    send("shared", shared, 2 * last - 2)
    sums[1, 1] = sums[1, 1].astype(jnp.bfloat16)
    both_sides = after(both_sides, sums[1, 1], shared)
    homeward((0, 1), (1, 1))
    *terms, swapped_sides = join(sums[0, 0], *travel.values(), swap_cores(both_sides))
    both_sides = pltpu.with_memory_space_constraint(both_sides, pltpu.HBM)
    return project(group, terms, both_sides, swapped_sides)


def solution(mesh):
    in_specs = (
        P(("rep", "grp", "ep"), None),
        P(("rep", "grp", "ep"), None),
        P(("rep", "grp", "ep"), None),
        P("ep", None),
        P(("grp", "ep"), None, None),
        P(("grp", "ep"), None, None),
        P(("grp", "ep"), None, None),
        P(None, "ep"),
    )
    out_specs = P(("rep", "grp", "ep"), None)
    return jax.shard_map(body, mesh=mesh, in_specs=in_specs, out_specs=out_specs, check_vma=False)
```

```python
import functools

import jax
import jax.numpy as jnp
from jax import lax
from jax.experimental import pallas as pl
from jax.experimental.pallas import tpu as pltpu
from jax.sharding import PartitionSpec as P

route_scale = 2.5
mebi = 1024 * 1024
in_vmem = pl.BlockSpec(memory_space=pltpu.VMEM)
in_smem = pl.BlockSpec(memory_space=pltpu.SMEM)
in_hbm = pl.BlockSpec(memory_space=pltpu.HBM)
anywhere = pl.BlockSpec(memory_space=pl.ANY)


def after(value, *others):
    return lax.optimization_barrier((value, *others))[0]


def join(*values):
    return lax.optimization_barrier(values)


def swap_cores(array):
    return lax.ppermute(array, "grp", [(0, 1), (1, 0)])


def swap_reps(array):
    return lax.ppermute(array, "rep", [(i, i ^ 1) for i in range(lax.axis_size("rep"))])


def swap_ep(array, mask):
    return lax.ppermute(array, "ep", [(i, i ^ mask) for i in range(lax.axis_size("ep"))])


def first_steps(piece, steps):
    return {0: piece} | {k: swap_ep(piece, 2 * k) for k in range(1, steps) if k & (k - 1) == 0}


def dense_weights(expert_ids, route_scores, expert_count):
    sigmoids = jax.nn.sigmoid(route_scores)
    weights = (route_scale * sigmoids / jnp.sum(sigmoids, axis=1, keepdims=True)).astype(
        jnp.bfloat16
    )
    named = expert_ids[None, :, :] == jnp.arange(expert_count, dtype=jnp.int32)[:, None, None]
    return jnp.sum(jnp.where(named, weights.astype(jnp.float32)[None, :, :], 0.0), axis=2)


def columns_kernel(ep_count, quarter, where, tokens, kept, given):
    place, side, group = where[0], where[1], where[2]
    for offset in range(ep_count):
        for core in range(2):
            to = pl.ds(((offset // 2 * 2 + core) * 2 + offset % 2) * quarter, quarter)
            shard = (place ^ offset) * 4 + (group ^ core)
            for half, part in ((side, kept), (1 - side, given)):
                start = pl.multiple_of((shard + 2 * half) * quarter, quarter)
                part[:, to] = tokens[:, pl.ds(start, quarter)]


def split_columns(tokens, ep_count, quarter, place, side, group):
    count = tokens.shape[0]
    if quarter % 128 == 0:
        half = jax.ShapeDtypeStruct((count, 2 * ep_count * quarter), tokens.dtype)
        return pl.pallas_call(
            functools.partial(columns_kernel, ep_count, quarter),
            out_shape=(half, half),
            in_specs=[in_smem, in_vmem],
            out_specs=(in_vmem, in_vmem),
            compiler_params=pltpu.CompilerParams(vmem_limit_bytes=8 * mebi),
            name="split_columns",
        )(jnp.stack([place, side, group]).astype(jnp.int32), tokens)
    cut = tokens.reshape(count, ep_count, 2, 2, quarter)
    parts = [], []
    for step in range(ep_count // 2):
        for core in (group, 1 - group):
            for offset in (2 * step, 2 * step + 1):
                for half, part in zip((side, 1 - side), parts):
                    start = (0, place ^ offset, half, core, 0)
                    part.append(lax.dynamic_slice(cut, start, (count, 1, 1, 1, quarter)))
    kept, given = [jnp.stack(part, axis=1).reshape(count, -1) for part in parts]
    return kept, given


def down_kernel(steps, last, *refs):
    (kept, given), blocks = refs[:2], refs[2 : 2 + 4 * len(steps)]
    so_far, results = (refs[-3], refs[-2:]) if last else (None, refs[-1:])
    depth = 2 * blocks[0].shape[0]
    width = 256
    for start in range(0, blocks[0].shape[1], width):
        columns = slice(start, start + width)
        total = 0.0 if so_far is None else so_far[:, columns]
        for i, step in enumerate(steps):
            for core in range(2):
                inner = pl.ds((2 * step + core) * depth, depth)
                rows = jnp.concatenate([kept[:, inner], given[:, inner]], axis=0)
                near, far = blocks[4 * i + 2 * core], blocks[4 * i + 2 * core + 1]
                block = jnp.concatenate([near[:, columns], far[:, columns]], axis=0)
                total += jnp.dot(rows, block, preferred_element_type=jnp.float32)
        if last:
            count = kept.shape[0]
            results[0][:, columns] = total[:count]
            results[1][:, columns] = total[count:].astype(jnp.bfloat16)
        else:
            results[0][:, columns] = total


def down_project(steps, kept, given, blocks, so_far=None):
    count, inner = kept.shape
    latent_width = blocks[0].shape[1]
    operands = (kept, given, *blocks) + (() if so_far is None else (so_far,))
    if so_far is None:
        shapes = (jax.ShapeDtypeStruct((2 * count, latent_width), jnp.float32),)
    else:
        shapes = (
            jax.ShapeDtypeStruct((count, latent_width), jnp.float32),
            jax.ShapeDtypeStruct((count, latent_width), jnp.bfloat16),
        )
    return pl.pallas_call(
        functools.partial(down_kernel, steps, so_far is not None),
        out_shape=shapes,
        in_specs=[in_vmem] * len(operands),
        out_specs=(in_vmem,) * len(shapes),
        compiler_params=pltpu.CompilerParams(vmem_limit_bytes=16 * mebi),
        cost_estimate=pl.CostEstimate(
            flops=16 * len(steps) * count * blocks[0].shape[0] * latent_width,
            bytes_accessed=2 * len(blocks) * blocks[0].shape[0] * latent_width,
            transcendentals=0,
        ),
        name="down_project",
    )(*operands)


def latent_kernel(own_part, arrived, weights, piece):
    count = own_part.shape[0]
    total = own_part[...] + arrived[...].astype(jnp.float32)
    piece[:count] = total.astype(jnp.bfloat16)
    extra = piece.shape[0] - count
    piece[count:] = jnp.zeros((extra, piece.shape[1]), jnp.bfloat16)
    piece[count:, :count] = weights[...]


def finish_latent(own_part, arrived, weights):
    count, latent_width = own_part.shape
    return pl.pallas_call(
        latent_kernel,
        out_shape=jax.ShapeDtypeStruct((count + weights.shape[0], latent_width), jnp.bfloat16),
        in_specs=[in_vmem] * 3,
        out_specs=in_vmem,
        compiler_params=pltpu.CompilerParams(vmem_limit_bytes=4 * mebi),
        name="finish_latent",
    )(own_part, arrived, weights)


def expert_kernel(positions, count, where, *refs):
    pieces = refs[: 2 * positions]
    gate, up, out = refs[2 * positions : 2 * positions + 3]
    own_sums, refs = refs[2 * positions + 3 : 3 * positions + 3], refs[3 * positions + 3 :]
    other_sums, rows, hidden, held, gate_block, up_block, out_block, sems = refs
    width = 256
    blocks = gate.shape[2] // width

    def columns_at(start):
        return pl.ds(pl.multiple_of(start, width), width)

    chunks = blocks // 2 + 1

    def read(j, part, size):
        source, target = ((gate, gate_block), (up, up_block), (out, out_block))[part]
        start = 2 * j * width if part == 2 else max(2 * j - 1, 0) * width
        return copy_columns(source, target, start, size, sems.at[part * chunks + j])

    def copy_columns(source, target, start, size, sem):
        columns = pl.ds(pl.multiple_of(start, width), size)
        return pltpu.make_async_copy(source.at[0, :, columns], target.at[:, columns], sem)

    def size_of(j):
        return width if j in (0, chunks - 1) else 2 * width

    out_chunks = out.shape[2] // (2 * width)
    for j in range(chunks):
        read(j, 0, size_of(j)).start()
        read(j, 1, size_of(j)).start()
    for j in range(out_chunks):
        read(j, 2, 2 * width).start()
    for i, piece in enumerate(pieces):
        rows[i * count : (i + 1) * count] = piece[:count]

    def scale_of(piece):
        weights = piece[count:, :count].astype(jnp.float32)
        expert = lax.broadcasted_iota(jnp.int32, weights.shape, 0)
        line = jnp.sum(jnp.where(expert == where[0], weights, 0.0), axis=0, keepdims=True)
        row = lax.broadcasted_iota(jnp.int32, (count, count), 0)
        column = lax.broadcasted_iota(jnp.int32, (count, count), 1)
        return jnp.sum(jnp.where(row == column, line, 0.0), axis=1, keepdims=True)

    scales = [scale_of(piece) for piece in pieces]

    def arrive(j, start, size):
        copy_columns(gate, gate_block, start, size, sems.at[j]).wait()
        copy_columns(up, up_block, start, size, sems.at[chunks + j]).wait()

    def products(i):
        columns = columns_at(i * width)
        return [
            jnp.dot(rows[...], block[:, columns], preferred_element_type=jnp.float32)
            for block in (gate_block, up_block)
        ]

    def activate(gate_value, up_value, i):
        value = gate_value / (1.0 + jnp.exp(-gate_value)) * up_value
        hidden[:, columns_at(i * width)] = value.astype(jnp.bfloat16)

    arrive(0, 0, width)
    held[0], held[1] = products(0)

    def step(i, carry):
        arrive(i + 1, (2 * i + 1) * width, 2 * width)
        first = products(2 * i + 1)
        activate(held[0], held[1], 2 * i)
        second = products(2 * i + 2)
        activate(*first, 2 * i + 1)
        held[0], held[1] = second
        return carry

    lax.fori_loop(0, blocks // 2 - 1, step, 0)
    arrive(chunks - 1, (blocks - 1) * width, width)
    last = products(blocks - 1)
    activate(held[0], held[1], blocks - 2)
    activate(*last, blocks - 1)

    def finish(i, carry):
        copy_columns(out, out_block, 2 * i * width, 2 * width, sems.at[2 * chunks + i]).wait()
        for half in range(2):
            columns = columns_at((2 * i + half) * width)
            value = jnp.dot(hidden[...], out_block[:, columns], preferred_element_type=jnp.float32)
            for j, scale in enumerate(scales):
                scaled = (value[j * count : (j + 1) * count] * scale).astype(jnp.bfloat16)
                if j < positions:
                    own_sums[j][:, columns] = scaled
                else:
                    start = (j - positions) * count
                    other_sums[start : start + count, columns] = scaled
        return carry

    lax.fori_loop(0, out_chunks, finish, 0)


def expert_apply(expert, owns, others, weights, count):
    positions = len(owns)
    latent_width = owns[0].shape[1]
    hidden_width = weights[0].shape[2]
    rows, width = 2 * positions * count, 256
    own_sum = jax.ShapeDtypeStruct((count, latent_width), jnp.bfloat16)
    other_sums = jax.ShapeDtypeStruct((positions * count, latent_width), jnp.bfloat16)
    return pl.pallas_call(
        functools.partial(expert_kernel, positions, count),
        out_shape=(own_sum,) * positions + (other_sums,),
        in_specs=[in_smem] + [in_vmem] * (2 * positions) + [in_hbm] * 3,
        out_specs=(in_vmem,) * (positions + 1),
        scratch_shapes=[
            pltpu.VMEM((rows, latent_width), jnp.bfloat16),
            pltpu.VMEM((rows, hidden_width), jnp.bfloat16),
            pltpu.VMEM((2, rows, width), jnp.float32),
        ]
        + [pltpu.VMEM(w.shape[1:], w.dtype) for w in weights]
        + [pltpu.SemaphoreType.DMA((hidden_width // width + 2 + latent_width // (2 * width),))],
        compiler_params=pltpu.CompilerParams(vmem_limit_bytes=28 * mebi),
        cost_estimate=pl.CostEstimate(
            flops=3 * rows * latent_width * hidden_width // 2,
            bytes_accessed=4 * rows * latent_width,
            transcendentals=0,
        ),
        name="expert",
    )(expert, *owns, *others, *weights)


def project_kernel(where, *refs):
    terms, refs = refs[:-8], refs[-8:]
    mine, swapped, layer_out, combined, held, blocks, read_sems, sems = refs
    sides, ep_count, inner, width = mine.shape

    def read(e, side):
        return pltpu.make_async_copy(
            mine.at[side, e], held.at[side, e], read_sems.at[sides * e + side]
        )

    for e in range(ep_count):
        for side in range(sides):
            read(e, side).start()
    total = terms[0][...].astype(jnp.float32)
    for term in terms[1:]:
        total += term[...].astype(jnp.float32)
    combined[...] = total.astype(jnp.bfloat16)

    def sent(e):
        columns = pl.ds(e * width, width)
        return pltpu.make_async_copy(blocks.at[:, columns], layer_out.at[:, columns], sems.at[e])

    for e in range(ep_count):
        value = 0.0
        for side in range(sides):
            read(e, side).wait()
            for core, array in ((1 - where[0], swapped), (where[0], held)):
                columns = pl.ds(pl.multiple_of((2 * side + core) * inner, inner), inner)
                value += jnp.dot(
                    combined[:, columns], array[side, e], preferred_element_type=jnp.float32
                )
        blocks[:, e * width : (e + 1) * width] = value.astype(jnp.bfloat16)
        sent(e).start()
    for e in range(ep_count):
        sent(e).wait()


def project(group, terms, mine, swapped):
    count, latent_width = terms[0].shape
    sides, ep_count, inner, width = mine.shape
    return pl.pallas_call(
        project_kernel,
        in_specs=[in_smem] + [in_vmem] * len(terms) + [in_hbm, in_vmem],
        out_specs=anywhere,
        out_shape=jax.ShapeDtypeStruct((count, ep_count * width), jnp.bfloat16),
        scratch_shapes=[
            pltpu.VMEM((count, latent_width), jnp.bfloat16),
            pltpu.VMEM(mine.shape, mine.dtype),
            pltpu.VMEM((count, ep_count * width), jnp.bfloat16),
            pltpu.SemaphoreType.DMA((sides * ep_count,)),
            pltpu.SemaphoreType.DMA((ep_count,)),
        ],
        compiler_params=pltpu.CompilerParams(vmem_limit_bytes=16 * mebi),
        cost_estimate=pl.CostEstimate(
            flops=2 * count * latent_width * ep_count * width,
            bytes_accessed=2 * latent_width * ep_count * width,
            transcendentals=0,
        ),
        name="project",
    )(group.reshape(1).astype(jnp.int32), *terms, mine, swapped)


def body(
    tokens, expert_ids, route_scores, down_latent, gate_weight, up_weight, out_weight, up_latent
):
    group_count = lax.axis_size("grp")
    ep_count = lax.axis_size("ep")
    expert_count = group_count * ep_count * gate_weight.shape[0]
    rep, group, place = lax.axis_index("rep"), lax.axis_index("grp"), lax.axis_index("ep")
    side = rep % 2
    own_quarter = 2 * side + group
    token_count = tokens.shape[0]
    latent_width = down_latent.shape[1]
    steps = ep_count // 2
    last = steps - 1

    quarter = down_latent.shape[0] // 4

    def own_piece(core):
        return lax.dynamic_slice_in_dim(down_latent, (2 * side + core) * quarter, quarter, 0)

    kept, given = split_columns(tokens, ep_count, quarter, place, side, group)
    taken = swap_reps(given)
    near = first_steps(own_piece(group), steps)
    far = {0: swap_ep(near[0], 1)}
    near[1], kept = join(near[1], kept)
    far[1] = swap_ep(near[1], 1)

    inner = latent_width // 4
    up_piece = lax.dynamic_slice_in_dim(up_latent, own_quarter * inner, inner, 0)
    mine = lax.all_gather(up_piece, "ep", axis=0)
    weights = dense_weights(after(expert_ids, near[1]), route_scores, expert_count)
    others = {k: near[k] for k in near if k > 1}
    far[1], weights, *arrived = join(far[1], weights, *others.values())
    near.update(zip(others, arrived))
    for k in range(2, steps):
        if k & (k - 1):
            low = k & -k
            near[k] = swap_ep(near[k ^ low], 2 * low)
        if k == last:
            near[k], far[0], taken = join(near[k], far[0], taken)
        far[k] = swap_ep(near[k], 1)
    blocks = []
    for k in range(steps):
        other = own_piece(1 - group) if k == 0 else swap_cores(near[k])
        blocks.append((near[k], far[k], other, swap_cores(far[k])))
    early = list(range(last))
    (partial,) = down_project(early, kept, taken, [b for k in early for b in blocks[k]])
    late = [after(blocks[-1][0], partial), *blocks[-1][1:]]
    own_part, sent_part = down_project([last], kept, taken, late, partial)
    latent = finish_latent(own_part, swap_reps(sent_part), weights.astype(jnp.bfloat16))

    expert = (group * ep_count + place).astype(jnp.int32).reshape(1)
    expert_weights = [
        pltpu.with_memory_space_constraint(w, pltpu.HBM)
        for w in (gate_weight, up_weight, out_weight)
    ]
    near = first_steps(latent, steps)
    far = {0: swap_ep(latent, 1)}
    sums, travel, taken_in = {}, {"up": mine}, set()

    def start_near(k):
        near[k] = swap_ep(near[k ^ (k & -k)], 2 * (k & -k))
        return near, k

    def start_far(k):
        far[k] = swap_ep(near[k], 1)
        return far, k

    def send(name, value, mask):
        travel[name] = swap_ep(value.astype(jnp.bfloat16), mask)
        return travel, name

    def run(which, *coming):
        owns = [(near, far)[y][k] for k, y in which]
        operands = join(*owns, *[swap_cores(own) for own in owns])
        count = len(which)
        out = expert_apply(expert, operands[:count], operands[count:], expert_weights, token_count)
        out = join(*out, *[table[key] for table, key in coming])
        for (table, key), value in zip(coming, out[count + 1 :]):
            table[key] = value
        from_core = swap_cores(out[count])
        for i, place_of in enumerate(which):
            swapped = from_core[i * token_count : (i + 1) * token_count]
            sums[place_of] = out[i].astype(jnp.float32) + swapped.astype(jnp.float32)

    special = [(0, 0), (last - 1, 0), (last - 1, 1), (last, 0)]

    def homeward(*previous):
        return [send(p, sums[p], 2 * p[0] + p[1]) for p in previous if p not in special]

    run([(0, 0)], *[(near, k) for k in near if k], (travel, "up"))
    sides = [[i, i + 1] for i in range(0, lax.axis_size("rep"), 2)]
    both_sides = lax.all_gather(travel.pop("up"), "rep", axis=0, axis_index_groups=sides)
    previous = [(2, 0), (1, 0)]
    run(previous, *[start_near(3)] * (last >= 3), start_far(2))
    for k in range(3, steps):
        coming = homeward(*previous) + [start_far(k)] + [(far, 0)] * (k == last)
        if k + 1 < steps and k + 1 not in near:
            coming.append(start_near(k + 1))
        previous = [(k, 0), (k - 1, 1)]
        run(previous, *coming)
    run(
        [(last, 1), (0, 1)],
        send((last - 1, 1), sums[last - 1, 1], 1),
        send((last, 0), sums[last, 0], 2),
        start_far(1),
    )
    run([(1, 1)], send((last, 1), sums[last, 1], 3))
    shared = sums[last - 1, 0]
    for name in ((last - 1, 1), (last, 0), (last, 1)):
        shared += travel.pop(name).astype(jnp.float32)
    shared = shared.astype(jnp.bfloat16)
    send("shared", shared, 2 * last - 2)
    sums[1, 1] = sums[1, 1].astype(jnp.bfloat16)
    both_sides = after(both_sides, sums[1, 1], shared)
    homeward((0, 1), (1, 1))
    *terms, swapped_sides = join(sums[0, 0], *travel.values(), swap_cores(both_sides))
    both_sides = pltpu.with_memory_space_constraint(both_sides, pltpu.HBM)
    return project(group, terms, both_sides, swapped_sides)


def solution(mesh):
    in_specs = (
        P(("rep", "grp", "ep"), None),
        P(("rep", "grp", "ep"), None),
        P(("rep", "grp", "ep"), None),
        P("ep", None),
        P(("grp", "ep"), None, None),
        P(("grp", "ep"), None, None),
        P(("grp", "ep"), None, None),
        P(None, "ep"),
    )
    out_specs = P(("rep", "grp", "ep"), None)
    return jax.shard_map(body, mesh=mesh, in_specs=in_specs, out_specs=out_specs, check_vma=False)
```

```python
import functools

import jax
import jax.numpy as jnp
from jax import lax
from jax.experimental import pallas as pl
from jax.experimental.pallas import tpu as pltpu
from jax.sharding import PartitionSpec as P

route_scale = 2.5
mebi = 1024 * 1024
in_vmem = pl.BlockSpec(memory_space=pltpu.VMEM)
in_smem = pl.BlockSpec(memory_space=pltpu.SMEM)
in_hbm = pl.BlockSpec(memory_space=pltpu.HBM)
anywhere = pl.BlockSpec(memory_space=pl.ANY)


def after(value, *others):
    return lax.optimization_barrier((value, *others))[0]


def join(*values):
    return lax.optimization_barrier(values)


def swap_cores(array):
    return lax.ppermute(array, "grp", [(0, 1), (1, 0)])


def swap_reps(array):
    return lax.ppermute(array, "rep", [(i, i ^ 1) for i in range(lax.axis_size("rep"))])


def swap_ep(array, mask):
    return lax.ppermute(array, "ep", [(i, i ^ mask) for i in range(lax.axis_size("ep"))])


def first_steps(piece, steps):
    return {0: piece} | {k: swap_ep(piece, 2 * k) for k in range(1, steps) if k & (k - 1) == 0}


def dense_weights(expert_ids, route_scores, expert_count):
    sigmoids = jax.nn.sigmoid(route_scores)
    weights = (route_scale * sigmoids / jnp.sum(sigmoids, axis=1, keepdims=True)).astype(
        jnp.bfloat16
    )
    named = expert_ids[None, :, :] == jnp.arange(expert_count, dtype=jnp.int32)[:, None, None]
    return jnp.sum(jnp.where(named, weights.astype(jnp.float32)[None, :, :], 0.0), axis=2)


def columns_kernel(ep_count, quarter, where, tokens, kept, given):
    place, side, group = where[0], where[1], where[2]
    for offset in range(ep_count):
        for core in range(2):
            to = pl.ds(((offset // 2 * 2 + core) * 2 + offset % 2) * quarter, quarter)
            shard = (place ^ offset) * 4 + (group ^ core)
            for half, part in ((side, kept), (1 - side, given)):
                start = pl.multiple_of((shard + 2 * half) * quarter, quarter)
                part[:, to] = tokens[:, pl.ds(start, quarter)]


def split_columns(tokens, ep_count, quarter, place, side, group):
    count = tokens.shape[0]
    if quarter % 128 == 0:
        half = jax.ShapeDtypeStruct((count, 2 * ep_count * quarter), tokens.dtype)
        return pl.pallas_call(
            functools.partial(columns_kernel, ep_count, quarter),
            out_shape=(half, half),
            in_specs=[in_smem, in_vmem],
            out_specs=(in_vmem, in_vmem),
            compiler_params=pltpu.CompilerParams(vmem_limit_bytes=8 * mebi),
            name="split_columns",
        )(jnp.stack([place, side, group]).astype(jnp.int32), tokens)
    cut = tokens.reshape(count, ep_count, 2, 2, quarter)
    parts = [], []
    for step in range(ep_count // 2):
        for core in (group, 1 - group):
            for offset in (2 * step, 2 * step + 1):
                for half, part in zip((side, 1 - side), parts):
                    start = (0, place ^ offset, half, core, 0)
                    part.append(lax.dynamic_slice(cut, start, (count, 1, 1, 1, quarter)))
    kept, given = [jnp.stack(part, axis=1).reshape(count, -1) for part in parts]
    return kept, given


def down_kernel(steps, last, *refs):
    (kept, given), blocks = refs[:2], refs[2 : 2 + 4 * len(steps)]
    so_far, results = (refs[-3], refs[-2:]) if last else (None, refs[-1:])
    depth = 2 * blocks[0].shape[0]
    width = 256
    for start in range(0, blocks[0].shape[1], width):
        columns = slice(start, start + width)
        total = 0.0 if so_far is None else so_far[:, columns]
        for i, step in enumerate(steps):
            for core in range(2):
                inner = pl.ds((2 * step + core) * depth, depth)
                rows = jnp.concatenate([kept[:, inner], given[:, inner]], axis=0)
                near, far = blocks[4 * i + 2 * core], blocks[4 * i + 2 * core + 1]
                block = jnp.concatenate([near[:, columns], far[:, columns]], axis=0)
                total += jnp.dot(rows, block, preferred_element_type=jnp.float32)
        if last:
            count = kept.shape[0]
            results[0][:, columns] = total[:count]
            results[1][:, columns] = total[count:].astype(jnp.bfloat16)
        else:
            results[0][:, columns] = total


def down_project(steps, kept, given, blocks, so_far=None):
    count, inner = kept.shape
    latent_width = blocks[0].shape[1]
    operands = (kept, given, *blocks) + (() if so_far is None else (so_far,))
    if so_far is None:
        shapes = (jax.ShapeDtypeStruct((2 * count, latent_width), jnp.float32),)
    else:
        shapes = (
            jax.ShapeDtypeStruct((count, latent_width), jnp.float32),
            jax.ShapeDtypeStruct((count, latent_width), jnp.bfloat16),
        )
    return pl.pallas_call(
        functools.partial(down_kernel, steps, so_far is not None),
        out_shape=shapes,
        in_specs=[in_vmem] * len(operands),
        out_specs=(in_vmem,) * len(shapes),
        compiler_params=pltpu.CompilerParams(vmem_limit_bytes=16 * mebi),
        cost_estimate=pl.CostEstimate(
            flops=16 * len(steps) * count * blocks[0].shape[0] * latent_width,
            bytes_accessed=2 * len(blocks) * blocks[0].shape[0] * latent_width,
            transcendentals=0,
        ),
        name="down_project",
    )(*operands)


def latent_kernel(own_part, arrived, weights, piece):
    count = own_part.shape[0]
    total = own_part[...] + arrived[...].astype(jnp.float32)
    piece[:count] = total.astype(jnp.bfloat16)
    extra = piece.shape[0] - count
    piece[count:] = jnp.zeros((extra, piece.shape[1]), jnp.bfloat16)
    piece[count:, :count] = weights[...]


def finish_latent(own_part, arrived, weights):
    count, latent_width = own_part.shape
    return pl.pallas_call(
        latent_kernel,
        out_shape=jax.ShapeDtypeStruct((count + weights.shape[0], latent_width), jnp.bfloat16),
        in_specs=[in_vmem] * 3,
        out_specs=in_vmem,
        compiler_params=pltpu.CompilerParams(vmem_limit_bytes=4 * mebi),
        name="finish_latent",
    )(own_part, arrived, weights)


def expert_kernel(positions, count, where, *refs):
    pieces = refs[: 2 * positions]
    gate, up, out = refs[2 * positions : 2 * positions + 3]
    own_sums, refs = refs[2 * positions + 3 : 3 * positions + 3], refs[3 * positions + 3 :]
    other_sums, rows, hidden, held, gate_block, up_block, out_block, sems = refs
    width = 256
    blocks = gate.shape[2] // width

    def columns_at(start):
        return pl.ds(pl.multiple_of(start, width), width)

    chunks = blocks // 2 + 1

    def read(j, part, size):
        source, target = ((gate, gate_block), (up, up_block), (out, out_block))[part]
        start = 2 * j * width if part == 2 else max(2 * j - 1, 0) * width
        return copy_columns(source, target, start, size, sems.at[part * chunks + j])

    def copy_columns(source, target, start, size, sem):
        columns = pl.ds(pl.multiple_of(start, width), size)
        return pltpu.make_async_copy(source.at[0, :, columns], target.at[:, columns], sem)

    def size_of(j):
        return width if j in (0, chunks - 1) else 2 * width

    out_chunks = out.shape[2] // (2 * width)
    for j in range(chunks):
        read(j, 0, size_of(j)).start()
        read(j, 1, size_of(j)).start()
    for j in range(out_chunks):
        read(j, 2, 2 * width).start()
    for i, piece in enumerate(pieces):
        rows[i * count : (i + 1) * count] = piece[:count]

    def scale_of(piece):
        weights = piece[count:, :count].astype(jnp.float32)
        expert = lax.broadcasted_iota(jnp.int32, weights.shape, 0)
        line = jnp.sum(jnp.where(expert == where[0], weights, 0.0), axis=0, keepdims=True)
        row = lax.broadcasted_iota(jnp.int32, (count, count), 0)
        column = lax.broadcasted_iota(jnp.int32, (count, count), 1)
        return jnp.sum(jnp.where(row == column, line, 0.0), axis=1, keepdims=True)

    scales = [scale_of(piece) for piece in pieces]

    def arrive(j, start, size):
        copy_columns(gate, gate_block, start, size, sems.at[j]).wait()
        copy_columns(up, up_block, start, size, sems.at[chunks + j]).wait()

    def products(i):
        columns = columns_at(i * width)
        return [
            jnp.dot(rows[...], block[:, columns], preferred_element_type=jnp.float32)
            for block in (gate_block, up_block)
        ]

    def activate(gate_value, up_value, i):
        value = gate_value / (1.0 + jnp.exp(-gate_value)) * up_value
        hidden[:, columns_at(i * width)] = value.astype(jnp.bfloat16)

    arrive(0, 0, width)
    held[0], held[1] = products(0)

    def step(i, carry):
        arrive(i + 1, (2 * i + 1) * width, 2 * width)
        first = products(2 * i + 1)
        activate(held[0], held[1], 2 * i)
        second = products(2 * i + 2)
        activate(*first, 2 * i + 1)
        held[0], held[1] = second
        return carry

    lax.fori_loop(0, blocks // 2 - 1, step, 0)
    arrive(chunks - 1, (blocks - 1) * width, width)
    last = products(blocks - 1)
    activate(held[0], held[1], blocks - 2)
    activate(*last, blocks - 1)

    def finish(i, carry):
        copy_columns(out, out_block, 2 * i * width, 2 * width, sems.at[2 * chunks + i]).wait()
        for half in range(2):
            columns = columns_at((2 * i + half) * width)
            value = jnp.dot(hidden[...], out_block[:, columns], preferred_element_type=jnp.float32)
            for j, scale in enumerate(scales):
                scaled = (value[j * count : (j + 1) * count] * scale).astype(jnp.bfloat16)
                if j < positions:
                    own_sums[j][:, columns] = scaled
                else:
                    start = (j - positions) * count
                    other_sums[start : start + count, columns] = scaled
        return carry

    lax.fori_loop(0, out_chunks, finish, 0)


def expert_apply(expert, owns, others, weights, count):
    positions = len(owns)
    latent_width = owns[0].shape[1]
    hidden_width = weights[0].shape[2]
    rows, width = 2 * positions * count, 256
    own_sum = jax.ShapeDtypeStruct((count, latent_width), jnp.bfloat16)
    other_sums = jax.ShapeDtypeStruct((positions * count, latent_width), jnp.bfloat16)
    return pl.pallas_call(
        functools.partial(expert_kernel, positions, count),
        out_shape=(own_sum,) * positions + (other_sums,),
        in_specs=[in_smem] + [in_vmem] * (2 * positions) + [in_hbm] * 3,
        out_specs=(in_vmem,) * (positions + 1),
        scratch_shapes=[
            pltpu.VMEM((rows, latent_width), jnp.bfloat16),
            pltpu.VMEM((rows, hidden_width), jnp.bfloat16),
            pltpu.VMEM((2, rows, width), jnp.float32),
        ]
        + [pltpu.VMEM(w.shape[1:], w.dtype) for w in weights]
        + [pltpu.SemaphoreType.DMA((hidden_width // width + 2 + latent_width // (2 * width),))],
        compiler_params=pltpu.CompilerParams(vmem_limit_bytes=28 * mebi),
        cost_estimate=pl.CostEstimate(
            flops=3 * rows * latent_width * hidden_width // 2,
            bytes_accessed=4 * rows * latent_width,
            transcendentals=0,
        ),
        name="expert",
    )(expert, *owns, *others, *weights)


def project_kernel(where, *refs):
    terms, refs = refs[:-9], refs[-9:]
    mine, swapped, layer_out, in_order, combined, held, blocks, read_sems, sems = refs
    sides, ep_count, inner, width = mine.shape

    def read(e, side):
        return pltpu.make_async_copy(
            mine.at[side, e], held.at[side, e], read_sems.at[sides * e + side]
        )

    for e in range(ep_count):
        for side in range(sides):
            read(e, side).start()
    total = terms[0][...].astype(jnp.float32)
    for term in terms[1:]:
        total += term[...].astype(jnp.float32)
    in_order[...] = total.astype(jnp.bfloat16)
    for side in range(sides):
        for i, core in enumerate((1 - where[0], where[0])):
            start = pl.multiple_of((2 * side + core) * inner, inner)
            to = pl.ds((2 * side + i) * inner, inner)
            combined[:, to] = in_order[:, pl.ds(start, inner)]

    def sent(e):
        columns = pl.ds(e * width, width)
        return pltpu.make_async_copy(blocks.at[:, columns], layer_out.at[:, columns], sems.at[e])

    for e in range(ep_count):
        rows = []
        for side in range(sides):
            read(e, side).wait()
            rows += [swapped[side, e], held[side, e]]
        value = jnp.dot(
            combined[...], jnp.concatenate(rows, axis=0), preferred_element_type=jnp.float32
        )
        blocks[:, e * width : (e + 1) * width] = value.astype(jnp.bfloat16)
        sent(e).start()
    for e in range(ep_count):
        sent(e).wait()


def project(group, terms, mine, swapped):
    count, latent_width = terms[0].shape
    sides, ep_count, inner, width = mine.shape
    return pl.pallas_call(
        project_kernel,
        in_specs=[in_smem] + [in_vmem] * len(terms) + [in_hbm, in_vmem],
        out_specs=anywhere,
        out_shape=jax.ShapeDtypeStruct((count, ep_count * width), jnp.bfloat16),
        scratch_shapes=[
            pltpu.VMEM((count, latent_width), jnp.bfloat16),
            pltpu.VMEM((count, latent_width), jnp.bfloat16),
            pltpu.VMEM(mine.shape, mine.dtype),
            pltpu.VMEM((count, ep_count * width), jnp.bfloat16),
            pltpu.SemaphoreType.DMA((sides * ep_count,)),
            pltpu.SemaphoreType.DMA((ep_count,)),
        ],
        compiler_params=pltpu.CompilerParams(vmem_limit_bytes=16 * mebi),
        cost_estimate=pl.CostEstimate(
            flops=2 * count * latent_width * ep_count * width,
            bytes_accessed=2 * latent_width * ep_count * width,
            transcendentals=0,
        ),
        name="project",
    )(group.reshape(1).astype(jnp.int32), *terms, mine, swapped)


def body(
    tokens, expert_ids, route_scores, down_latent, gate_weight, up_weight, out_weight, up_latent
):
    group_count = lax.axis_size("grp")
    ep_count = lax.axis_size("ep")
    expert_count = group_count * ep_count * gate_weight.shape[0]
    rep, group, place = lax.axis_index("rep"), lax.axis_index("grp"), lax.axis_index("ep")
    side = rep % 2
    own_quarter = 2 * side + group
    token_count = tokens.shape[0]
    latent_width = down_latent.shape[1]
    steps = ep_count // 2
    last = steps - 1

    quarter = down_latent.shape[0] // 4

    def own_piece(core):
        return lax.dynamic_slice_in_dim(down_latent, (2 * side + core) * quarter, quarter, 0)

    kept, given = split_columns(tokens, ep_count, quarter, place, side, group)
    taken = swap_reps(given)
    near = first_steps(own_piece(group), steps)
    far = {0: swap_ep(near[0], 1)}
    near[1], kept = join(near[1], kept)
    far[1] = swap_ep(near[1], 1)

    inner = latent_width // 4
    up_piece = lax.dynamic_slice_in_dim(up_latent, own_quarter * inner, inner, 0)
    mine = lax.all_gather(up_piece, "ep", axis=0)
    weights = dense_weights(after(expert_ids, near[1]), route_scores, expert_count)
    others = {k: near[k] for k in near if k > 1}
    far[1], weights, *arrived = join(far[1], weights, *others.values())
    near.update(zip(others, arrived))
    for k in range(2, steps):
        if k & (k - 1):
            low = k & -k
            near[k] = swap_ep(near[k ^ low], 2 * low)
        if k == last:
            near[k], far[0], taken = join(near[k], far[0], taken)
        far[k] = swap_ep(near[k], 1)
    blocks = []
    for k in range(steps):
        other = own_piece(1 - group) if k == 0 else swap_cores(near[k])
        blocks.append((near[k], far[k], other, swap_cores(far[k])))
    early = list(range(last))
    (partial,) = down_project(early, kept, taken, [b for k in early for b in blocks[k]])
    late = [after(blocks[-1][0], partial), *blocks[-1][1:]]
    own_part, sent_part = down_project([last], kept, taken, late, partial)
    latent = finish_latent(own_part, swap_reps(sent_part), weights.astype(jnp.bfloat16))

    expert = (group * ep_count + place).astype(jnp.int32).reshape(1)
    expert_weights = [
        pltpu.with_memory_space_constraint(w, pltpu.HBM)
        for w in (gate_weight, up_weight, out_weight)
    ]
    near = first_steps(latent, steps)
    far = {0: swap_ep(latent, 1)}
    sums, travel, taken_in = {}, {"up": mine}, set()

    def start_near(k):
        near[k] = swap_ep(near[k ^ (k & -k)], 2 * (k & -k))
        return near, k

    def start_far(k):
        far[k] = swap_ep(near[k], 1)
        return far, k

    def send(name, value, mask):
        travel[name] = swap_ep(value.astype(jnp.bfloat16), mask)
        return travel, name

    def run(which, *coming):
        owns = [(near, far)[y][k] for k, y in which]
        operands = join(*owns, *[swap_cores(own) for own in owns])
        count = len(which)
        out = expert_apply(expert, operands[:count], operands[count:], expert_weights, token_count)
        out = join(*out, *[table[key] for table, key in coming])
        for (table, key), value in zip(coming, out[count + 1 :]):
            table[key] = value
        from_core = swap_cores(out[count])
        for i, place_of in enumerate(which):
            swapped = from_core[i * token_count : (i + 1) * token_count]
            sums[place_of] = out[i].astype(jnp.float32) + swapped.astype(jnp.float32)

    special = [(0, 0), (last - 1, 0), (last - 1, 1), (last, 0)]

    def homeward(*previous):
        return [send(p, sums[p], 2 * p[0] + p[1]) for p in previous if p not in special]

    run([(0, 0)], (near, 1), (travel, "up"))
    start_far(1)
    arrived = [k for k in near if k > 1]
    far[1], *values = join(far[1], *[near[k] for k in arrived])
    near.update(zip(arrived, values))
    sides = [[i, i + 1] for i in range(0, lax.axis_size("rep"), 2)]
    both_sides = lax.all_gather(travel.pop("up"), "rep", axis=0, axis_index_groups=sides)
    previous = [(2, 0), (1, 1)]
    run(previous, *[start_near(3)] * (last >= 3), start_far(2))
    for k in range(3, steps):
        coming = homeward(*previous) + [start_far(k)] + [(far, 0)] * (k == last)
        if k + 1 < steps and k + 1 not in near:
            coming.append(start_near(k + 1))
        previous = [(k, 0), (k - 1, 1)]
        run(previous, *coming)
    run(
        [(last, 1), (0, 1)],
        send((last - 1, 1), sums[last - 1, 1], 1),
        send((last, 0), sums[last, 0], 2),
    )
    run([(1, 0)], send((last, 1), sums[last, 1], 3))
    shared = sums[last - 1, 0]
    for name in ((last - 1, 1), (last, 0), (last, 1)):
        shared += travel.pop(name).astype(jnp.float32)
    shared = shared.astype(jnp.bfloat16)
    send("shared", shared, 2 * last - 2)
    sums[1, 0] = sums[1, 0].astype(jnp.bfloat16)
    both_sides = after(both_sides, sums[1, 0], shared)
    homeward((0, 1), (1, 0))
    *terms, swapped_sides = join(sums[0, 0], *travel.values(), swap_cores(both_sides))
    both_sides = pltpu.with_memory_space_constraint(both_sides, pltpu.HBM)
    return project(group, terms, both_sides, swapped_sides)


def solution(mesh):
    in_specs = (
        P(("rep", "grp", "ep"), None),
        P(("rep", "grp", "ep"), None),
        P(("rep", "grp", "ep"), None),
        P("ep", None),
        P(("grp", "ep"), None, None),
        P(("grp", "ep"), None, None),
        P(("grp", "ep"), None, None),
        P(None, "ep"),
    )
    out_specs = P(("rep", "grp", "ep"), None)
    return jax.shard_map(body, mesh=mesh, in_specs=in_specs, out_specs=out_specs, check_vma=False)
```

```python
import functools

import jax
import jax.numpy as jnp
from jax import lax
from jax.experimental import pallas as pl
from jax.experimental.pallas import tpu as pltpu
from jax.sharding import PartitionSpec as P

route_scale = 2.5
mebi = 1024 * 1024
in_vmem = pl.BlockSpec(memory_space=pltpu.VMEM)
in_smem = pl.BlockSpec(memory_space=pltpu.SMEM)
in_hbm = pl.BlockSpec(memory_space=pltpu.HBM)
anywhere = pl.BlockSpec(memory_space=pl.ANY)


def after(value, *others):
    return lax.optimization_barrier((value, *others))[0]


def join(*values):
    return lax.optimization_barrier(values)


def swap_cores(array):
    return lax.ppermute(array, "grp", [(0, 1), (1, 0)])


def swap_reps(array):
    return lax.ppermute(array, "rep", [(i, i ^ 1) for i in range(lax.axis_size("rep"))])


def swap_ep(array, mask):
    return lax.ppermute(array, "ep", [(i, i ^ mask) for i in range(lax.axis_size("ep"))])


def first_steps(piece, steps):
    return {0: piece} | {k: swap_ep(piece, 2 * k) for k in range(1, steps) if k & (k - 1) == 0}


def dense_weights(expert_ids, route_scores, expert_count):
    sigmoids = jax.nn.sigmoid(route_scores)
    weights = (route_scale * sigmoids / jnp.sum(sigmoids, axis=1, keepdims=True)).astype(
        jnp.bfloat16
    )
    named = expert_ids[None, :, :] == jnp.arange(expert_count, dtype=jnp.int32)[:, None, None]
    return jnp.sum(jnp.where(named, weights.astype(jnp.float32)[None, :, :], 0.0), axis=2)


def columns_kernel(ep_count, quarter, where, tokens, kept, given):
    place, side, group = where[0], where[1], where[2]
    for offset in range(ep_count):
        for core in range(2):
            to = pl.ds(((offset // 2 * 2 + core) * 2 + offset % 2) * quarter, quarter)
            shard = (place ^ offset) * 4 + (group ^ core)
            for half, part in ((side, kept), (1 - side, given)):
                start = pl.multiple_of((shard + 2 * half) * quarter, quarter)
                part[:, to] = tokens[:, pl.ds(start, quarter)]


def split_columns(tokens, ep_count, quarter, place, side, group):
    count = tokens.shape[0]
    if quarter % 128 == 0:
        half = jax.ShapeDtypeStruct((count, 2 * ep_count * quarter), tokens.dtype)
        return pl.pallas_call(
            functools.partial(columns_kernel, ep_count, quarter),
            out_shape=(half, half),
            in_specs=[in_smem, in_vmem],
            out_specs=(in_vmem, in_vmem),
            compiler_params=pltpu.CompilerParams(vmem_limit_bytes=8 * mebi),
            name="split_columns",
        )(jnp.stack([place, side, group]).astype(jnp.int32), tokens)
    cut = tokens.reshape(count, ep_count, 2, 2, quarter)
    parts = [], []
    for step in range(ep_count // 2):
        for core in (group, 1 - group):
            for offset in (2 * step, 2 * step + 1):
                for half, part in zip((side, 1 - side), parts):
                    start = (0, place ^ offset, half, core, 0)
                    part.append(lax.dynamic_slice(cut, start, (count, 1, 1, 1, quarter)))
    kept, given = [jnp.stack(part, axis=1).reshape(count, -1) for part in parts]
    return kept, given


def down_kernel(steps, last, *refs):
    (kept, given), blocks = refs[:2], refs[2 : 2 + 4 * len(steps)]
    so_far, results = (refs[-3], refs[-2:]) if last else (None, refs[-1:])
    depth = 2 * blocks[0].shape[0]
    width = 256
    for start in range(0, blocks[0].shape[1], width):
        columns = slice(start, start + width)
        total = 0.0 if so_far is None else so_far[:, columns]
        for i, step in enumerate(steps):
            for core in range(2):
                inner = pl.ds((2 * step + core) * depth, depth)
                rows = jnp.concatenate([kept[:, inner], given[:, inner]], axis=0)
                near, far = blocks[4 * i + 2 * core], blocks[4 * i + 2 * core + 1]
                block = jnp.concatenate([near[:, columns], far[:, columns]], axis=0)
                total += jnp.dot(rows, block, preferred_element_type=jnp.float32)
        if last:
            count = kept.shape[0]
            results[0][:, columns] = total[:count]
            results[1][:, columns] = total[count:].astype(jnp.bfloat16)
        else:
            results[0][:, columns] = total


def down_project(steps, kept, given, blocks, so_far=None):
    count, inner = kept.shape
    latent_width = blocks[0].shape[1]
    operands = (kept, given, *blocks) + (() if so_far is None else (so_far,))
    if so_far is None:
        shapes = (jax.ShapeDtypeStruct((2 * count, latent_width), jnp.float32),)
    else:
        shapes = (
            jax.ShapeDtypeStruct((count, latent_width), jnp.float32),
            jax.ShapeDtypeStruct((count, latent_width), jnp.bfloat16),
        )
    return pl.pallas_call(
        functools.partial(down_kernel, steps, so_far is not None),
        out_shape=shapes,
        in_specs=[in_vmem] * len(operands),
        out_specs=(in_vmem,) * len(shapes),
        compiler_params=pltpu.CompilerParams(vmem_limit_bytes=16 * mebi),
        cost_estimate=pl.CostEstimate(
            flops=16 * len(steps) * count * blocks[0].shape[0] * latent_width,
            bytes_accessed=2 * len(blocks) * blocks[0].shape[0] * latent_width,
            transcendentals=0,
        ),
        name="down_project",
    )(*operands)


def latent_kernel(own_part, arrived, weights, piece):
    count = own_part.shape[0]
    total = own_part[...] + arrived[...].astype(jnp.float32)
    piece[:count] = total.astype(jnp.bfloat16)
    extra = piece.shape[0] - count
    piece[count:] = jnp.zeros((extra, piece.shape[1]), jnp.bfloat16)
    piece[count:, :count] = weights[...]


def finish_latent(own_part, arrived, weights):
    count, latent_width = own_part.shape
    return pl.pallas_call(
        latent_kernel,
        out_shape=jax.ShapeDtypeStruct((count + weights.shape[0], latent_width), jnp.bfloat16),
        in_specs=[in_vmem] * 3,
        out_specs=in_vmem,
        compiler_params=pltpu.CompilerParams(vmem_limit_bytes=4 * mebi),
        name="finish_latent",
    )(own_part, arrived, weights)


def expert_kernel(positions, count, where, *refs):
    pieces = refs[: 2 * positions]
    gate, up, out = refs[2 * positions : 2 * positions + 3]
    own_sums, refs = refs[2 * positions + 3 : 3 * positions + 3], refs[3 * positions + 3 :]
    other_sums, rows, hidden, held, gate_block, up_block, out_block, sems = refs
    width = 256
    blocks = gate.shape[2] // width

    def columns_at(start):
        return pl.ds(pl.multiple_of(start, width), width)

    chunks = blocks // 2 + 1

    def read(j, part, size):
        source, target = ((gate, gate_block), (up, up_block), (out, out_block))[part]
        start = 2 * j * width if part == 2 else max(2 * j - 1, 0) * width
        return copy_columns(source, target, start, size, sems.at[part * chunks + j])

    def copy_columns(source, target, start, size, sem):
        columns = pl.ds(pl.multiple_of(start, width), size)
        return pltpu.make_async_copy(source.at[0, :, columns], target.at[:, columns], sem)

    def size_of(j):
        return width if j in (0, chunks - 1) else 2 * width

    out_chunks = out.shape[2] // (2 * width)
    for j in range(chunks):
        read(j, 0, size_of(j)).start()
        read(j, 1, size_of(j)).start()
    for j in range(out_chunks):
        read(j, 2, 2 * width).start()
    for i, piece in enumerate(pieces):
        rows[i * count : (i + 1) * count] = piece[:count]

    def scale_of(piece):
        weights = piece[count:, :count].astype(jnp.float32)
        expert = lax.broadcasted_iota(jnp.int32, weights.shape, 0)
        line = jnp.sum(jnp.where(expert == where[0], weights, 0.0), axis=0, keepdims=True)
        row = lax.broadcasted_iota(jnp.int32, (count, count), 0)
        column = lax.broadcasted_iota(jnp.int32, (count, count), 1)
        return jnp.sum(jnp.where(row == column, line, 0.0), axis=1, keepdims=True)

    scales = [scale_of(piece) for piece in pieces]

    def arrive(j, start, size):
        copy_columns(gate, gate_block, start, size, sems.at[j]).wait()
        copy_columns(up, up_block, start, size, sems.at[chunks + j]).wait()

    def products(i):
        columns = columns_at(i * width)
        return [
            jnp.dot(rows[...], block[:, columns], preferred_element_type=jnp.float32)
            for block in (gate_block, up_block)
        ]

    def activate(gate_value, up_value, i):
        value = gate_value / (1.0 + jnp.exp(-gate_value)) * up_value
        hidden[:, columns_at(i * width)] = value.astype(jnp.bfloat16)

    arrive(0, 0, width)
    held[0], held[1] = products(0)

    def step(i, carry):
        arrive(i + 1, (2 * i + 1) * width, 2 * width)
        first = products(2 * i + 1)
        activate(held[0], held[1], 2 * i)
        second = products(2 * i + 2)
        activate(*first, 2 * i + 1)
        held[0], held[1] = second
        return carry

    lax.fori_loop(0, blocks // 2 - 1, step, 0)
    arrive(chunks - 1, (blocks - 1) * width, width)
    last = products(blocks - 1)
    activate(held[0], held[1], blocks - 2)
    activate(*last, blocks - 1)

    def finish(i, carry):
        copy_columns(out, out_block, 2 * i * width, 2 * width, sems.at[2 * chunks + i]).wait()
        for half in range(2):
            columns = columns_at((2 * i + half) * width)
            value = jnp.dot(hidden[...], out_block[:, columns], preferred_element_type=jnp.float32)
            for j, scale in enumerate(scales):
                scaled = (value[j * count : (j + 1) * count] * scale).astype(jnp.bfloat16)
                if j < positions:
                    own_sums[j][:, columns] = scaled
                else:
                    start = (j - positions) * count
                    other_sums[start : start + count, columns] = scaled
        return carry

    lax.fori_loop(0, out_chunks, finish, 0)


def expert_apply(expert, owns, others, weights, count):
    positions = len(owns)
    latent_width = owns[0].shape[1]
    hidden_width = weights[0].shape[2]
    rows, width = 2 * positions * count, 256
    own_sum = jax.ShapeDtypeStruct((count, latent_width), jnp.bfloat16)
    other_sums = jax.ShapeDtypeStruct((positions * count, latent_width), jnp.bfloat16)
    return pl.pallas_call(
        functools.partial(expert_kernel, positions, count),
        out_shape=(own_sum,) * positions + (other_sums,),
        in_specs=[in_smem] + [in_vmem] * (2 * positions) + [in_hbm] * 3,
        out_specs=(in_vmem,) * (positions + 1),
        scratch_shapes=[
            pltpu.VMEM((rows, latent_width), jnp.bfloat16),
            pltpu.VMEM((rows, hidden_width), jnp.bfloat16),
            pltpu.VMEM((2, rows, width), jnp.float32),
        ]
        + [pltpu.VMEM(w.shape[1:], w.dtype) for w in weights]
        + [pltpu.SemaphoreType.DMA((hidden_width // width + 2 + latent_width // (2 * width),))],
        compiler_params=pltpu.CompilerParams(vmem_limit_bytes=28 * mebi),
        cost_estimate=pl.CostEstimate(
            flops=3 * rows * latent_width * hidden_width // 2,
            bytes_accessed=4 * rows * latent_width,
            transcendentals=0,
        ),
        name="expert",
    )(expert, *owns, *others, *weights)


def project_kernel(where, *refs):
    terms, refs = refs[:-8], refs[-8:]
    mine, swapped, layer_out, combined, held, blocks, read_sems, sems = refs
    sides, ep_count, inner, width = mine.shape

    def read(e, side):
        return pltpu.make_async_copy(
            mine.at[side, e], held.at[side, e], read_sems.at[sides * e + side]
        )

    for e in range(ep_count):
        for side in range(sides):
            read(e, side).start()
    total = terms[0][...].astype(jnp.float32)
    for term in terms[1:]:
        total += term[...].astype(jnp.float32)
    combined[...] = total.astype(jnp.bfloat16)

    def sent(e):
        columns = pl.ds(e * width, width)
        return pltpu.make_async_copy(blocks.at[:, columns], layer_out.at[:, columns], sems.at[e])

    for e in range(ep_count):
        value = 0.0
        for side in range(sides):
            read(e, side).wait()
            for core, array in ((1 - where[0], swapped), (where[0], held)):
                columns = pl.ds(pl.multiple_of((2 * side + core) * inner, inner), inner)
                value += jnp.dot(
                    combined[:, columns], array[side, e], preferred_element_type=jnp.float32
                )
        blocks[:, e * width : (e + 1) * width] = value.astype(jnp.bfloat16)
        sent(e).start()
    for e in range(ep_count):
        sent(e).wait()


def project(group, terms, mine, swapped):
    count, latent_width = terms[0].shape
    sides, ep_count, inner, width = mine.shape
    return pl.pallas_call(
        project_kernel,
        in_specs=[in_smem] + [in_vmem] * len(terms) + [in_hbm, in_vmem],
        out_specs=anywhere,
        out_shape=jax.ShapeDtypeStruct((count, ep_count * width), jnp.bfloat16),
        scratch_shapes=[
            pltpu.VMEM((count, latent_width), jnp.bfloat16),
            pltpu.VMEM(mine.shape, mine.dtype),
            pltpu.VMEM((count, ep_count * width), jnp.bfloat16),
            pltpu.SemaphoreType.DMA((sides * ep_count,)),
            pltpu.SemaphoreType.DMA((ep_count,)),
        ],
        compiler_params=pltpu.CompilerParams(vmem_limit_bytes=16 * mebi),
        cost_estimate=pl.CostEstimate(
            flops=2 * count * latent_width * ep_count * width,
            bytes_accessed=2 * latent_width * ep_count * width,
            transcendentals=0,
        ),
        name="project",
    )(group.reshape(1).astype(jnp.int32), *terms, mine, swapped)


def body(
    tokens, expert_ids, route_scores, down_latent, gate_weight, up_weight, out_weight, up_latent
):
    group_count = lax.axis_size("grp")
    ep_count = lax.axis_size("ep")
    expert_count = group_count * ep_count * gate_weight.shape[0]
    rep, group, place = lax.axis_index("rep"), lax.axis_index("grp"), lax.axis_index("ep")
    side = rep % 2
    own_quarter = 2 * side + group
    token_count = tokens.shape[0]
    latent_width = down_latent.shape[1]
    steps = ep_count // 2
    last = steps - 1

    quarter = down_latent.shape[0] // 4

    def own_piece(core):
        return lax.dynamic_slice_in_dim(down_latent, (2 * side + core) * quarter, quarter, 0)

    kept, given = split_columns(tokens, ep_count, quarter, place, side, group)
    taken = swap_reps(given)
    near = first_steps(own_piece(group), steps)
    far = {0: swap_ep(near[0], 1)}
    near[1], kept = join(near[1], kept)
    far[1] = swap_ep(near[1], 1)

    inner = latent_width // 4
    up_piece = lax.dynamic_slice_in_dim(up_latent, own_quarter * inner, inner, 0)
    mine = lax.all_gather(up_piece, "ep", axis=0)
    weights = dense_weights(after(expert_ids, near[1]), route_scores, expert_count)
    others = {k: near[k] for k in near if k > 1}
    weights, *arrived = join(weights, *others.values())
    near.update(zip(others, arrived))
    for k in range(2, steps):
        if k & (k - 1):
            low = k & -k
            near[k] = swap_ep(near[k ^ low], 2 * low)
        if k == last:
            near[k], far[0], far[1], taken = join(near[k], far[0], far[1], taken)
        far[k] = swap_ep(near[k], 1)
    blocks = []
    for k in range(steps):
        other = own_piece(1 - group) if k == 0 else swap_cores(near[k])
        blocks.append((near[k], far[k], other, swap_cores(far[k])))
    early = list(range(last))
    (partial,) = down_project(early, kept, taken, [b for k in early for b in blocks[k]])
    late = [after(blocks[-1][0], partial), *blocks[-1][1:]]
    own_part, sent_part = down_project([last], kept, taken, late, partial)
    latent = finish_latent(own_part, swap_reps(sent_part), weights.astype(jnp.bfloat16))

    expert = (group * ep_count + place).astype(jnp.int32).reshape(1)
    expert_weights = [
        pltpu.with_memory_space_constraint(w, pltpu.HBM)
        for w in (gate_weight, up_weight, out_weight)
    ]
    near = first_steps(latent, steps)
    far = {0: swap_ep(latent, 1)}
    sums, travel, taken_in = {}, {"up": mine}, set()

    def start_near(k):
        near[k] = swap_ep(near[k ^ (k & -k)], 2 * (k & -k))
        return near, k

    def start_far(k):
        far[k] = swap_ep(near[k], 1)
        return far, k

    def send(name, value, mask):
        travel[name] = swap_ep(value.astype(jnp.bfloat16), mask)
        return travel, name

    def run(which, *coming):
        owns = [(near, far)[y][k] for k, y in which]
        operands = join(*owns, *[swap_cores(own) for own in owns])
        count = len(which)
        out = expert_apply(expert, operands[:count], operands[count:], expert_weights, token_count)
        out = join(*out, *[table[key] for table, key in coming])
        for (table, key), value in zip(coming, out[count + 1 :]):
            table[key] = value
        from_core = swap_cores(out[count])
        for i, place_of in enumerate(which):
            swapped = from_core[i * token_count : (i + 1) * token_count]
            sums[place_of] = out[i].astype(jnp.float32) + swapped.astype(jnp.float32)

    special = [(0, 0), (last - 1, 0), (last - 1, 1), (last, 0)]

    def homeward(*previous):
        return [send(p, sums[p], 2 * p[0] + p[1]) for p in previous if p not in special]

    run([(0, 0)], *[(near, k) for k in near if k], (travel, "up"))
    sides = [[i, i + 1] for i in range(0, lax.axis_size("rep"), 2)]
    both_sides = lax.all_gather(travel.pop("up"), "rep", axis=0, axis_index_groups=sides)
    previous = [(2, 0), (1, 0)]
    run(previous, *[start_near(3)] * (last >= 3), start_far(2))
    for k in range(3, steps):
        coming = homeward(*previous) + [start_far(k)] + [(far, 0)] * (k == last)
        if k + 1 < steps and k + 1 not in near:
            coming.append(start_near(k + 1))
        previous = [(k, 0), (k - 1, 1)]
        run(previous, *coming)
    run(
        [(last, 1), (0, 1)],
        send((last - 1, 1), sums[last - 1, 1], 1),
        send((last, 0), sums[last, 0], 2),
        start_far(1),
    )
    run([(1, 1)], send((last, 1), sums[last, 1], 3))
    shared = sums[last - 1, 0]
    for name in ((last - 1, 1), (last, 0), (last, 1)):
        shared += travel.pop(name).astype(jnp.float32)
    shared = shared.astype(jnp.bfloat16)
    send("shared", shared, 2 * last - 2)
    sums[1, 1] = sums[1, 1].astype(jnp.bfloat16)
    both_sides = after(both_sides, sums[1, 1], shared)
    homeward((0, 1), (1, 1))
    *terms, swapped_sides = join(sums[0, 0], *travel.values(), swap_cores(both_sides))
    both_sides = pltpu.with_memory_space_constraint(both_sides, pltpu.HBM)
    return project(group, terms, both_sides, swapped_sides)


def solution(mesh):
    in_specs = (
        P(("rep", "grp", "ep"), None),
        P(("rep", "grp", "ep"), None),
        P(("rep", "grp", "ep"), None),
        P("ep", None),
        P(("grp", "ep"), None, None),
        P(("grp", "ep"), None, None),
        P(("grp", "ep"), None, None),
        P(None, "ep"),
    )
    out_specs = P(("rep", "grp", "ep"), None)
    return jax.shard_map(body, mesh=mesh, in_specs=in_specs, out_specs=out_specs, check_vma=False)
```

```python
import functools

import jax
import jax.numpy as jnp
from jax import lax
from jax.experimental import pallas as pl
from jax.experimental.pallas import tpu as pltpu
from jax.sharding import PartitionSpec as P

route_scale = 2.5
mebi = 1024 * 1024
in_vmem = pl.BlockSpec(memory_space=pltpu.VMEM)
in_smem = pl.BlockSpec(memory_space=pltpu.SMEM)
in_hbm = pl.BlockSpec(memory_space=pltpu.HBM)
anywhere = pl.BlockSpec(memory_space=pl.ANY)


def after(value, *others):
    return lax.optimization_barrier((value, *others))[0]


def join(*values):
    return lax.optimization_barrier(values)


def swap_cores(array):
    return lax.ppermute(array, "grp", [(0, 1), (1, 0)])


def swap_reps(array):
    return lax.ppermute(array, "rep", [(i, i ^ 1) for i in range(lax.axis_size("rep"))])


def swap_ep(array, mask):
    return lax.ppermute(array, "ep", [(i, i ^ mask) for i in range(lax.axis_size("ep"))])


def first_steps(piece, steps):
    return {0: piece} | {k: swap_ep(piece, 2 * k) for k in range(1, steps) if k & (k - 1) == 0}


def dense_weights(expert_ids, route_scores, expert_count):
    sigmoids = jax.nn.sigmoid(route_scores)
    weights = (route_scale * sigmoids / jnp.sum(sigmoids, axis=1, keepdims=True)).astype(
        jnp.bfloat16
    )
    named = expert_ids[None, :, :] == jnp.arange(expert_count, dtype=jnp.int32)[:, None, None]
    return jnp.sum(jnp.where(named, weights.astype(jnp.float32)[None, :, :], 0.0), axis=2)


def columns_kernel(ep_count, quarter, where, tokens, kept, given):
    place, side, group = where[0], where[1], where[2]
    for offset in range(ep_count):
        for core in range(2):
            to = pl.ds(((offset // 2 * 2 + core) * 2 + offset % 2) * quarter, quarter)
            shard = (place ^ offset) * 4 + (group ^ core)
            for half, part in ((side, kept), (1 - side, given)):
                start = pl.multiple_of((shard + 2 * half) * quarter, quarter)
                part[:, to] = tokens[:, pl.ds(start, quarter)]


def split_columns(tokens, ep_count, quarter, place, side, group):
    count = tokens.shape[0]
    if quarter % 128 == 0:
        half = jax.ShapeDtypeStruct((count, 2 * ep_count * quarter), tokens.dtype)
        return pl.pallas_call(
            functools.partial(columns_kernel, ep_count, quarter),
            out_shape=(half, half),
            in_specs=[in_smem, in_vmem],
            out_specs=(in_vmem, in_vmem),
            compiler_params=pltpu.CompilerParams(vmem_limit_bytes=8 * mebi),
            name="split_columns",
        )(jnp.stack([place, side, group]).astype(jnp.int32), tokens)
    cut = tokens.reshape(count, ep_count, 2, 2, quarter)
    parts = [], []
    for step in range(ep_count // 2):
        for core in (group, 1 - group):
            for offset in (2 * step, 2 * step + 1):
                for half, part in zip((side, 1 - side), parts):
                    start = (0, place ^ offset, half, core, 0)
                    part.append(lax.dynamic_slice(cut, start, (count, 1, 1, 1, quarter)))
    kept, given = [jnp.stack(part, axis=1).reshape(count, -1) for part in parts]
    return kept, given


def down_kernel(steps, last, *refs):
    (kept, given), blocks = refs[:2], refs[2 : 2 + 4 * len(steps)]
    so_far, results = (refs[-3], refs[-2:]) if last else (None, refs[-1:])
    depth = 2 * blocks[0].shape[0]
    width = 256
    for start in range(0, blocks[0].shape[1], width):
        columns = slice(start, start + width)
        total = 0.0 if so_far is None else so_far[:, columns]
        for i, step in enumerate(steps):
            for core in range(2):
                inner = pl.ds((2 * step + core) * depth, depth)
                rows = jnp.concatenate([kept[:, inner], given[:, inner]], axis=0)
                near, far = blocks[4 * i + 2 * core], blocks[4 * i + 2 * core + 1]
                block = jnp.concatenate([near[:, columns], far[:, columns]], axis=0)
                total += jnp.dot(rows, block, preferred_element_type=jnp.float32)
        if last:
            count = kept.shape[0]
            results[0][:, columns] = total[:count]
            results[1][:, columns] = total[count:].astype(jnp.bfloat16)
        else:
            results[0][:, columns] = total


def down_project(steps, kept, given, blocks, so_far=None):
    count, inner = kept.shape
    latent_width = blocks[0].shape[1]
    operands = (kept, given, *blocks) + (() if so_far is None else (so_far,))
    if so_far is None:
        shapes = (jax.ShapeDtypeStruct((2 * count, latent_width), jnp.float32),)
    else:
        shapes = (
            jax.ShapeDtypeStruct((count, latent_width), jnp.float32),
            jax.ShapeDtypeStruct((count, latent_width), jnp.bfloat16),
        )
    return pl.pallas_call(
        functools.partial(down_kernel, steps, so_far is not None),
        out_shape=shapes,
        in_specs=[in_vmem] * len(operands),
        out_specs=(in_vmem,) * len(shapes),
        compiler_params=pltpu.CompilerParams(vmem_limit_bytes=16 * mebi),
        cost_estimate=pl.CostEstimate(
            flops=16 * len(steps) * count * blocks[0].shape[0] * latent_width,
            bytes_accessed=2 * len(blocks) * blocks[0].shape[0] * latent_width,
            transcendentals=0,
        ),
        name="down_project",
    )(*operands)


def latent_kernel(own_part, arrived, weights, piece):
    count = own_part.shape[0]
    total = own_part[...] + arrived[...].astype(jnp.float32)
    piece[:count] = total.astype(jnp.bfloat16)
    extra = piece.shape[0] - count
    piece[count:] = jnp.zeros((extra, piece.shape[1]), jnp.bfloat16)
    piece[count:, :count] = weights[...]


def finish_latent(own_part, arrived, weights):
    count, latent_width = own_part.shape
    return pl.pallas_call(
        latent_kernel,
        out_shape=jax.ShapeDtypeStruct((count + weights.shape[0], latent_width), jnp.bfloat16),
        in_specs=[in_vmem] * 3,
        out_specs=in_vmem,
        compiler_params=pltpu.CompilerParams(vmem_limit_bytes=4 * mebi),
        name="finish_latent",
    )(own_part, arrived, weights)


def expert_kernel(positions, count, where, *refs):
    pieces = refs[: 2 * positions]
    gate, up, out = refs[2 * positions : 2 * positions + 3]
    own_sums, refs = refs[2 * positions + 3 : 3 * positions + 3], refs[3 * positions + 3 :]
    other_sums, rows, hidden, held, gate_block, up_block, out_block, sems = refs
    width = 256
    blocks = gate.shape[2] // width

    def columns_at(start):
        return pl.ds(pl.multiple_of(start, width), width)

    chunks = blocks // 2 + 1

    def read(j, part, size):
        source, target = ((gate, gate_block), (up, up_block), (out, out_block))[part]
        start = 2 * j * width if part == 2 else max(2 * j - 1, 0) * width
        return copy_columns(source, target, start, size, sems.at[part * chunks + j])

    def copy_columns(source, target, start, size, sem):
        columns = pl.ds(pl.multiple_of(start, width), size)
        return pltpu.make_async_copy(source.at[0, :, columns], target.at[:, columns], sem)

    def size_of(j):
        return width if j in (0, chunks - 1) else 2 * width

    out_chunks = out.shape[2] // (2 * width)
    for j in range(chunks):
        read(j, 0, size_of(j)).start()
        read(j, 1, size_of(j)).start()
    for j in range(out_chunks):
        read(j, 2, 2 * width).start()
    for i, piece in enumerate(pieces):
        rows[i * count : (i + 1) * count] = piece[:count]

    def scale_of(piece):
        weights = piece[count:, :count].astype(jnp.float32)
        expert = lax.broadcasted_iota(jnp.int32, weights.shape, 0)
        line = jnp.sum(jnp.where(expert == where[0], weights, 0.0), axis=0, keepdims=True)
        row = lax.broadcasted_iota(jnp.int32, (count, count), 0)
        column = lax.broadcasted_iota(jnp.int32, (count, count), 1)
        return jnp.sum(jnp.where(row == column, line, 0.0), axis=1, keepdims=True)

    scales = [scale_of(piece) for piece in pieces]

    def arrive(j, start, size):
        copy_columns(gate, gate_block, start, size, sems.at[j]).wait()
        copy_columns(up, up_block, start, size, sems.at[chunks + j]).wait()

    def products(i):
        columns = columns_at(i * width)
        return [
            jnp.dot(rows[...], block[:, columns], preferred_element_type=jnp.float32)
            for block in (gate_block, up_block)
        ]

    def activate(gate_value, up_value, i):
        value = gate_value / (1.0 + jnp.exp(-gate_value)) * up_value
        hidden[:, columns_at(i * width)] = value.astype(jnp.bfloat16)

    arrive(0, 0, width)
    held[0], held[1] = products(0)

    def step(i, carry):
        arrive(i + 1, (2 * i + 1) * width, 2 * width)
        first = products(2 * i + 1)
        activate(held[0], held[1], 2 * i)
        second = products(2 * i + 2)
        activate(*first, 2 * i + 1)
        held[0], held[1] = second
        return carry

    lax.fori_loop(0, blocks // 2 - 1, step, 0)
    arrive(chunks - 1, (blocks - 1) * width, width)
    last = products(blocks - 1)
    activate(held[0], held[1], blocks - 2)
    activate(*last, blocks - 1)

    def finish(i, carry):
        copy_columns(out, out_block, 2 * i * width, 2 * width, sems.at[2 * chunks + i]).wait()
        for half in range(2):
            columns = columns_at((2 * i + half) * width)
            value = jnp.dot(hidden[...], out_block[:, columns], preferred_element_type=jnp.float32)
            for j, scale in enumerate(scales):
                scaled = (value[j * count : (j + 1) * count] * scale).astype(jnp.bfloat16)
                if j < positions:
                    own_sums[j][:, columns] = scaled
                else:
                    start = (j - positions) * count
                    other_sums[start : start + count, columns] = scaled
        return carry

    lax.fori_loop(0, out_chunks, finish, 0)


def expert_apply(expert, owns, others, weights, count):
    positions = len(owns)
    latent_width = owns[0].shape[1]
    hidden_width = weights[0].shape[2]
    rows, width = 2 * positions * count, 256
    own_sum = jax.ShapeDtypeStruct((count, latent_width), jnp.bfloat16)
    other_sums = jax.ShapeDtypeStruct((positions * count, latent_width), jnp.bfloat16)
    return pl.pallas_call(
        functools.partial(expert_kernel, positions, count),
        out_shape=(own_sum,) * positions + (other_sums,),
        in_specs=[in_smem] + [in_vmem] * (2 * positions) + [in_hbm] * 3,
        out_specs=(in_vmem,) * (positions + 1),
        scratch_shapes=[
            pltpu.VMEM((rows, latent_width), jnp.bfloat16),
            pltpu.VMEM((rows, hidden_width), jnp.bfloat16),
            pltpu.VMEM((2, rows, width), jnp.float32),
        ]
        + [pltpu.VMEM(w.shape[1:], w.dtype) for w in weights]
        + [pltpu.SemaphoreType.DMA((hidden_width // width + 2 + latent_width // (2 * width),))],
        compiler_params=pltpu.CompilerParams(vmem_limit_bytes=32 * mebi),
        cost_estimate=pl.CostEstimate(
            flops=3 * rows * latent_width * hidden_width // 2,
            bytes_accessed=4 * rows * latent_width,
            transcendentals=0,
        ),
        name="expert",
    )(expert, *owns, *others, *weights)


def project_kernel(where, *refs):
    terms, refs = refs[:-8], refs[-8:]
    mine, swapped, layer_out, combined, held, blocks, read_sems, sems = refs
    sides, ep_count, inner, width = mine.shape

    def read(e, side):
        return pltpu.make_async_copy(
            mine.at[side, e], held.at[side, e], read_sems.at[sides * e + side]
        )

    for e in range(ep_count):
        for side in range(sides):
            read(e, side).start()
    total = terms[0][...].astype(jnp.float32)
    for term in terms[1:]:
        total += term[...].astype(jnp.float32)
    combined[...] = total.astype(jnp.bfloat16)

    def sent(e):
        columns = pl.ds(e * width, width)
        return pltpu.make_async_copy(blocks.at[:, columns], layer_out.at[:, columns], sems.at[e])

    for e in range(ep_count):
        value = 0.0
        for side in range(sides):
            read(e, side).wait()
            for core, array in ((1 - where[0], swapped), (where[0], held)):
                columns = pl.ds(pl.multiple_of((2 * side + core) * inner, inner), inner)
                value += jnp.dot(
                    combined[:, columns], array[side, e], preferred_element_type=jnp.float32
                )
        blocks[:, e * width : (e + 1) * width] = value.astype(jnp.bfloat16)
        sent(e).start()
    for e in range(ep_count):
        sent(e).wait()


def project(group, terms, mine, swapped):
    count, latent_width = terms[0].shape
    sides, ep_count, inner, width = mine.shape
    return pl.pallas_call(
        project_kernel,
        in_specs=[in_smem] + [in_vmem] * len(terms) + [in_hbm, in_vmem],
        out_specs=anywhere,
        out_shape=jax.ShapeDtypeStruct((count, ep_count * width), jnp.bfloat16),
        scratch_shapes=[
            pltpu.VMEM((count, latent_width), jnp.bfloat16),
            pltpu.VMEM(mine.shape, mine.dtype),
            pltpu.VMEM((count, ep_count * width), jnp.bfloat16),
            pltpu.SemaphoreType.DMA((sides * ep_count,)),
            pltpu.SemaphoreType.DMA((ep_count,)),
        ],
        compiler_params=pltpu.CompilerParams(vmem_limit_bytes=16 * mebi),
        cost_estimate=pl.CostEstimate(
            flops=2 * count * latent_width * ep_count * width,
            bytes_accessed=2 * latent_width * ep_count * width,
            transcendentals=0,
        ),
        name="project",
    )(group.reshape(1).astype(jnp.int32), *terms, mine, swapped)


def body(
    tokens, expert_ids, route_scores, down_latent, gate_weight, up_weight, out_weight, up_latent
):
    group_count = lax.axis_size("grp")
    ep_count = lax.axis_size("ep")
    expert_count = group_count * ep_count * gate_weight.shape[0]
    rep, group, place = lax.axis_index("rep"), lax.axis_index("grp"), lax.axis_index("ep")
    side = rep % 2
    own_quarter = 2 * side + group
    token_count = tokens.shape[0]
    latent_width = down_latent.shape[1]
    steps = ep_count // 2
    last = steps - 1

    quarter = down_latent.shape[0] // 4

    def own_piece(core):
        return lax.dynamic_slice_in_dim(down_latent, (2 * side + core) * quarter, quarter, 0)

    kept, given = split_columns(tokens, ep_count, quarter, place, side, group)
    taken = swap_reps(given)
    near = first_steps(own_piece(group), steps)
    far = {0: swap_ep(near[0], 1)}
    near[1], kept = join(near[1], kept)
    far[1] = swap_ep(near[1], 1)

    inner = latent_width // 4
    up_piece = lax.dynamic_slice_in_dim(up_latent, own_quarter * inner, inner, 0)
    mine = lax.all_gather(up_piece, "ep", axis=0)
    weights = dense_weights(after(expert_ids, near[1]), route_scores, expert_count)
    others = {k: near[k] for k in near if k > 1}
    far[1], weights, *arrived = join(far[1], weights, *others.values())
    near.update(zip(others, arrived))
    for k in range(2, steps):
        if k & (k - 1):
            low = k & -k
            near[k] = swap_ep(near[k ^ low], 2 * low)
        if k == last:
            near[k], far[0], taken = join(near[k], far[0], taken)
        far[k] = swap_ep(near[k], 1)
    blocks = []
    for k in range(steps):
        other = own_piece(1 - group) if k == 0 else swap_cores(near[k])
        blocks.append((near[k], far[k], other, swap_cores(far[k])))
    early = list(range(last))
    (partial,) = down_project(early, kept, taken, [b for k in early for b in blocks[k]])
    late = [after(blocks[-1][0], partial), *blocks[-1][1:]]
    own_part, sent_part = down_project([last], kept, taken, late, partial)
    latent = finish_latent(own_part, swap_reps(sent_part), weights.astype(jnp.bfloat16))

    expert = (group * ep_count + place).astype(jnp.int32).reshape(1)
    expert_weights = [
        pltpu.with_memory_space_constraint(w, pltpu.HBM)
        for w in (gate_weight, up_weight, out_weight)
    ]
    near = first_steps(latent, steps)
    far = {0: swap_ep(latent, 1)}
    sums, travel, taken_in = {}, {"up": mine}, set()

    def start_near(k):
        near[k] = swap_ep(near[k ^ (k & -k)], 2 * (k & -k))
        return near, k

    def start_far(k):
        far[k] = swap_ep(near[k], 1)
        return far, k

    def send(name, value, mask):
        travel[name] = swap_ep(value.astype(jnp.bfloat16), mask)
        return travel, name

    def run(which, *coming):
        owns = [(near, far)[y][k] for k, y in which]
        operands = join(*owns, *[swap_cores(own) for own in owns])
        count = len(which)
        out = expert_apply(expert, operands[:count], operands[count:], expert_weights, token_count)
        out = join(*out, *[table[key] for table, key in coming])
        for (table, key), value in zip(coming, out[count + 1 :]):
            table[key] = value
        from_core = swap_cores(out[count])
        for i, place_of in enumerate(which):
            swapped = from_core[i * token_count : (i + 1) * token_count]
            sums[place_of] = out[i].astype(jnp.float32) + swapped.astype(jnp.float32)

    special = [(0, 0), (last - 1, 0), (last - 1, 1), (last, 0)]

    def homeward(*previous):
        return [send(p, sums[p], 2 * p[0] + p[1]) for p in previous if p not in special]

    run([(0, 0)], *[(near, k) for k in near if k], (far, 0), (travel, "up"))
    sides = [[i, i + 1] for i in range(0, lax.axis_size("rep"), 2)]
    both_sides = lax.all_gather(travel.pop("up"), "rep", axis=0, axis_index_groups=sides)
    previous = [(2, 0), (1, 0), (0, 1)]
    run(previous, *[start_near(3)] * (last >= 3), start_far(2))
    for k in range(3, steps):
        coming = homeward(*previous) + [start_far(k)]
        if k + 1 < steps and k + 1 not in near:
            coming.append(start_near(k + 1))
        previous = [(k, 0), (k - 1, 1)]
        run(previous, *coming)
    run(
        [(last, 1)],
        send((last - 1, 1), sums[last - 1, 1], 1),
        send((last, 0), sums[last, 0], 2),
        start_far(1),
    )
    run([(1, 1)], send((last, 1), sums[last, 1], 3))
    shared = sums[last - 1, 0]
    for name in ((last - 1, 1), (last, 0), (last, 1)):
        shared += travel.pop(name).astype(jnp.float32)
    shared = shared.astype(jnp.bfloat16)
    send("shared", shared, 2 * last - 2)
    sums[1, 1] = sums[1, 1].astype(jnp.bfloat16)
    both_sides = after(both_sides, sums[1, 1], shared)
    homeward((1, 1))
    *terms, swapped_sides = join(sums[0, 0], *travel.values(), swap_cores(both_sides))
    both_sides = pltpu.with_memory_space_constraint(both_sides, pltpu.HBM)
    return project(group, terms, both_sides, swapped_sides)


def solution(mesh):
    in_specs = (
        P(("rep", "grp", "ep"), None),
        P(("rep", "grp", "ep"), None),
        P(("rep", "grp", "ep"), None),
        P("ep", None),
        P(("grp", "ep"), None, None),
        P(("grp", "ep"), None, None),
        P(("grp", "ep"), None, None),
        P(None, "ep"),
    )
    out_specs = P(("rep", "grp", "ep"), None)
    return jax.shard_map(body, mesh=mesh, in_specs=in_specs, out_specs=out_specs, check_vma=False)
```

```python
import functools

import jax
import jax.numpy as jnp
from jax import lax
from jax.experimental import pallas as pl
from jax.experimental.pallas import tpu as pltpu
from jax.sharding import PartitionSpec as P

route_scale = 2.5
mebi = 1024 * 1024
in_vmem = pl.BlockSpec(memory_space=pltpu.VMEM)
in_smem = pl.BlockSpec(memory_space=pltpu.SMEM)
in_hbm = pl.BlockSpec(memory_space=pltpu.HBM)
anywhere = pl.BlockSpec(memory_space=pl.ANY)


def after(value, *others):
    return lax.optimization_barrier((value, *others))[0]


def join(*values):
    return lax.optimization_barrier(values)


def swap_cores(array):
    return lax.ppermute(array, "grp", [(0, 1), (1, 0)])


def swap_reps(array):
    return lax.ppermute(array, "rep", [(i, i ^ 1) for i in range(lax.axis_size("rep"))])


def swap_ep(array, mask):
    return lax.ppermute(array, "ep", [(i, i ^ mask) for i in range(lax.axis_size("ep"))])


def first_steps(piece, steps):
    return {0: piece} | {k: swap_ep(piece, 2 * k) for k in range(1, steps) if k & (k - 1) == 0}


def dense_weights(expert_ids, route_scores, expert_count):
    sigmoids = jax.nn.sigmoid(route_scores)
    weights = (route_scale * sigmoids / jnp.sum(sigmoids, axis=1, keepdims=True)).astype(
        jnp.bfloat16
    )
    named = expert_ids[None, :, :] == jnp.arange(expert_count, dtype=jnp.int32)[:, None, None]
    return jnp.sum(jnp.where(named, weights.astype(jnp.float32)[None, :, :], 0.0), axis=2)


def columns_kernel(ep_count, quarter, where, tokens, kept, given):
    place, side, group = where[0], where[1], where[2]
    for offset in range(ep_count):
        for core in range(2):
            to = pl.ds(((offset // 2 * 2 + core) * 2 + offset % 2) * quarter, quarter)
            shard = (place ^ offset) * 4 + (group ^ core)
            for half, part in ((side, kept), (1 - side, given)):
                start = pl.multiple_of((shard + 2 * half) * quarter, quarter)
                part[:, to] = tokens[:, pl.ds(start, quarter)]


def split_columns(tokens, ep_count, quarter, place, side, group):
    count = tokens.shape[0]
    if quarter % 128 == 0:
        half = jax.ShapeDtypeStruct((count, 2 * ep_count * quarter), tokens.dtype)
        return pl.pallas_call(
            functools.partial(columns_kernel, ep_count, quarter),
            out_shape=(half, half),
            in_specs=[in_smem, in_vmem],
            out_specs=(in_vmem, in_vmem),
            compiler_params=pltpu.CompilerParams(vmem_limit_bytes=8 * mebi),
            name="split_columns",
        )(jnp.stack([place, side, group]).astype(jnp.int32), tokens)
    cut = tokens.reshape(count, ep_count, 2, 2, quarter)
    parts = [], []
    for step in range(ep_count // 2):
        for core in (group, 1 - group):
            for offset in (2 * step, 2 * step + 1):
                for half, part in zip((side, 1 - side), parts):
                    start = (0, place ^ offset, half, core, 0)
                    part.append(lax.dynamic_slice(cut, start, (count, 1, 1, 1, quarter)))
    kept, given = [jnp.stack(part, axis=1).reshape(count, -1) for part in parts]
    return kept, given


def down_kernel(steps, last, *refs):
    (kept, given), blocks = refs[:2], refs[2 : 2 + 4 * len(steps)]
    so_far, results = (refs[-3], refs[-2:]) if last else (None, refs[-1:])
    depth = 2 * blocks[0].shape[0]
    width = 256
    for start in range(0, blocks[0].shape[1], width):
        columns = slice(start, start + width)
        total = 0.0 if so_far is None else so_far[:, columns]
        for i, step in enumerate(steps):
            for core in range(2):
                inner = pl.ds((2 * step + core) * depth, depth)
                rows = jnp.concatenate([kept[:, inner], given[:, inner]], axis=0)
                near, far = blocks[4 * i + 2 * core], blocks[4 * i + 2 * core + 1]
                block = jnp.concatenate([near[:, columns], far[:, columns]], axis=0)
                total += jnp.dot(rows, block, preferred_element_type=jnp.float32)
        if last:
            count = kept.shape[0]
            results[0][:, columns] = total[:count]
            results[1][:, columns] = total[count:].astype(jnp.bfloat16)
        else:
            results[0][:, columns] = total


def down_project(steps, kept, given, blocks, so_far=None):
    count, inner = kept.shape
    latent_width = blocks[0].shape[1]
    operands = (kept, given, *blocks) + (() if so_far is None else (so_far,))
    if so_far is None:
        shapes = (jax.ShapeDtypeStruct((2 * count, latent_width), jnp.float32),)
    else:
        shapes = (
            jax.ShapeDtypeStruct((count, latent_width), jnp.float32),
            jax.ShapeDtypeStruct((count, latent_width), jnp.bfloat16),
        )
    return pl.pallas_call(
        functools.partial(down_kernel, steps, so_far is not None),
        out_shape=shapes,
        in_specs=[in_vmem] * len(operands),
        out_specs=(in_vmem,) * len(shapes),
        compiler_params=pltpu.CompilerParams(vmem_limit_bytes=16 * mebi),
        cost_estimate=pl.CostEstimate(
            flops=16 * len(steps) * count * blocks[0].shape[0] * latent_width,
            bytes_accessed=2 * len(blocks) * blocks[0].shape[0] * latent_width,
            transcendentals=0,
        ),
        name="down_project",
    )(*operands)


def latent_kernel(own_part, arrived, weights, piece):
    count = own_part.shape[0]
    total = own_part[...] + arrived[...].astype(jnp.float32)
    piece[:count] = total.astype(jnp.bfloat16)
    extra = piece.shape[0] - count
    piece[count:] = jnp.zeros((extra, piece.shape[1]), jnp.bfloat16)
    piece[count:, :count] = weights[...]


def finish_latent(own_part, arrived, weights):
    count, latent_width = own_part.shape
    return pl.pallas_call(
        latent_kernel,
        out_shape=jax.ShapeDtypeStruct((count + weights.shape[0], latent_width), jnp.bfloat16),
        in_specs=[in_vmem] * 3,
        out_specs=in_vmem,
        compiler_params=pltpu.CompilerParams(vmem_limit_bytes=4 * mebi),
        name="finish_latent",
    )(own_part, arrived, weights)


def expert_kernel(positions, count, where, *refs):
    pieces = refs[: 2 * positions]
    gate, up, out = refs[2 * positions : 2 * positions + 3]
    own_sums, refs = refs[2 * positions + 3 : 3 * positions + 3], refs[3 * positions + 3 :]
    other_sums, rows, hidden, held, gate_block, up_block, out_block, sems = refs
    width = 256
    blocks = gate.shape[2] // width

    def columns_at(start):
        return pl.ds(pl.multiple_of(start, width), width)

    chunks = blocks // 2 + 1

    def read(j, part, size):
        source, target = ((gate, gate_block), (up, up_block), (out, out_block))[part]
        start = 2 * j * width if part == 2 else max(2 * j - 1, 0) * width
        return copy_columns(source, target, start, size, sems.at[part * chunks + j])

    def copy_columns(source, target, start, size, sem):
        columns = pl.ds(pl.multiple_of(start, width), size)
        return pltpu.make_async_copy(source.at[0, :, columns], target.at[:, columns], sem)

    def size_of(j):
        return width if j in (0, chunks - 1) else 2 * width

    out_chunks = out.shape[2] // (2 * width)
    for j in range(chunks):
        read(j, 0, size_of(j)).start()
        read(j, 1, size_of(j)).start()
    for j in range(out_chunks):
        read(j, 2, 2 * width).start()
    for i, piece in enumerate(pieces):
        rows[i * count : (i + 1) * count] = piece[:count]

    def scale_of(piece):
        weights = piece[count:, :count].astype(jnp.float32)
        expert = lax.broadcasted_iota(jnp.int32, weights.shape, 0)
        line = jnp.sum(jnp.where(expert == where[0], weights, 0.0), axis=0, keepdims=True)
        row = lax.broadcasted_iota(jnp.int32, (count, count), 0)
        column = lax.broadcasted_iota(jnp.int32, (count, count), 1)
        return jnp.sum(jnp.where(row == column, line, 0.0), axis=1, keepdims=True)

    scales = [scale_of(piece) for piece in pieces]

    def arrive(j, start, size):
        copy_columns(gate, gate_block, start, size, sems.at[j]).wait()
        copy_columns(up, up_block, start, size, sems.at[chunks + j]).wait()

    def products(i):
        columns = columns_at(i * width)
        return [
            jnp.dot(rows[...], block[:, columns], preferred_element_type=jnp.float32)
            for block in (gate_block, up_block)
        ]

    def activate(gate_value, up_value, i):
        value = gate_value / (1.0 + jnp.exp(-gate_value)) * up_value
        hidden[:, columns_at(i * width)] = value.astype(jnp.bfloat16)

    arrive(0, 0, width)
    held[0], held[1] = products(0)

    def step(i, carry):
        arrive(i + 1, (2 * i + 1) * width, 2 * width)
        first = products(2 * i + 1)
        activate(held[0], held[1], 2 * i)
        second = products(2 * i + 2)
        activate(*first, 2 * i + 1)
        held[0], held[1] = second
        return carry

    lax.fori_loop(0, blocks // 2 - 1, step, 0)
    arrive(chunks - 1, (blocks - 1) * width, width)
    last = products(blocks - 1)
    activate(held[0], held[1], blocks - 2)
    activate(*last, blocks - 1)

    def finish(i, carry):
        copy_columns(out, out_block, 2 * i * width, 2 * width, sems.at[2 * chunks + i]).wait()
        for half in range(2):
            columns = columns_at((2 * i + half) * width)
            value = jnp.dot(hidden[...], out_block[:, columns], preferred_element_type=jnp.float32)
            for j, scale in enumerate(scales):
                scaled = (value[j * count : (j + 1) * count] * scale).astype(jnp.bfloat16)
                if j < positions:
                    own_sums[j][:, columns] = scaled
                else:
                    start = (j - positions) * count
                    other_sums[start : start + count, columns] = scaled
        return carry

    lax.fori_loop(0, out_chunks, finish, 0)


def expert_apply(expert, owns, others, weights, count):
    positions = len(owns)
    latent_width = owns[0].shape[1]
    hidden_width = weights[0].shape[2]
    rows, width = 2 * positions * count, 256
    own_sum = jax.ShapeDtypeStruct((count, latent_width), jnp.bfloat16)
    other_sums = jax.ShapeDtypeStruct((positions * count, latent_width), jnp.bfloat16)
    return pl.pallas_call(
        functools.partial(expert_kernel, positions, count),
        out_shape=(own_sum,) * positions + (other_sums,),
        in_specs=[in_smem] + [in_vmem] * (2 * positions) + [in_hbm] * 3,
        out_specs=(in_vmem,) * (positions + 1),
        scratch_shapes=[
            pltpu.VMEM((rows, latent_width), jnp.bfloat16),
            pltpu.VMEM((rows, hidden_width), jnp.bfloat16),
            pltpu.VMEM((2, rows, width), jnp.float32),
        ]
        + [pltpu.VMEM(w.shape[1:], w.dtype) for w in weights]
        + [pltpu.SemaphoreType.DMA((hidden_width // width + 2 + latent_width // (2 * width),))],
        compiler_params=pltpu.CompilerParams(vmem_limit_bytes=32 * mebi),
        cost_estimate=pl.CostEstimate(
            flops=3 * rows * latent_width * hidden_width // 2,
            bytes_accessed=4 * rows * latent_width,
            transcendentals=0,
        ),
        name="expert",
    )(expert, *owns, *others, *weights)


def project_kernel(where, *refs):
    terms, refs = refs[:-8], refs[-8:]
    mine, swapped, layer_out, combined, held, blocks, read_sems, sems = refs
    sides, ep_count, inner, width = mine.shape

    def read(e, side):
        return pltpu.make_async_copy(
            mine.at[side, e], held.at[side, e], read_sems.at[sides * e + side]
        )

    for e in range(ep_count):
        for side in range(sides):
            read(e, side).start()
    total = terms[0][...].astype(jnp.float32)
    for term in terms[1:]:
        total += term[...].astype(jnp.float32)
    combined[...] = total.astype(jnp.bfloat16)

    def sent(e):
        columns = pl.ds(e * width, width)
        return pltpu.make_async_copy(blocks.at[:, columns], layer_out.at[:, columns], sems.at[e])

    for e in range(ep_count):
        value = 0.0
        for side in range(sides):
            read(e, side).wait()
            for core, array in ((1 - where[0], swapped), (where[0], held)):
                columns = pl.ds(pl.multiple_of((2 * side + core) * inner, inner), inner)
                value += jnp.dot(
                    combined[:, columns], array[side, e], preferred_element_type=jnp.float32
                )
        blocks[:, e * width : (e + 1) * width] = value.astype(jnp.bfloat16)
        sent(e).start()
    for e in range(ep_count):
        sent(e).wait()


def project(group, terms, mine, swapped):
    count, latent_width = terms[0].shape
    sides, ep_count, inner, width = mine.shape
    return pl.pallas_call(
        project_kernel,
        in_specs=[in_smem] + [in_vmem] * len(terms) + [in_hbm, in_vmem],
        out_specs=anywhere,
        out_shape=jax.ShapeDtypeStruct((count, ep_count * width), jnp.bfloat16),
        scratch_shapes=[
            pltpu.VMEM((count, latent_width), jnp.bfloat16),
            pltpu.VMEM(mine.shape, mine.dtype),
            pltpu.VMEM((count, ep_count * width), jnp.bfloat16),
            pltpu.SemaphoreType.DMA((sides * ep_count,)),
            pltpu.SemaphoreType.DMA((ep_count,)),
        ],
        compiler_params=pltpu.CompilerParams(vmem_limit_bytes=16 * mebi),
        cost_estimate=pl.CostEstimate(
            flops=2 * count * latent_width * ep_count * width,
            bytes_accessed=2 * latent_width * ep_count * width,
            transcendentals=0,
        ),
        name="project",
    )(group.reshape(1).astype(jnp.int32), *terms, mine, swapped)


def body(
    tokens, expert_ids, route_scores, down_latent, gate_weight, up_weight, out_weight, up_latent
):
    group_count = lax.axis_size("grp")
    ep_count = lax.axis_size("ep")
    expert_count = group_count * ep_count * gate_weight.shape[0]
    rep, group, place = lax.axis_index("rep"), lax.axis_index("grp"), lax.axis_index("ep")
    side = rep % 2
    own_quarter = 2 * side + group
    token_count = tokens.shape[0]
    latent_width = down_latent.shape[1]
    steps = ep_count // 2
    last = steps - 1

    quarter = down_latent.shape[0] // 4

    def own_piece(core):
        return lax.dynamic_slice_in_dim(down_latent, (2 * side + core) * quarter, quarter, 0)

    kept, given = split_columns(tokens, ep_count, quarter, place, side, group)
    taken = swap_reps(given)
    near = first_steps(own_piece(group), steps)
    far = {0: swap_ep(near[0], 1)}
    near[1], kept = join(near[1], kept)
    far[1] = swap_ep(near[1], 1)

    inner = latent_width // 4
    up_piece = lax.dynamic_slice_in_dim(up_latent, own_quarter * inner, inner, 0)
    mine = lax.all_gather(up_piece, "ep", axis=0)
    weights = dense_weights(after(expert_ids, near[1]), route_scores, expert_count)
    others = {k: near[k] for k in near if k > 1}
    far[1], weights, *arrived = join(far[1], weights, *others.values())
    near.update(zip(others, arrived))
    for k in range(2, steps):
        if k & (k - 1):
            low = k & -k
            near[k] = swap_ep(near[k ^ low], 2 * low)
        if k == last:
            near[k], far[0], taken = join(near[k], far[0], taken)
        far[k] = swap_ep(near[k], 1)
    blocks = []
    for k in range(steps):
        other = own_piece(1 - group) if k == 0 else swap_cores(near[k])
        blocks.append((near[k], far[k], other, swap_cores(far[k])))
    early = list(range(last))
    (partial,) = down_project(early, kept, taken, [b for k in early for b in blocks[k]])
    late = [after(blocks[-1][0], partial), *blocks[-1][1:]]
    own_part, sent_part = down_project([last], kept, taken, late, partial)
    latent = finish_latent(own_part, swap_reps(sent_part), weights.astype(jnp.bfloat16))

    expert = (group * ep_count + place).astype(jnp.int32).reshape(1)
    expert_weights = [
        pltpu.with_memory_space_constraint(w, pltpu.HBM)
        for w in (gate_weight, up_weight, out_weight)
    ]
    near = first_steps(latent, steps)
    far = {0: swap_ep(latent, 1)}
    sums, travel, taken_in = {}, {"up": mine}, set()

    def start_near(k):
        near[k] = swap_ep(near[k ^ (k & -k)], 2 * (k & -k))
        return near, k

    def start_far(k):
        far[k] = swap_ep(near[k], 1)
        return far, k

    def send(name, value, mask):
        travel[name] = swap_ep(value.astype(jnp.bfloat16), mask)
        return travel, name

    def run(which, *coming):
        owns = [(near, far)[y][k] for k, y in which]
        operands = join(*owns, *[swap_cores(own) for own in owns])
        count = len(which)
        out = expert_apply(expert, operands[:count], operands[count:], expert_weights, token_count)
        out = join(*out, *[table[key] for table, key in coming])
        for (table, key), value in zip(coming, out[count + 1 :]):
            table[key] = value
        from_core = swap_cores(out[count])
        for i, place_of in enumerate(which):
            swapped = from_core[i * token_count : (i + 1) * token_count]
            sums[place_of] = out[i].astype(jnp.float32) + swapped.astype(jnp.float32)

    special = [(0, 0), (last - 1, 0), (last - 1, 1), (last, 0)]

    def homeward(*previous):
        return [send(p, sums[p], 2 * p[0] + p[1]) for p in previous if p not in special]

    run([(0, 0)], *[(near, k) for k in near if k], (far, 0), (travel, "up"))
    sides = [[i, i + 1] for i in range(0, lax.axis_size("rep"), 2)]
    both_sides = lax.all_gather(travel.pop("up"), "rep", axis=0, axis_index_groups=sides)
    previous = [(2, 0), (1, 0), (0, 1)]
    run(previous, *[start_near(3)] * (last >= 3), start_far(2), start_far(1))
    for k in range(3, steps):
        coming = homeward(*previous) + [start_far(k)]
        if k + 1 < steps and k + 1 not in near:
            coming.append(start_near(k + 1))
        previous = [(k, 0), (k - 1, 1)]
        run(previous, *coming)
    run(
        [(last, 1), (1, 1)],
        send((last - 1, 1), sums[last - 1, 1], 1),
        send((last, 0), sums[last, 0], 2),
    )
    send((last, 1), sums[last, 1], 3)
    shared = sums[last - 1, 0]
    for name in ((last - 1, 1), (last, 0), (last, 1)):
        shared += travel.pop(name).astype(jnp.float32)
    shared = shared.astype(jnp.bfloat16)
    send("shared", shared, 2 * last - 2)
    sums[1, 1] = sums[1, 1].astype(jnp.bfloat16)
    both_sides = after(both_sides, sums[1, 1], shared)
    homeward((1, 1))
    *terms, swapped_sides = join(sums[0, 0], *travel.values(), swap_cores(both_sides))
    both_sides = pltpu.with_memory_space_constraint(both_sides, pltpu.HBM)
    return project(group, terms, both_sides, swapped_sides)


def solution(mesh):
    in_specs = (
        P(("rep", "grp", "ep"), None),
        P(("rep", "grp", "ep"), None),
        P(("rep", "grp", "ep"), None),
        P("ep", None),
        P(("grp", "ep"), None, None),
        P(("grp", "ep"), None, None),
        P(("grp", "ep"), None, None),
        P(None, "ep"),
    )
    out_specs = P(("rep", "grp", "ep"), None)
    return jax.shard_map(body, mesh=mesh, in_specs=in_specs, out_specs=out_specs, check_vma=False)
```
